32 devices in a mesh: rows: 8 (over z, core), tm: 4 (over y, x).
Axes of the slice: x: 2, y: 2, z: 4, core: 2. Of those that a mesh axis runs over, the one named last changes fastest.
Arguments:
- frames: bfloat16 [16, 1536, 512], P('rows', 'tm'), may hold values from -6 to 6
- cotangent: bfloat16 [16, 1536, 512], P('rows', 'tm'), may hold values from -6 to 6
- lengths: int32 [16], P('rows'), may hold values from 192 to 1536, as said below
- early_gain: bfloat16 [512], replicated, may hold values from 0.5 to 1.5
- early_shift: bfloat16 [512], replicated, may hold values from -3 to 3
- early_up: bfloat16 [512, 2048], replicated, may hold values from -0.25 to 0.25
- early_down: bfloat16 [2048, 512], replicated, may hold values from -0.125 to 0.125
- attend_gain: bfloat16 [512], replicated, may hold values from 0.5 to 1.5
- attend_shift: bfloat16 [512], replicated, may hold values from -3 to 3
- attend_input: bfloat16 [512, 1536], replicated, may hold values from -0.25 to 0.25
- attend_output: bfloat16 [512, 512], replicated, may hold values from -1 to 1
- distance_bias: bfloat16 [32, 8], replicated, may hold values from -4 to 4
- convolve_gain: bfloat16 [512], replicated, may hold values from 0.5 to 1.5
- convolve_shift: bfloat16 [512], replicated, may hold values from -3 to 3
- convolve_input: bfloat16 [512, 2048], replicated, may hold values from -0.25 to 0.25
- depthwise: bfloat16 [1024, 15], replicated, may hold values from -1.5 to 1.5
- inner_gain: bfloat16 [1024], replicated, may hold values from 0.5 to 1.5
- inner_shift: bfloat16 [1024], replicated, may hold values from -3 to 3
- convolve_output: bfloat16 [1024, 512], replicated, may hold values from -0.1875 to 0.1875
- late_gain: bfloat16 [512], replicated, may hold values from 0.5 to 1.5
- late_shift: bfloat16 [512], replicated, may hold values from -3 to 3
- late_up: bfloat16 [512, 2048], replicated, may hold values from -0.25 to 0.25
- late_down: bfloat16 [2048, 512], replicated, may hold values from -0.125 to 0.125
- final_gain: bfloat16 [512], replicated, may hold values from 0.5 to 1.5
- final_shift: bfloat16 [512], replicated, may hold values from -3 to 3
Outputs:
- layer_out: bfloat16 [16, 1536, 512], P('rows', 'tm')
- frames_gradient: bfloat16 [16, 1536, 512], P('rows', 'tm')
- early_gain_gradient: float32 [512], P('rows')
- early_shift_gradient: float32 [512], P('rows')
- early_up_gradient: float32 [512, 2048], P('rows')
- early_down_gradient: float32 [2048, 512], P('rows')
- attend_gain_gradient: float32 [512], P('rows')
- attend_shift_gradient: float32 [512], P('rows')
- attend_input_gradient: float32 [512, 1536], P('rows')
- attend_output_gradient: float32 [512, 512], P('rows')
- distance_bias_gradient: float32 [32, 8], P('rows')
- convolve_gain_gradient: float32 [512], P('rows')
- convolve_shift_gradient: float32 [512], P('rows')
- convolve_input_gradient: float32 [512, 2048], P('rows')
- depthwise_gradient: float32 [1024, 15], P('rows')
- inner_gain_gradient: float32 [1024], P('rows')
- inner_shift_gradient: float32 [1024], P('rows')
- convolve_output_gradient: float32 [1024, 512], P('rows')
- late_gain_gradient: float32 [512], P('rows')
- late_shift_gradient: float32 [512], P('rows')
- late_up_gradient: float32 [512, 2048], P('rows')
- late_down_gradient: float32 [2048, 512], P('rows')
- final_gain_gradient: float32 [512], P('rows')
- final_shift_gradient: float32 [512], P('rows')
The draws below stay inside these ranges and needn't reach their ends.
Inputs may be any that keep to these rules, and one draw needn't show every extreme that they name: `lengths`: in every draw one recording has all 1536 frames valid and one has 192; shorter recordings are more common than longer ones.
All inputs are finite; a program needn't handle non-finite values.
Results may differ from the reference program's by a relative error of at most 0.02.
Values may be sent and summed in bfloat16 or wider, within the bound.
No kernel may reach another device: no remote copies, remote signals or barrier semaphores. Data moves between devices by JAX's collectives and lax.ppermute only.
A program may use at most 192 MiB of HBM per device.

```python
import jax
import jax.numpy as jnp
from jax import lax

D = 512
HEADS = 8
HEAD_DIM = 64
FF = 2048
CONV = 1024
KERNEL = 15
BUCKETS = 32
TC = 384
LEN = 1536
NSEQ = 16


def draw_lengths(key, part):
    lowest = LEN // 8
    draw_one = jax.random.randint(jax.random.fold_in(key, 11), (NSEQ,), lowest, LEN + 1)
    draw_two = jax.random.randint(jax.random.fold_in(key, 12), (NSEQ,), lowest, LEN + 1)
    counts = jnp.minimum(draw_one, draw_two)
    longest = jax.random.randint(jax.random.fold_in(key, 13), (), 0, NSEQ)
    offset = jax.random.randint(jax.random.fold_in(key, 14), (), 1, NSEQ)
    shortest = (longest + offset) % NSEQ
    places = jnp.arange(NSEQ, dtype=jnp.int32)
    counts = jnp.where(places == longest, LEN, counts)
    counts = jnp.where(places == shortest, lowest, counts)
    return counts.astype(jnp.int32)


def level_of(rng, shape, cuts, least, largest):
    def one(position, parts):
        heights = jax.random.uniform(jax.random.fold_in(jax.random.fold_in(rng, 6), position), (parts,), jnp.float32, least / len(cuts), largest / len(cuts))
        return jnp.repeat(jnp.exp(heights), shape[position] // parts).reshape((-1,) + (1,) * (len(shape) - position - 1))

    factor_of = one(*cuts[0])
    for cut in cuts[1:]:
        factor_of = factor_of * one(*cut)
    return factor_of


def scatter_about(rng, extent, scale, limit, cuts=(), kind=jnp.bfloat16):
    gain = level_of(rng, extent, cuts, -0.22, 0.18) if cuts else 1.0
    values = jax.random.normal(rng, extent, jnp.float32) * scale * gain
    return jnp.minimum(jnp.maximum(values, -limit), limit).astype(kind)


def setup_inputs(seed: int = 0) -> dict:
    keys = jax.random.split(jax.random.key(seed), 26)
    return {
        "frames": scatter_about(keys[0], (NSEQ, LEN, D), 1.0, 6.0, ((0, 8), (1, 4))),
        "cotangent": scatter_about(keys[1], (NSEQ, LEN, D), 1.0, 6.0, ((0, 8), (1, 4))),
        "lengths": draw_lengths(jax.random.fold_in(keys[25], 71), 0),
        "early_gain": jnp.clip(1.0 + 0.1 * jax.random.normal(keys[3], (D,), jnp.float32), 0.5, 1.5).astype(jnp.bfloat16),
        "early_shift": scatter_about(keys[4], (D,), 0.5, 3.0),
        "early_up": scatter_about(keys[5], (D, FF), D ** -0.5, 0.25),
        "early_down": scatter_about(keys[6], (FF, D), FF ** -0.5, 0.125),
        "attend_gain": jnp.clip(1.0 + 0.1 * jax.random.normal(keys[7], (D,), jnp.float32), 0.5, 1.5).astype(jnp.bfloat16),
        "attend_shift": scatter_about(keys[8], (D,), 0.5, 3.0),
        "attend_input": scatter_about(keys[9], (D, 3 * D), D ** -0.5, 0.25),
        "attend_output": scatter_about(keys[10], (D, D), (D // 16) ** -0.5, 1.0),
        "distance_bias": scatter_about(keys[11], (BUCKETS, HEADS), 1.0, 4.0),
        "convolve_gain": jnp.clip(1.0 + 0.1 * jax.random.normal(keys[12], (D,), jnp.float32), 0.5, 1.5).astype(jnp.bfloat16),
        "convolve_shift": scatter_about(keys[13], (D,), 0.5, 3.0),
        "convolve_input": scatter_about(keys[14], (D, 2 * CONV), D ** -0.5, 0.25),
        "depthwise": scatter_about(keys[15], (CONV, KERNEL), KERNEL ** -0.5, 1.5),
        "inner_gain": jnp.clip(1.0 + 0.1 * jax.random.normal(keys[16], (CONV,), jnp.float32), 0.5, 1.5).astype(jnp.bfloat16),
        "inner_shift": scatter_about(keys[17], (CONV,), 0.5, 3.0),
        "convolve_output": scatter_about(keys[18], (CONV, D), CONV ** -0.5, 0.1875),
        "late_gain": jnp.clip(1.0 + 0.1 * jax.random.normal(keys[19], (D,), jnp.float32), 0.5, 1.5).astype(jnp.bfloat16),
        "late_shift": scatter_about(keys[20], (D,), 0.5, 3.0),
        "late_up": scatter_about(keys[21], (D, FF), D ** -0.5, 0.25),
        "late_down": scatter_about(keys[22], (FF, D), FF ** -0.5, 0.125),
        "final_gain": jnp.clip(1.0 + 0.1 * jax.random.normal(keys[23], (D,), jnp.float32), 0.5, 1.5).astype(jnp.bfloat16),
        "final_shift": scatter_about(keys[24], (D,), 0.5, 3.0),
    }


@jax.custom_vjp
def low(v):
    return lax.optimization_barrier(v.astype(jnp.bfloat16)).astype(jnp.float32)

@jax.custom_vjp
def low_back(v):
    return v

def low_keep(v):
    return (low(v), None)

def low_pass(kept, grad):
    return (grad,)

def back_keep(v):
    return (v, None)

def back_low(kept, grad):
    return (low(grad),)
low.defvjp(low_keep, low_pass)
low_back.defvjp(back_keep, back_low)
EPSILON = 1e-05
NEGATIVE = -1e+30
HIGHEST = lax.Precision.HIGHEST

def boundaries(seq_total):
    edges_list = list(range(1, 16))
    for exponent in range(16):
        edges_list.append(int(16.0 * (seq_total / 16.0) ** (exponent / 16.0)))
    return edges_list

def bucket_index(distance, seq_total):
    limits = jnp.array(boundaries(seq_total), jnp.int32)
    return lax.optimization_barrier(jnp.sum((distance[..., None] >= limits).astype(jnp.int32), axis=-1))

def layer_norm(inputs, norm_gain, norm_shift):
    center = inputs - lax.optimization_barrier(jnp.mean(inputs, axis=-1, keepdims=True))
    variance = lax.optimization_barrier(jnp.mean(center * center, axis=-1, keepdims=True))
    return center * lax.rsqrt(variance + EPSILON) * norm_gain + norm_shift

def product(left_side, right_side):
    return jnp.dot(left_side, right_side, precision=HIGHEST)

def feed_forward(inputs, norm_gain, norm_shift, weight_up, weight_down):
    normed = low(layer_norm(inputs, norm_gain, norm_shift))
    hidden = low_back(product(normed, weight_up))
    active = low(jax.nn.silu(hidden))
    return low_back(product(active, weight_down))

def attention(inputs, seq_length, norm_gain, norm_shift, weight_in, weight_out, table):
    normed = low(layer_norm(inputs, norm_gain, norm_shift))
    projected = low(low_back(product(normed, weight_in)))
    queries = projected[:, :D].reshape(LEN, HEADS, HEAD_DIM)
    key_rows = projected[:, D:2 * D].reshape(LEN, HEADS, HEAD_DIM)
    value_rows = projected[:, 2 * D:].reshape(LEN, HEADS, HEAD_DIM)
    score_scale = HEAD_DIM ** (-0.5)
    positions = jnp.arange(LEN, dtype=jnp.int32)
    key_valid = positions < seq_length

    def attend_block(row_start):
        query_block = lax.dynamic_slice_in_dim(queries, row_start, TC, 0)
        distance = (row_start + jnp.arange(TC, dtype=jnp.int32))[:, None] - positions[None, :]
        position_terms = table[bucket_index(jnp.maximum(distance, 0), LEN)]
        scores = jnp.einsum('qhd,khd->hqk', query_block, key_rows, precision=HIGHEST) * score_scale
        scores = low_back(scores + jnp.transpose(position_terms, (2, 0, 1)))
        allowed = (distance >= 0) & key_valid[None, :]
        scores = jnp.where(allowed[None], scores, NEGATIVE)
        weights = jax.nn.softmax(scores, axis=-1)
        return jnp.einsum('hqk,khd->qhd', low(weights), value_rows, precision=HIGHEST)
    row_starts = jnp.arange(LEN // TC, dtype=jnp.int32) * TC
    attended = lax.map(jax.checkpoint(attend_block), row_starts).reshape(LEN, D)
    attended = low(low_back(attended))
    return low_back(product(attended, weight_out))

def convolution(inputs, seq_length, norm_gain, norm_shift, weight_in, depth, inner_gain, inner_shift, weight_out):
    normed = low(layer_norm(inputs, norm_gain, norm_shift))
    projected = low_back(product(normed, weight_in))
    valid_rows = (jnp.arange(LEN, dtype=jnp.int32) < seq_length).astype(jnp.float32)[:, None]
    gated_units = low(projected[:, :CONV] * jax.nn.sigmoid(projected[:, CONV:]) * valid_rows)
    padded = jnp.concatenate([jnp.zeros((KERNEL - 1, CONV), jnp.float32), gated_units], axis=0)
    filtered = depth[:, 0] * padded[0:LEN]
    for tap_index in range(1, KERNEL):
        filtered = filtered + depth[:, tap_index] * padded[tap_index:tap_index + LEN]
    active = low(jax.nn.silu(layer_norm(filtered, inner_gain, inner_shift)))
    return low_back(product(active, weight_out))

def layer(inputs, seq_length, weights_all):
    early_gain, early_shift, early_up, early_down, attend_gain, attend_shift, attend_input, attend_output, distance_bias, convolve_gain, convolve_shift, convolve_input, depthwise, inner_gain, inner_shift, convolve_output, late_gain, late_shift, late_up, late_down, final_gain, final_shift = weights_all
    residual = inputs + 0.5 * feed_forward(inputs, early_gain, early_shift, early_up, early_down)
    residual = residual + attention(residual, seq_length, attend_gain, attend_shift, attend_input, attend_output, distance_bias)
    residual = residual + convolution(residual, seq_length, convolve_gain, convolve_shift, convolve_input, depthwise, inner_gain, inner_shift, convolve_output)
    residual = residual + 0.5 * feed_forward(residual, late_gain, late_shift, late_up, late_down)
    return layer_norm(residual, final_gain, final_shift)

def reference(frames, cotangent, lengths, early_gain, early_shift, early_up, early_down, attend_gain, attend_shift, attend_input, attend_output, distance_bias, convolve_gain, convolve_shift, convolve_input, depthwise, inner_gain, inner_shift, convolve_output, late_gain, late_shift, late_up, late_down, final_gain, final_shift):
    weights_all = tuple((weight_arg.astype(jnp.float32) for weight_arg in (early_gain, early_shift, early_up, early_down, attend_gain, attend_shift, attend_input, attend_output, distance_bias, convolve_gain, convolve_shift, convolve_input, depthwise, inner_gain, inner_shift, convolve_output, late_gain, late_shift, late_up, late_down, final_gain, final_shift)))
    start_sums = jax.tree.map(jnp.zeros_like, weights_all)

    def per_sequence(running, scanned):
        inputs, grad_out, seq_length = scanned
        result, pullback = jax.vjp(lambda values, params: layer(values, seq_length, params), inputs.astype(jnp.float32), weights_all)
        grad_inputs, grad_weights = pullback(grad_out.astype(jnp.float32))
        running = jax.tree.map(jnp.add, running, grad_weights)
        return (running, (result.astype(jnp.bfloat16), grad_inputs.astype(jnp.bfloat16)))
    totals, outputs = lax.scan(per_sequence, start_sums, (frames, cotangent, lengths))
    return (outputs[0], outputs[1], totals[0], totals[1], totals[2], totals[3], totals[4], totals[5], totals[6], totals[7], totals[8], totals[9], totals[10], totals[11], totals[12], totals[13], totals[14], totals[15], totals[16], totals[17], totals[18], totals[19], totals[20], totals[21])
```

```python
import functools

import jax
import jax.numpy as jnp
from jax import lax
from jax.experimental import pallas as pl
from jax.experimental.pallas import tpu as pltpu
from jax.sharding import PartitionSpec as P

EPSILON = 1e-05
NEGATIVE = -1e30
HIGHEST = lax.Precision.HIGHEST
BFLOAT = jnp.bfloat16
FLOAT = jnp.float32
NEG = NEGATIVE
F32 = FLOAT
BF = BFLOAT


def passed_along(block, axis, distance):
    devices = range(lax.axis_size(axis))
    route = [(i - distance, i) for i in devices if i - distance in devices]
    return lax.ppermute(block, axis, route)


def boundaries(seq_total):
    edges_list = list(range(1, 16))
    for exponent in range(16):
        edges_list.append(int(16.0 * (seq_total / 16.0) ** (exponent / 16.0)))
    return edges_list


def nt(a,b): return lax.dot_general(a,b,(((1,),(1,)),((),())),preferred_element_type=F32)
def nn(a,b): return lax.dot_general(a,b,(((1,),(0,)),((),())),preferred_element_type=F32)

def strip_kernel(base_ref, out_ref):
    nh,T,L=out_ref.shape
    for h in range(nh):
        e=base_ref[h]
        for g in range(T//8):
            out_ref[h,8*g:8*g+8,:]=pltpu.roll(e,8*g,1)[:,T:] if g else e[:,T:]

def make_strip(base8,T,L):
    nh=base8.shape[0]
    return pl.pallas_call(strip_kernel,out_shape=jax.ShapeDtypeStruct((nh,T,L),F32),
        compiler_params=pltpu.CompilerParams(vmem_limit_bytes=40*2**20))(base8)

def headmask(shape,h):
    lane=lax.broadcasted_iota(jnp.int32,shape,1)
    return (lane>=64*h)&(lane<64*h+64), lane==((64*h+64)%128)

def fwd_kernel(len_ref,x_ref,b_ref,o_ref,ot_ref,lse_ref,kh,vt,acc,*,nh,BQ):
    G=x_ref.shape[0]; T=x_ref.shape[3]
    n=len_ref[pl.program_id(0)]
    nk=(n+T-1)//T
    def prep(t,_):
        k=x_ref[t,1,0].astype(F32)
        pos=t*T+lax.broadcasted_iota(jnp.int32,(T,128),0)
        for h in range(nh):
            hm,sp=headmask((T,128),h)
            kh[h,t]=jnp.where(hm,k,jnp.where(sp&(pos>=n),NEG,0.0)).astype(BF)
        vt[t]=x_ref[t,2,0].T
        return 0
    lax.fori_loop(0,nk,prep,0)
    def qloop(qb,_):
        q=x_ref[qb,0,0].astype(F32)*0.125
        for h in range(nh):
            acc[h]=jnp.zeros((64,T),F32)
        qh=[]
        for h in range(nh):
            hm,sp=headmask((T,128),h)
            qh.append(jnp.where(hm,q,jnp.where(sp,1.0,0.0)).astype(BF))
        def kloop(kb,c):
            off=pl.multiple_of((qb-kb)*T,128)
            res=[]
            for h in range(nh):
                m,l=c[h]
                s=nt(kh[h,kb],qh[h])+b_ref[h,:,pl.ds(off,T)]
                mn=jnp.maximum(m,jnp.max(s,axis=0,keepdims=True))
                p=jnp.exp(s-mn)
                al=jnp.exp(m-mn)
                l=l*al+jnp.sum(p,axis=0,keepdims=True)
                acc[h]=acc[h]*al+nn(vt[kb,64*h:64*h+64,:],p.astype(BF))
                res.append((mn,l))
            return tuple(res)
        c=lax.fori_loop(0,jnp.minimum(qb+1,nk),kloop,tuple((jnp.full((1,T),NEG,F32),jnp.zeros((1,T),F32)) for _ in range(nh)))
        for h in range(nh):
            m,l=c[h]
            lse_ref[0,h,qb]=m+jnp.log(l)
            ot_ref[0,qb,64*h:64*h+64,:]=acc[h]/l
        if nh==1: ot_ref[0,qb,64:128,:]=jnp.zeros((64,T),F32)
        o_ref[qb,0]=ot_ref[0,qb].T.astype(BF)
        return 0
    lax.fori_loop(0,G,qloop,0)

def attn_fwd(lengths,x,strip,nh):
    G,_,R,T,W=x.shape; L=G*T
    gs=pltpu.PrefetchScalarGridSpec(num_scalar_prefetch=1,grid=(R,),
      in_specs=[pl.BlockSpec((G,3,1,T,W),lambda r,l:(0,0,r,0,0)),pl.BlockSpec((nh,T,L),lambda r,l:(0,0,0))],
      out_specs=[pl.BlockSpec((G,1,T,W),lambda r,l:(0,r,0,0)),pl.BlockSpec((1,G,W,T),lambda r,l:(r,0,0,0)),pl.BlockSpec((1,nh,G,1,T),lambda r,l:(r,0,0,0,0))],
      scratch_shapes=[pltpu.VMEM((nh,G,T,W),BF),pltpu.VMEM((G,W,T),BF),pltpu.VMEM((nh,64,T),F32)])
    return pl.pallas_call(functools.partial(fwd_kernel,nh=nh,BQ=T),grid_spec=gs,
      out_shape=[jax.ShapeDtypeStruct((G,R,T,W),BF),jax.ShapeDtypeStruct((R,G,W,T),F32),jax.ShapeDtypeStruct((R,nh,G,1,T),F32)],
      compiler_params=pltpu.CompilerParams(vmem_limit_bytes=56*2**20))(lengths,x,strip)

def bwd_kernel(len_ref,x_ref,do_ref,ot_ref,lse_ref,b_ref,dx_ref,db_ref,kh,vh,qh,qs,kt,dqt,dl,dk,dv,dbs,*,nh):
    G=x_ref.shape[0]; T=x_ref.shape[3]; L=G*T
    r=pl.program_id(0)
    n=len_ref[r]
    nk=(n+T-1)//T
    @pl.when(r==0)
    def _(): dbs[...]=jnp.zeros_like(dbs)
    def prepq(t,_):
        q=x_ref[t,0,0].astype(F32)*0.125
        qs[t]=q.astype(BF)
        for h in range(nh):
            hm,sp=headmask((T,128),h)
            qh[h,t]=jnp.where(hm,q,jnp.where(sp,1.0,0.0)).astype(BF)
        pr=do_ref[t,0].astype(F32).T*ot_ref[0,t]
        for h in range(nh):
            dl[h,t]=jnp.sum(pr[64*h:64*h+64],axis=0,keepdims=True)
        dqt[t]=jnp.zeros((128,T),F32)
        return 0
    lax.fori_loop(0,G,prepq,0)
    def kloop(kb,_):
        k=x_ref[kb,1,0].astype(F32)
        v=x_ref[kb,2,0].astype(F32)
        kt[...]=x_ref[kb,1,0].T
        pos=kb*T+lax.broadcasted_iota(jnp.int32,(T,128),0)
        for h in range(nh):
            hm,sp=headmask((T,128),h)
            kh[h]=jnp.where(hm,k,jnp.where(sp&(pos>=n),NEG,0.0)).astype(BF)
            vh[h]=jnp.where(hm,v,0.0).astype(BF)
        dk[...]=jnp.zeros_like(dk); dv[...]=jnp.zeros_like(dv)
        def qloop(qb,_):
            off=pl.multiple_of((qb-kb)*T,128)
            do=do_ref[qb,0]; q=qs[qb]
            for h in range(nh):
                s=nt(kh[h],qh[h,qb])+b_ref[h,:,pl.ds(off,T)]
                p=jnp.exp(s-lse_ref[0,h,qb])
                dp=nt(vh[h],do)
                ds=p*(dp-dl[h,qb])
                dsb=ds.astype(BF)
                dv[h]+=nn(p.astype(BF),do)
                dk[h]+=nn(dsb,q)
                dqt[qb,64*h:64*h+64,:]+=nn(kt[64*h:64*h+64,:],dsb)
                dbs[h,:,pl.ds(off,T)]+=ds
            return 0
        lax.fori_loop(kb,G,qloop,0)
        if nh==2:
            hm,_=headmask((T,128),0)
            dx_ref[kb,1,0]=jnp.where(hm,dk[0],dk[1]).astype(BF)
            dx_ref[kb,2,0]=jnp.where(hm,dv[0],dv[1]).astype(BF)
        else:
            dx_ref[kb,1,0]=dk[0].astype(BF)
            dx_ref[kb,2,0]=dv[0].astype(BF)
        return 0
    lax.fori_loop(0,nk,kloop,0)
    def zloop(kb,_):
        dx_ref[kb,1,0]=jnp.zeros((T,128),BF)
        dx_ref[kb,2,0]=jnp.zeros((T,128),BF)
        return 0
    lax.fori_loop(nk,G,zloop,0)
    def oloop(t,_):
        dx_ref[t,0,0]=(dqt[t]*0.125).T.astype(BF)
        return 0
    lax.fori_loop(0,G,oloop,0)
    @pl.when(r==pl.num_programs(0)-1)
    def _():
        for h in range(nh):
            a=dbs[h,0:8,:]
            for g in range(1,T//8):
                a=a+pltpu.roll(dbs[h,8*g:8*g+8,:],L-8*g,1)
            db_ref[h]=a

def attn_bwd(lengths,x,do,ot,lse,strip,nh):
    G,_,R,T,W=x.shape; L=G*T
    gs=pltpu.PrefetchScalarGridSpec(num_scalar_prefetch=1,grid=(R,),
      in_specs=[pl.BlockSpec((G,3,1,T,W),lambda r,l:(0,0,r,0,0)),pl.BlockSpec((G,1,T,W),lambda r,l:(0,r,0,0)),
        pl.BlockSpec((1,G,W,T),lambda r,l:(r,0,0,0)),pl.BlockSpec((1,nh,G,1,T),lambda r,l:(r,0,0,0,0)),pl.BlockSpec((nh,T,L),lambda r,l:(0,0,0))],
      out_specs=[pl.BlockSpec((G,3,1,T,W),lambda r,l:(0,0,r,0,0)),pl.BlockSpec((nh,8,L),lambda r,l:(0,0,0))],
      scratch_shapes=[pltpu.VMEM((nh,T,W),BF),pltpu.VMEM((nh,T,W),BF),pltpu.VMEM((nh,G,T,W),BF),pltpu.VMEM((G,T,W),BF),pltpu.VMEM((W,T),BF),
        pltpu.VMEM((G,W,T),F32),pltpu.VMEM((nh,G,1,T),F32),pltpu.VMEM((nh,T,W),F32),pltpu.VMEM((nh,T,W),F32),pltpu.VMEM((nh,T,L),F32)])
    return pl.pallas_call(functools.partial(bwd_kernel,nh=nh),grid_spec=gs,
      out_shape=[jax.ShapeDtypeStruct((G,3,R,T,W),BF),jax.ShapeDtypeStruct((nh,8,L),F32)],
      compiler_params=pltpu.CompilerParams(vmem_limit_bytes=58*2**20))(lengths,x,do,ot,lse,strip)


def tn(a, b):
    return lax.dot_general(a, b, (((0,), (0,)), ((), ())), preferred_element_type=F32)


def sigmoid(v):
    return 0.5 * jnp.tanh(0.5 * v) + 0.5


def row(ref):
    return ref[...].astype(F32)


def norm_parts(v):
    center = v - jnp.mean(v, axis=-1, keepdims=True)
    inverse = lax.rsqrt(jnp.mean(center * center, axis=-1, keepdims=True) + EPSILON)
    return center * inverse, inverse


def norm_pull(n, inverse, gain, grad):
    dn = grad * gain
    return (
        dn - jnp.mean(dn, axis=-1, keepdims=True) - n * jnp.mean(dn * n, axis=-1, keepdims=True)
    ) * inverse


def add_rows(ref, place, values):
    total = jnp.sum(values, axis=0, keepdims=True)
    for c in range(values.shape[1] // 512):
        ref[place + c : place + c + 1, :] += total[:, 512 * c : 512 * c + 512]


def start_small(ref):
    @pl.when(pl.program_id(0) == 0)
    def _():
        ref[...] = jnp.zeros_like(ref)


def put_heads(write, value, nh):
    for pair in range(value.shape[1] // 128):
        part = value[:, 128 * pair : 128 * pair + 128]
        if nh == 2:
            write(pair, part.astype(BF))
        else:
            low = lax.broadcasted_iota(jnp.int32, part.shape, 1) < 64
            write(2 * pair, jnp.where(low, part, 0.0).astype(BF))
            write(2 * pair + 1, jnp.where(low, pltpu.roll(part, 64, 1), 0.0).astype(BF))


def take_heads(read, units, nh):
    if nh == 2:
        return jnp.concatenate([read(u) for u in range(units)], axis=1)
    pairs = [
        (read(2 * u).astype(F32) + pltpu.roll(read(2 * u + 1).astype(F32), 64, 1)).astype(BF)
        for u in range(units // 2)
    ]
    return jnp.concatenate(pairs, axis=1)


def open_kernel(
    x_ref, g1, s1, wu, wd, g2, s2, wi, x1_ref, h1_ref, a_ref, sp_ref, h2_ref, u_ref, *, nh
):
    x0 = x_ref[0].astype(F32)
    n, _ = norm_parts(x0)
    h1 = (n * row(g1) + row(s1)).astype(BF)
    h1_ref[0] = h1
    y = None
    for f in range(wu.shape[1] // 512):
        at = slice(512 * f, 512 * f + 512)
        z = nn(h1, wu[:, at])
        sig = sigmoid(z)
        a = (z * sig).astype(BF)
        a_ref[0, :, at] = a
        sp_ref[0, :, at] = (sig * (1.0 + z * (1.0 - sig))).astype(BF)
        part = nn(a, wd[at, :])
        y = part if y is None else y + part
    x1 = x0 + 0.5 * y
    x1_ref[0] = x1
    n, _ = norm_parts(x1)
    h2 = (n * row(g2) + row(s2)).astype(BF)
    h2_ref[0] = h2
    for kind in range(3):

        def write(unit, part):
            u_ref[unit, 0, kind, 0] = part

        put_heads(write, nn(h2, wi[:, 512 * kind : 512 * kind + 512]), nh)


def gate_kernel(
    len_ref, o_ref, x1_ref, wo, g3, s3, wc, att_ref, x2_ref, h3_ref, g_ref, ga_ref, gb_ref, *, nh
):
    units = o_ref.shape[0]
    rows = x1_ref.shape[1]
    att = take_heads(lambda u: o_ref[u, 0, 0], units, nh)
    att_ref[0] = att
    x2 = x1_ref[0] + nn(att, wo[...])
    x2_ref[0] = x2
    n, _ = norm_parts(x2)
    h3 = (n * row(g3) + row(s3)).astype(BF)
    h3_ref[0] = h3
    channels = g_ref.shape[2]
    limit = len_ref[pl.program_id(0)] - len_ref[len_ref.shape[0] - 1]
    place = lax.broadcasted_iota(jnp.int32, (rows, 1), 0)
    valid = jnp.where(place < limit, 1.0, 0.0)
    for f in range(channels // 512):
        at = slice(512 * f, 512 * f + 512)
        lin = nn(h3, wc[:, at])
        gate = nn(h3, wc[:, channels + 512 * f : channels + 512 * f + 512])
        sig = sigmoid(gate)
        sv = sig * valid
        g = lin * sv
        g_ref[0, :, at] = g.astype(BF)
        ga_ref[0, :, at] = sv.astype(BF)
        gb_ref[0, :, at] = (g * (1.0 - sig)).astype(BF)


def middle_kernel(
    g_ref, halo_ref, x2_ref, cot_ref, dep, ig, si, wco, lg, ls, wu, wd, fg, fs,
    out_ref, dx3_ref, dg_ref, dhalo_ref, small_ref, ddep_ref, pack_ref,
    gx, cs, dcx, sp3, h4s, a4s, sp4, dz4s, dy4s, a3s, dy3s,
):
    rec = pl.program_id(0)
    rows = x2_ref.shape[1]
    channels = g_ref.shape[2]
    taps = dep.shape[0] - 1
    start_small(small_ref)
    start_small(ddep_ref)
    mine = pl.ds(pl.multiple_of(rec * rows, 128), rows)
    gx[0:16, :] = halo_ref[0].astype(F32)
    gx[16:, :] = g_ref[0].astype(F32)
    for c in range(channels // 128):
        at = slice(128 * c, 128 * c + 128)
        total = dep[0:1, at] * gx[2 : 2 + rows, at]
        for r in range(1, taps):
            total = total + dep[r : r + 1, at] * gx[2 + r : 2 + r + rows, at]
        cs[:, at] = total
    n3, inv3 = norm_parts(cs[...])
    cs[...] = n3
    w = n3 * row(ig) + row(si)
    sig = sigmoid(w)
    a3 = (w * sig).astype(BF)
    a3s[mine, :] = a3
    sp3[...] = (sig * (1.0 + w * (1.0 - sig))).astype(BF)
    x3 = x2_ref[0] + nn(a3, wco[...])
    n4, inv4 = norm_parts(x3)
    h4 = (n4 * row(lg) + row(ls)).astype(BF)
    h4s[mine, :] = h4
    y = None
    for f in range(wu.shape[1] // 512):
        at = slice(512 * f, 512 * f + 512)
        z = nn(h4, wu[:, at])
        sig = sigmoid(z)
        a = (z * sig).astype(BF)
        a4s[mine, at] = a
        sp4[:, at] = (sig * (1.0 + z * (1.0 - sig))).astype(BF)
        part = nn(a, wd[at, :])
        y = part if y is None else y + part
    x4 = x3 + 0.5 * y
    n5, inv5 = norm_parts(x4)
    out_ref[0] = (n5 * row(fg) + row(fs)).astype(BF)
    cot = cot_ref[0].astype(F32)
    add_rows(small_ref, 8, cot * n5)
    add_rows(small_ref, 9, cot)
    dx4 = norm_pull(n5, inv5, row(fg), cot)
    dy4 = (0.5 * dx4).astype(BF)
    dy4s[mine, :] = dy4
    dh = None
    for f in range(wu.shape[1] // 512):
        at = slice(512 * f, 512 * f + 512)
        dz = (nt(dy4, wd[at, :]) * sp4[:, at].astype(F32)).astype(BF)
        dz4s[mine, at] = dz
        part = nt(dz, wu[:, at])
        dh = part if dh is None else dh + part
    add_rows(small_ref, 6, dh * n4)
    add_rows(small_ref, 7, dh)
    dx3 = dx4 + norm_pull(n4, inv4, row(lg), dh)
    dx3_ref[0] = dx3
    dy3 = dx3.astype(BF)
    dy3s[mine, :] = dy3
    dw = nt(dy3, wco[...]) * sp3[...].astype(F32)
    n3 = cs[...]
    add_rows(small_ref, 2, dw * n3)
    add_rows(small_ref, 4, dw)
    dcx[0:16, :] = jnp.zeros((16, channels), F32)
    dcx[16 + rows :, :] = jnp.zeros((16, channels), F32)
    dcx[16 : 16 + rows, :] = norm_pull(n3, inv3, row(ig), dw)
    for c in range(channels // 128):
        at = slice(128 * c, 128 * c + 128)
        dc = dcx[16 : 16 + rows, at]
        for r in range(taps):
            ddep_ref[r : r + 1, at] += jnp.sum(
                dc * gx[2 + r : 2 + r + rows, at], axis=0, keepdims=True
            )
        total = dep[0:1, at] * dcx[14 : 30 + rows, at]
        for r in range(1, taps):
            total = total + dep[r : r + 1, at] * dcx[14 - r : 30 - r + rows, at]
        dhalo_ref[0, :, at] = total[0:16].astype(BF)
        dg_ref[0, :, at] = total[16:].astype(BF)

    @pl.when(rec == pl.num_programs(0) - 1)
    def _():
        count = pack_ref.shape[0]
        place = 0
        for f in range(wu.shape[1] // 512):
            at = slice(512 * f, 512 * f + 512)
            put_share(pack_ref, place, tn(h4s[...], dz4s[:, at]), 0, 1)
            place += 512 // count
        for f in range(wd.shape[0] // 512):
            at = slice(512 * f, 512 * f + 512)
            put_share(pack_ref, place, tn(a4s[:, at], dy4s[...]), f, wd.shape[0] // 512)
        place += wd.shape[0] // count
        for f in range(channels // 512):
            at = slice(512 * f, 512 * f + 512)
            put_share(pack_ref, place, tn(a3s[:, at], dy3s[...]), f, channels // 512)


def put_share(pack_ref, place, block, index, blocks):
    count = pack_ref.shape[0]
    height = 512 * blocks // count
    if height >= 512:
        shard, within = divmod(512 * index, height)
        pack_ref[shard, place + within : place + within + 512, :] = block.astype(BF)
        return
    held = 512 // height
    pack_ref[held * index : held * index + held, place : place + height, :] = block.reshape(
        held, height, 512
    ).astype(BF)


def ungate_kernel(
    dg_ref, back_ref, ga_ref, gb_ref, dx3_ref, x2_ref, g3, wc, wo,
    dx2_ref, du_ref, dy2_ref, do_ref, small_ref, dgx, *, nh,
):
    start_small(small_ref)
    rows = x2_ref.shape[1]
    channels = ga_ref.shape[2]
    dgx[...] = dg_ref[0].astype(F32)
    dgx[rows - 16 :, :] += back_ref[0].astype(F32)
    dh = None
    for f in range(channels // 512):
        at = slice(512 * f, 512 * f + 512)
        up = slice(channels + 512 * f, channels + 512 * f + 512)
        dg = dgx[:, at]
        lin = (dg * ga_ref[0, :, at].astype(F32)).astype(BF)
        gate = (dg * gb_ref[0, :, at].astype(F32)).astype(BF)
        du_ref[0, :, at] = lin
        du_ref[0, :, up] = gate
        part = nt(lin, wc[:, at]) + nt(gate, wc[:, up])
        dh = part if dh is None else dh + part
    n, inverse = norm_parts(x2_ref[0])
    add_rows(small_ref, 0, dh * n)
    add_rows(small_ref, 1, dh)
    dx2 = dx3_ref[0] + norm_pull(n, inverse, row(g3), dh)
    dx2_ref[0] = dx2
    dy2 = dx2.astype(BF)
    dy2_ref[0] = dy2

    def write(unit, part):
        do_ref[unit, 0, 0] = part

    put_heads(write, nt(dy2, wo[...]), nh)


def close_kernel(
    u_ref, h2_ref, x1_ref, dx2_ref, x_ref, h1_ref, a_ref, sp_ref, g1, wu, wd, g2, wi,
    out_ref, small_ref, pack_ref, dps, h2s, h1s, a1s, dzs, dys, *, nh,
):
    rec = pl.program_id(0)
    rows = x1_ref.shape[1]
    start_small(small_ref)
    mine = pl.ds(pl.multiple_of(rec * rows, 128), rows)
    h2s[mine, :] = h2_ref[0]
    h1s[mine, :] = h1_ref[0]
    a1s[mine, :] = a_ref[0]
    dh = None
    for kind in range(3):
        at = slice(512 * kind, 512 * kind + 512)
        dp = take_heads(lambda u: u_ref[u, 0, kind, 0], u_ref.shape[0], nh)
        dps[mine, at] = dp
        part = nt(dp, wi[:, at])
        dh = part if dh is None else dh + part
    n, inverse = norm_parts(x1_ref[0])
    add_rows(small_ref, 2, dh * n)
    add_rows(small_ref, 3, dh)
    dx1 = dx2_ref[0] + norm_pull(n, inverse, row(g2), dh)
    dy = (0.5 * dx1).astype(BF)
    dys[mine, :] = dy
    dh = None
    for f in range(wu.shape[1] // 512):
        at = slice(512 * f, 512 * f + 512)
        dz = (nt(dy, wd[at, :]) * sp_ref[0, :, at].astype(F32)).astype(BF)
        dzs[mine, at] = dz
        part = nt(dz, wu[:, at])
        dh = part if dh is None else dh + part
    n, inverse = norm_parts(x_ref[0].astype(F32))
    add_rows(small_ref, 0, dh * n)
    add_rows(small_ref, 1, dh)
    out_ref[0] = (dx1 + norm_pull(n, inverse, row(g1), dh)).astype(BF)

    @pl.when(rec == pl.num_programs(0) - 1)
    def _():
        count = pack_ref.shape[0]
        place = 0
        for f in range(wi.shape[1] // 512):
            at = slice(512 * f, 512 * f + 512)
            put_share(pack_ref, place, tn(h2s[...], dps[:, at]), 0, 1)
            place += 512 // count
        for f in range(wu.shape[1] // 512):
            at = slice(512 * f, 512 * f + 512)
            put_share(pack_ref, place, tn(h1s[...], dzs[:, at]), 0, 1)
            place += 512 // count
        for f in range(wd.shape[0] // 512):
            at = slice(512 * f, 512 * f + 512)
            put_share(pack_ref, place, tn(a1s[:, at], dys[...]), f, wd.shape[0] // 512)


def weights_kernel(h3_ref, du_ref, att_ref, dy_ref, pack_ref):
    count = pack_ref.shape[0]
    place = 0
    for f in range(du_ref.shape[1] // 512):
        at = slice(512 * f, 512 * f + 512)
        put_share(pack_ref, place, tn(h3_ref[...], du_ref[:, at]), 0, 1)
        place += 512 // count
    put_share(pack_ref, place, tn(att_ref[...], dy_ref[...]), 0, 1)


def per_rec(array):
    shape = (1,) + array.shape[1:]
    tail = (0,) * (array.ndim - 1)
    return pl.BlockSpec(shape, lambda r, *_: (r,) + tail)


def whole(array):
    zeros = (0,) * array.ndim
    return pl.BlockSpec(array.shape, lambda r, *_: zeros)


def per_unit(array, recs):
    units, rest = array.shape[0], array.shape[2:]
    if array.ndim == 6:
        return pl.BlockSpec(
            (units, 1, rest[0], 1) + rest[2:], lambda r, *_: (0, r // recs, 0, r % recs, 0, 0)
        )
    return pl.BlockSpec((units, 1, 1) + rest[1:], lambda r, *_: (0, r // recs, r % recs, 0, 0))


def spot(shape, kind=F32):
    return jax.ShapeDtypeStruct(shape, kind)


MEGA = 2**20


def run(kernel, seqs, ins, in_specs, outs, out_specs, scratch=(), prefetch=(), room=56):
    return pl.pallas_call(
        kernel,
        grid_spec=pltpu.PrefetchScalarGridSpec(
            num_scalar_prefetch=len(prefetch),
            grid=(seqs,),
            in_specs=in_specs,
            out_specs=out_specs,
            scratch_shapes=list(scratch),
        ),
        out_shape=outs,
        compiler_params=pltpu.CompilerParams(vmem_limit_bytes=room * MEGA),
    )(*prefetch, *ins)


def unit_plan(seqs, heads):
    parts = lax.axis_size("tm")
    if parts <= heads:
        return heads // parts, seqs, 1
    return 1, seqs * heads // parts, parts // heads


def distance_hot(seq_total, bucket_count):
    limits = jnp.array(boundaries(seq_total), jnp.int32)
    places = jnp.arange(seq_total, dtype=jnp.int32)
    bucket = jnp.sum((places[:, None] >= limits[None, :]).astype(jnp.int32), axis=1)
    return (bucket[:, None] == jnp.arange(bucket_count, dtype=jnp.int32)[None, :]).astype(FLOAT)


def bias_strip(table, hot, nh, split, local_frames):
    seq_total = hot.shape[0]
    first = lax.axis_index("tm") // split * nh
    mine = lax.dynamic_slice_in_dim(table, first, nh, 1)
    per = jnp.dot(hot, mine, precision=HIGHEST).T
    shifted = [
        jnp.pad(per, ((0, 0), (local_frames + s, 0)), constant_values=NEGATIVE)[
            :, : local_frames + seq_total
        ]
        for s in range(8)
    ]
    return make_strip(jnp.stack(shifted, 1), local_frames, seq_total)


def table_grad(diagonals, hot, nh, split, heads):
    seq_total = hot.shape[0]
    per = sum(
        jnp.pad(diagonals[:, s, s:], ((0, 0), (0, s))) for s in range(8)
    )
    mine = jnp.dot(hot.T, per.T, precision=HIGHEST)
    first = lax.axis_index("tm") // split * nh
    return lax.dynamic_update_slice_in_dim(
        jnp.zeros((hot.shape[1], heads), FLOAT), mine, first, 1
    )


def swap(values):
    return lax.all_to_all(values, "tm", 0, 0, tiled=True)


def total_over(packed):
    sent = packed.reshape((-1,) + packed.shape[2:])
    part = lax.psum_scatter(sent, "rows", scatter_dimension=0, tiled=True)
    return lax.psum(part, "tm")


def body(
    frames, cotangent, lengths,
    early_gain, early_shift, early_up, early_down,
    attend_gain, attend_shift, attend_input, attend_output, distance_bias,
    convolve_gain, convolve_shift, convolve_input, depthwise, inner_gain, inner_shift, convolve_output,
    late_gain, late_shift, late_up, late_down, final_gain, final_shift,
):
    seqs, rows, width = frames.shape
    heads = distance_bias.shape[1]
    count = lax.axis_size("rows")
    parts = lax.axis_size("tm")
    hidden = early_up.shape[1]
    channels = convolve_output.shape[0]
    nh, recs, split = unit_plan(seqs, heads)
    units = heads // nh
    flat = lambda v: v.reshape(1, -1)

    def wide(kinds):
        return spot((units, split, kinds, recs, rows, 128), BF)

    ins = (
        frames, flat(early_gain), flat(early_shift), early_up, early_down,
        flat(attend_gain), flat(attend_shift), attend_input,
    )
    outs = (
        spot((seqs, rows, width)), spot((seqs, rows, width), BF), spot((seqs, rows, hidden), BF),
        spot((seqs, rows, hidden), BF), spot((seqs, rows, width), BF), wide(3),
    )
    x1, h1, a1, sp1, h2, qkv = run(
        functools.partial(open_kernel, nh=nh), seqs, ins,
        [per_rec(frames)] + [whole(v) for v in ins[1:]],
        outs, [per_rec(v) for v in outs[:5]] + [per_unit(outs[5], recs)],
    )
    units_in = swap(qkv.reshape(parts, 3, recs, rows, 128))
    mine = lax.dynamic_slice_in_dim(lengths, lax.axis_index("tm") % split * recs, recs, 0)
    hot = distance_hot(rows * parts, distance_bias.shape[0])
    strip = bias_strip(distance_bias.astype(FLOAT), hot, nh, split, rows)
    out, out_t, lse = attn_fwd(mine, units_in, strip, nh)
    back = swap(out).reshape(units, split, recs, rows, 128)

    first = lax.axis_index("tm") * rows
    limits = jnp.concatenate([lengths, first[None].astype(jnp.int32)])
    ins = (back, x1, attend_output, flat(convolve_gain), flat(convolve_shift), convolve_input)
    outs = (
        spot((seqs, rows, width), BF), spot((seqs, rows, width)), spot((seqs, rows, width), BF),
        spot((seqs, rows, channels), BF), spot((seqs, rows, channels), BF), spot((seqs, rows, channels), BF),
    )
    att, x2, h3, g, ga, gb = run(
        functools.partial(gate_kernel, nh=nh), seqs, ins,
        [per_unit(back, recs), per_rec(x1)] + [whole(v) for v in ins[2:]],
        outs, [per_rec(v) for v in outs], prefetch=(limits,),
    )
    halo = passed_along(g[:, rows - 16 :, :], "tm", 1)

    dep = jnp.pad(depthwise.astype(FLOAT).T, ((0, 1), (0, 0)))
    ins = (
        g, halo, x2, cotangent, dep, flat(inner_gain), flat(inner_shift), convolve_output,
        flat(late_gain), flat(late_shift), late_up, late_down, flat(final_gain), flat(final_shift),
    )
    height = (width * hidden * 2 + channels * width) // 512 // count
    outs = (
        spot((seqs, rows, width), BF), spot((seqs, rows, width)), spot((seqs, rows, channels), BF),
        spot((seqs, 16, channels), BF), spot((16, 512)), spot((16, channels)), spot((count, height, 512), BF),
    )
    tokens = seqs * rows
    layer_out, dx3, dg, dhalo, small_mid, ddep, pack_mid = run(
        middle_kernel, seqs, ins,
        [per_rec(v) for v in ins[:4]] + [whole(v) for v in ins[4:]],
        outs, [per_rec(v) for v in outs[:4]] + [whole(v) for v in outs[4:]],
        scratch=(
            pltpu.VMEM((rows + 16, channels), F32), pltpu.VMEM((rows, channels), F32),
            pltpu.VMEM((rows + 32, channels), F32), pltpu.VMEM((rows, channels), BF),
            pltpu.VMEM((tokens, width), BF), pltpu.VMEM((tokens, hidden), BF), pltpu.VMEM((rows, hidden), BF),
            pltpu.VMEM((tokens, hidden), BF), pltpu.VMEM((tokens, width), BF),
            pltpu.VMEM((tokens, channels), BF), pltpu.VMEM((tokens, width), BF),
        ),
    )
    returned = passed_along(dhalo, "tm", -1)

    ins = (dg, returned, ga, gb, dx3, x2, flat(convolve_gain), convolve_input, attend_output)
    outs = (
        spot((seqs, rows, width)), spot((seqs, rows, 2 * channels), BF), spot((seqs, rows, width), BF),
        spot((units, split, recs, rows, 128), BF), spot((8, 512)),
    )
    dx2, du, dy2, do, small_gate = run(
        functools.partial(ungate_kernel, nh=nh), seqs, ins,
        [per_rec(v) for v in ins[:6]] + [whole(v) for v in ins[6:]],
        outs, [per_rec(v) for v in outs[:3]] + [per_unit(outs[3], recs), whole(outs[4])],
        scratch=(pltpu.VMEM((rows, channels), F32),),
    )
    grad_units = swap(do.reshape(parts, recs, rows, 128))
    merge = lambda v: v.reshape(tokens, -1)
    ins = (merge(h3), merge(du), merge(att), merge(dy2))
    outs = spot((count, (2 * channels * width + width * width) // 512 // count, 512), BF)
    pack_gate = run(weights_kernel, 1, ins, [whole(v) for v in ins], outs, whole(outs))
    grad_own, diagonals = attn_bwd(mine, units_in, grad_units, out_t, lse, strip, nh)
    grad_back = swap(grad_own).reshape(units, split, 3, recs, rows, 128)

    ins = (
        grad_back, h2, x1, dx2, frames, h1, a1, sp1,
        flat(early_gain), early_up, early_down, flat(attend_gain), attend_input,
    )
    height = (width * hidden * 2 + width * 3 * width) // 512 // count
    outs = (spot((seqs, rows, width), BF), spot((8, 512)), spot((count, height, 512), BF))
    dx0, small_open, pack_open = run(
        functools.partial(close_kernel, nh=nh), seqs, ins,
        [per_unit(grad_back, recs)] + [per_rec(v) for v in ins[1:8]] + [whole(v) for v in ins[8:]],
        outs, [per_rec(outs[0])] + [whole(v) for v in outs[1:]],
        scratch=(
            pltpu.VMEM((tokens, 3 * width), BF), pltpu.VMEM((tokens, width), BF), pltpu.VMEM((tokens, width), BF),
            pltpu.VMEM((tokens, hidden), BF), pltpu.VMEM((tokens, hidden), BF), pltpu.VMEM((tokens, width), BF),
        ),
    )
    grad_table = table_grad(diagonals, hot, nh, split, heads)

    lines = jnp.concatenate([small_open[:4], small_gate[:2], small_mid[:10]], axis=0)
    lines = jnp.transpose(lines.reshape(8, 2, count, 256 // count * 2 // 2), (2, 0, 1, 3)) if False else lines
    totals_mid = total_over(pack_mid)
    totals_gate = total_over(pack_gate)
    shape_small = (small_open, small_gate, small_mid, ddep, grad_table)
    small = pack_small(*shape_small, count)
    extra = small.shape[1]
    totals_open = total_over(jnp.concatenate([pack_open, small], axis=1))
    return finish(
        layer_out, dx0, totals_mid.astype(FLOAT), totals_gate.astype(FLOAT), totals_open.astype(FLOAT),
        count, width, hidden, channels, depthwise.shape[1], distance_bias.shape,
    )


def vectors(small_open, small_gate, small_mid):
    return [
        small_open[0:1], small_open[1:2], small_open[2:3], small_open[3:4],
        small_gate[0:1], small_gate[1:2], small_mid[2:4], small_mid[4:6],
        small_mid[6:7], small_mid[7:8], small_mid[8:9], small_mid[9:10],
    ]


def pack_small(small_open, small_gate, small_mid, ddep, grad_table, count):
    shares = [v.reshape(count, -1) for v in vectors(small_open, small_gate, small_mid)]
    shares.append(jnp.transpose(ddep.reshape(16, count, -1), (1, 0, 2)).reshape(count, -1))
    shares.append(grad_table.reshape(count, -1))
    line = jnp.concatenate(shares, axis=1)
    line = jnp.pad(line, ((0, 0), (0, -line.shape[1] % (64 * 512))))
    return line.reshape(count, -1, 512).astype(BF)


def columns(block, blocks):
    return jnp.concatenate(jnp.split(block, blocks, axis=0), axis=1)


def finish(layer_out, dx0, mid, gate, opened, count, width, hidden, channels, taps, table_shape):
    share = width // count
    wide = hidden // 512
    late_up = columns(mid[: share * wide], wide)
    late_down = mid[share * wide : share * wide + hidden // count]
    conv_out = mid[share * wide + hidden // count :]
    conv_in = columns(gate[: share * (2 * channels // 512)], 2 * channels // 512)
    attend_out = gate[share * (2 * channels // 512) :]
    attend_in = columns(opened[: 3 * share], 3)
    at = 3 * share
    early_up = columns(opened[at : at + share * wide], wide)
    at += share * wide
    early_down = opened[at : at + hidden // count]
    at += hidden // count
    line = opened[at:].reshape(-1)
    sizes = [share] * 6 + [channels // count] * 2 + [share] * 4
    got = []
    at = 0
    for size in sizes:
        got.append(line[at : at + size])
        at += size
    depth = line[at : at + 16 * channels // count].reshape(16, -1)[:taps].T
    at += 16 * channels // count
    table = line[at : at + table_shape[0] * table_shape[1] // count].reshape(-1, table_shape[1])
    return (
        layer_out, dx0, got[0], got[1], early_up, early_down, got[2], got[3], attend_in, attend_out, table,
        got[4], got[5], conv_in, depth, got[6], got[7], conv_out,
        got[8], got[9], late_up, late_down, got[10], got[11],
    )


def solution(mesh):
    placed = (
        P("rows", "tm", None),
        P("rows", "tm", None),
        P("rows"),
        P(),
        P(),
        P(),
        P(),
        P(),
        P(),
        P(),
        P(),
        P(),
        P(),
        P(),
        P(),
        P(),
        P(),
        P(),
        P(),
        P(),
        P(),
        P(),
        P(),
        P(),
        P(),
    )
    return jax.shard_map(
        body,
        mesh=mesh,
        in_specs=placed,
        out_specs=(
            P("rows", "tm", None),
            P("rows", "tm", None),
            P("rows"),
            P("rows"),
            P("rows", None),
            P("rows", None),
            P("rows"),
            P("rows"),
            P("rows", None),
            P("rows", None),
            P("rows", None),
            P("rows"),
            P("rows"),
            P("rows", None),
            P("rows", None),
            P("rows"),
            P("rows"),
            P("rows", None),
            P("rows"),
            P("rows"),
            P("rows", None),
            P("rows", None),
            P("rows"),
            P("rows"),
        ),
        check_vma=False,
    )
```

```python
import functools

import jax
import jax.numpy as jnp
from jax import lax
from jax.experimental import pallas as pl
from jax.experimental.pallas import tpu as pltpu
from jax.sharding import PartitionSpec as P

EPSILON = 1e-05
NEGATIVE = -1e30
HIGHEST = lax.Precision.HIGHEST
BFLOAT = jnp.bfloat16
FLOAT = jnp.float32
NEG = NEGATIVE
F32 = FLOAT
BF = BFLOAT


MEGA = 2**20
SCALE = 1


def cost(micros):
    micros = micros * SCALE
    return pl.CostEstimate(
        flops=int(micros * 1.1e9), bytes_accessed=int(micros * 3.6e6), transcendentals=0
    )


def passed_along(block, axis, distance):
    devices = range(lax.axis_size(axis))
    route = [(i - distance, i) for i in devices if i - distance in devices]
    return lax.ppermute(block, axis, route)


def boundaries(seq_total):
    edges_list = list(range(1, 16))
    for exponent in range(16):
        edges_list.append(int(16.0 * (seq_total / 16.0) ** (exponent / 16.0)))
    return edges_list


KEYS = 256
QUERIES = 512


def nt(a, b):
    return lax.dot_general(a, b, (((1,), (1,)), ((), ())), preferred_element_type=F32)


def nn(a, b):
    return lax.dot_general(a, b, (((1,), (0,)), ((), ())), preferred_element_type=F32)


def strip_kernel(base_ref, out_ref):
    heads, keys, _ = out_ref.shape
    for h in range(heads):
        base = base_ref[h]
        for g in range(keys // 8):
            out_ref[h, 8 * g : 8 * g + 8, :] = pltpu.roll(base, 8 * g, 1)[:, keys:] if g else base[:, keys:]


def make_strip(base):
    heads, _, wide = base.shape
    return pl.pallas_call(
        strip_kernel,
        out_shape=jax.ShapeDtypeStruct((heads, KEYS, wide - KEYS), F32),
        compiler_params=pltpu.CompilerParams(vmem_limit_bytes=58 * MEGA),
        cost_estimate=cost(3),
    )(base)


def head_lanes(shape, h):
    lane = lax.broadcasted_iota(jnp.int32, shape, 1)
    return (lane >= 64 * h) & (lane < 64 * h + 64), lane == ((64 * h + 64) % 128)


def masked_queries(q, h):
    mine, spare = head_lanes(q.shape, h)
    return jnp.where(mine, q, jnp.where(spare, 1.0, 0.0)).astype(BF)


def masked_keys(k, h, first, length):
    mine, spare = head_lanes(k.shape, h)
    beyond = first + lax.broadcasted_iota(jnp.int32, k.shape, 0) >= length
    return jnp.where(mine, k, jnp.where(spare & beyond, NEG, 0.0)).astype(BF)


def block_of(index, size):
    return pl.ds(pl.multiple_of(index * size, 128), size)


def loop(first, last, step):
    def turn(index, carried):
        step(index)
        return carried

    lax.fori_loop(first, last, turn, 0)


def attend_kernel(len_ref, x_ref, strip_ref, o_ref, lse_ref, kh, vt, qh, acc, ot, *, nh):
    parts, rows = x_ref.shape[0], x_ref.shape[3]
    total = parts * rows
    length = len_ref[pl.program_id(0)]

    def prepare(t):
        at = block_of(t, rows)
        q = x_ref[t, 0, 0].astype(F32) * 0.125
        k = x_ref[t, 1, 0].astype(F32)
        v = x_ref[t, 2, 0].astype(F32).T.astype(BF)
        for h in range(nh):
            qh[h, at, :] = masked_queries(q, h)
            kh[h, at, :] = masked_keys(k, h, t * rows, length)
            vt[h, 0:64, at] = v[64 * h : 64 * h + 64]
            ones = lax.broadcasted_iota(jnp.int32, (16, rows), 0) == 0
            vt[h, 64:80, at] = jnp.where(ones, 1.0, 0.0).astype(BF)

    loop(0, parts, prepare)

    def queries(qb):
        at = block_of(qb, QUERIES)
        for h in range(nh):
            acc[h] = jnp.zeros((80, QUERIES), F32)

        def keys(kb, peaks):
            there = block_of(kb, QUERIES)
            after = []
            for h in range(nh):
                scores = []
                for half in range(QUERIES // KEYS):
                    first = kb * QUERIES + half * KEYS
                    off = pl.ds(pl.multiple_of(KEYS + qb * QUERIES - first, 128), QUERIES)
                    k = kh[h, pl.ds(pl.multiple_of(first, 128), KEYS), :]
                    scores.append(nt(k, qh[h, at, :]) + strip_ref[h, :, off])
                peak = peaks[h]
                for s in scores:
                    peak = jnp.maximum(peak, jnp.max(s, axis=0, keepdims=True))
                p = jnp.concatenate([jnp.exp(s - peak).astype(BF) for s in scores], axis=0)
                acc[h] = acc[h] * jnp.exp(peaks[h] - peak) + nn(vt[h, :, there], p)
                after.append(peak)
            return tuple(after)

        last = jnp.minimum(qb + 1, (length + QUERIES - 1) // QUERIES)
        peaks = lax.fori_loop(
            0, last, keys, tuple(jnp.full((1, QUERIES), NEG, F32) for _ in range(nh))
        )
        for h in range(nh):
            sums = acc[h, 64:65, :]
            lse_ref[0, h, :, at] = peaks[h] + jnp.log(sums)
            ot[64 * h : 64 * h + 64, at] = acc[h, 0:64, :] / sums
        if nh == 1:
            ot[64:128, at] = jnp.zeros((64, QUERIES), F32)

    loop(0, total // QUERIES, queries)

    def give(t):
        o_ref[t, 0] = ot[:, block_of(t, rows)].T.astype(BF)

    loop(0, parts, give)


def once(shape):
    zeros = (0,) * len(shape)
    return pl.BlockSpec(shape, lambda r, l: zeros, pipeline_mode=pl.Buffered(1))


def attn_fwd(lengths, x, strip, nh):
    parts, _, recs, rows, wide = x.shape
    total = parts * rows
    return pl.pallas_call(
        functools.partial(attend_kernel, nh=nh),
        grid_spec=pltpu.PrefetchScalarGridSpec(
            num_scalar_prefetch=1,
            grid=(recs,),
            in_specs=[
                pl.BlockSpec((parts, 3, 1, rows, wide), lambda r, l: (0, 0, r, 0, 0)), once(strip.shape),
            ],
            out_specs=[
                pl.BlockSpec((parts, 1, rows, wide), lambda r, l: (0, r, 0, 0)),
                pl.BlockSpec((1, nh, 1, total), lambda r, l: (r, 0, 0, 0)),
            ],
            scratch_shapes=[
                pltpu.VMEM((nh, total, wide), BF), pltpu.VMEM((nh, 80, total), BF),
                pltpu.VMEM((nh, total, wide), BF), pltpu.VMEM((nh, 80, QUERIES), F32),
                pltpu.VMEM((wide, total), F32),
            ],
        ),
        out_shape=[
            jax.ShapeDtypeStruct((parts, recs, rows, wide), BF),
            jax.ShapeDtypeStruct((recs, nh, 1, total), F32),
        ],
        compiler_params=pltpu.CompilerParams(vmem_limit_bytes=58 * MEGA),
        cost_estimate=cost(11),
    )(lengths, x, strip)


def attend_back_kernel(
    len_ref, x_ref, do_ref, o_ref, lse_ref, strip_ref, dx_ref, db_ref,
    kh, vh, qh, qs, dos, kt, dqt, delta, dk, dv, dks, dvs, dbs, *, nh,
):
    parts, rows = x_ref.shape[0], x_ref.shape[3]
    total = parts * rows
    length = len_ref[pl.program_id(0)]
    blocks = (length + KEYS - 1) // KEYS

    @pl.when(pl.program_id(0) == 0)
    def _():
        dbs[...] = jnp.zeros_like(dbs)

    dqt[...] = jnp.zeros_like(dqt)

    def prepare(t):
        at = block_of(t, rows)
        q = x_ref[t, 0, 0].astype(F32) * 0.125
        k = x_ref[t, 1, 0].astype(F32)
        v = x_ref[t, 2, 0].astype(F32)
        do = do_ref[t, 0]
        qs[at, :] = q.astype(BF)
        dos[at, :] = do
        kt[:, at] = k.T.astype(BF)
        product = (do.astype(F32) * o_ref[t, 0].astype(F32)).T
        for h in range(nh):
            qh[h, at, :] = masked_queries(q, h)
            kh[h, at, :] = masked_keys(k, h, t * rows, length)
            vh[h, at, :] = jnp.where(head_lanes(v.shape, h)[0], v, 0.0).astype(BF)
            delta[h, :, at] = jnp.sum(product[64 * h : 64 * h + 64], axis=0, keepdims=True)

    loop(0, parts, prepare)

    def keys(kb):
        there = block_of(kb, KEYS)
        dk[...] = jnp.zeros_like(dk)
        dv[...] = jnp.zeros_like(dv)

        def queries(qb):
            at = block_of(qb, QUERIES)
            off = pl.ds(pl.multiple_of(KEYS + qb * QUERIES - kb * KEYS, 128), QUERIES)
            for h in range(nh):
                s = nt(kh[h, there, :], qh[h, at, :]) + strip_ref[h, :, off]
                p = jnp.exp(s - lse_ref[0, h, :, at])
                ds = p * (nt(vh[h, there, :], dos[at, :]) - delta[h, :, at])
                low = ds.astype(BF)
                dv[h] += nn(p.astype(BF), dos[at, :])
                dk[h] += nn(low, qs[at, :])
                dqt[64 * h : 64 * h + 64, at] += nn(kt[64 * h : 64 * h + 64, there], low)
                dbs[h, :, off] += ds

        loop(kb * KEYS // QUERIES, total // QUERIES, queries)
        first, _ = head_lanes((KEYS, 128), 0)
        dks[there, :] = (jnp.where(first, dk[0], dk[1]) if nh == 2 else dk[0]).astype(BF)
        dvs[there, :] = (jnp.where(first, dv[0], dv[1]) if nh == 2 else dv[0]).astype(BF)

    loop(0, blocks, keys)

    def nothing(kb):
        dks[block_of(kb, KEYS), :] = jnp.zeros((KEYS, 128), BF)
        dvs[block_of(kb, KEYS), :] = jnp.zeros((KEYS, 128), BF)

    loop(blocks, total // KEYS, nothing)

    def give(t):
        at = block_of(t, rows)
        dx_ref[t, 0, 0] = (dqt[:, at] * 0.125).T.astype(BF)
        dx_ref[t, 1, 0] = dks[at, :]
        dx_ref[t, 2, 0] = dvs[at, :]

    loop(0, parts, give)

    @pl.when(pl.program_id(0) == pl.num_programs(0) - 1)
    def _():
        wide = dbs.shape[2]
        for h in range(nh):
            sums = dbs[h, 0:8, :]
            for g in range(1, KEYS // 8):
                sums = sums + pltpu.roll(dbs[h, 8 * g : 8 * g + 8, :], wide - 8 * g, 1)
            db_ref[h] = sums


def attn_bwd(lengths, x, do, o, lse, strip, nh):
    parts, _, recs, rows, wide = x.shape
    total = parts * rows
    several = pltpu.VMEM((nh, total, wide), BF)
    single = pltpu.VMEM((total, wide), BF)
    part = pltpu.VMEM((nh, KEYS, wide), F32)
    return pl.pallas_call(
        functools.partial(attend_back_kernel, nh=nh),
        grid_spec=pltpu.PrefetchScalarGridSpec(
            num_scalar_prefetch=1,
            grid=(recs,),
            in_specs=[
                pl.BlockSpec((parts, 3, 1, rows, wide), lambda r, l: (0, 0, r, 0, 0)),
                pl.BlockSpec((parts, 1, rows, wide), lambda r, l: (0, r, 0, 0)),
                pl.BlockSpec((parts, 1, rows, wide), lambda r, l: (0, r, 0, 0)),
                pl.BlockSpec((1, nh, 1, total), lambda r, l: (r, 0, 0, 0)),
                once(strip.shape),
            ],
            out_specs=[
                pl.BlockSpec((parts, 3, 1, rows, wide), lambda r, l: (0, 0, r, 0, 0)),
                pl.BlockSpec((nh, 8, strip.shape[2]), lambda r, l: (0, 0, 0)),
            ],
            scratch_shapes=[
                several, several, several, single, single, pltpu.VMEM((wide, total), BF),
                pltpu.VMEM((wide, total), F32), pltpu.VMEM((nh, 1, total), F32), part, part, single, single,
                pltpu.VMEM(strip.shape, F32),
            ],
        ),
        out_shape=[
            jax.ShapeDtypeStruct((parts, 3, recs, rows, wide), BF),
            jax.ShapeDtypeStruct((nh, 8, strip.shape[2]), F32),
        ],
        compiler_params=pltpu.CompilerParams(vmem_limit_bytes=58 * MEGA),
        cost_estimate=cost(15),
    )(lengths, x, do, o, lse, strip)


def tn(a, b):
    return lax.dot_general(a, b, (((0,), (0,)), ((), ())), preferred_element_type=F32)


def sigmoid(v):
    return 0.5 * jnp.tanh(0.5 * v) + 0.5


LINES = {
    "early_gain": 0, "early_shift": 1, "attend_gain": 2, "attend_shift": 3, "convolve_gain": 4, "convolve_shift": 5,
    "late_gain": 6, "late_shift": 7, "final_gain": 8, "final_shift": 9, "inner_gain": 10,
}


def row(ref, name):
    place = LINES[name]
    return ref[place : place + 1, :]


def broad_row(ref, name, width):
    blocks = width // 512
    place = LINES["inner_gain"] + (blocks if name == "inner_shift" else 0)
    return jnp.concatenate([ref[place + c : place + c + 1, :] for c in range(blocks)], axis=1)


def part_of(index, size=512):
    return pl.ds(pl.multiple_of(index * size, 128), size)


def repeat(count, step):
    def turn(index, carried):
        step(index)
        return carried

    lax.fori_loop(0, count, turn, 0)


def mover(sems):
    spent = []

    def move(source, target):
        copy = pltpu.make_async_copy(source, target, sems.at[len(spent)])
        spent.append(copy)
        copy.start()
        return copy

    return move


def pieces(width):
    return [slice(first, first + 512) for first in range(0, width, 512)]


def settle(copies):
    for copy in copies:
        copy.wait()


def feed(h, wu, wd, up, down, keep):
    y = None
    for f, at in enumerate(pieces(wu.shape[1])):
        up(f)
        z = nn(h, wu[:, at])
        sig = sigmoid(z)
        a = (z * sig).astype(BF)
        keep(at, a, (sig * (1.0 + z * (1.0 - sig))).astype(BF))
        down(f)
        part = nn(a, wd[at, :])
        y = part if y is None else y + part
    return y


def feed_back(dy, wu, wd, up, down, slope, keep):
    dh = None
    for f, at in enumerate(pieces(wu.shape[1])):
        down(f)
        dz = (nt(dy, wd[at, :]) * slope(f, at).astype(F32)).astype(BF)
        keep(at, dz)
        up(f)
        part = nt(dz, wu[:, at])
        dh = part if dh is None else dh + part
    return dh


def share_columns(send, held, place, left, right, ready):
    count = held.shape[0] * held.shape[1]
    height = left.shape[1] // count
    for f, at in enumerate(pieces(right.shape[1])):
        ready(f)
        there = slice(place, place + height)
        block = tn(left[...], right[:, at]).astype(BF)
        held[:, :, there, :] = block.reshape(held.shape[:2] + (height, 512))
        send(slice(0, held.shape[0]), there)
        place += height
    return place


def share_rows(send, held, place, left, right, ready):
    height = left.shape[1] // (held.shape[0] * held.shape[1])
    each = 512 // (held.shape[1] * height)
    for f, at in enumerate(pieces(left.shape[1])):
        ready(f)
        who, there = slice(each * f, each * f + each), slice(place, place + height)
        block = tn(left[:, at], right[...]).astype(BF)
        held[who, :, there, :] = block.reshape(each, held.shape[1], height, 512)
        send(who, there)
    return place + height


def norm_parts(v):
    center = v - jnp.mean(v, axis=-1, keepdims=True)
    inverse = lax.rsqrt(jnp.mean(center * center, axis=-1, keepdims=True) + EPSILON)
    return center * inverse, inverse


def norm_pull(n, inverse, gain, grad):
    dn = grad * gain
    return (
        dn - jnp.mean(dn, axis=-1, keepdims=True) - n * jnp.mean(dn * n, axis=-1, keepdims=True)
    ) * inverse


def add_rows(ref, place, values):
    total = jnp.sum(values, axis=0, keepdims=True)
    for c in range(values.shape[1] // 512):
        ref[place + c : place + c + 1, :] += total[:, 512 * c : 512 * c + 512]


def start_small(ref):
    @pl.when(pl.program_id(0) == 0)
    def _():
        ref[...] = jnp.zeros_like(ref)


def put_heads(write, value, nh):
    for pair in range(value.shape[1] // 128):
        part = value[:, 128 * pair : 128 * pair + 128]
        if nh == 2:
            write(pair, part.astype(BF))
        else:
            low = lax.broadcasted_iota(jnp.int32, part.shape, 1) < 64
            write(2 * pair, jnp.where(low, part, 0.0).astype(BF))
            write(2 * pair + 1, jnp.where(low, pltpu.roll(part, 64, 1), 0.0).astype(BF))


def take_heads(read, units, nh):
    if nh == 2:
        return jnp.concatenate([read(u) for u in range(units)], axis=1)
    pairs = [
        (read(2 * u).astype(F32) + pltpu.roll(read(2 * u + 1).astype(F32), 64, 1)).astype(BF)
        for u in range(units // 2)
    ]
    return jnp.concatenate(pairs, axis=1)


def lines_kernel(*refs):
    out = refs[-1]
    out[...] = jnp.zeros_like(out)
    place = 0
    for ref in refs[:-1]:
        for c in range(ref.shape[0] // 512):
            out[place : place + 1, :] = ref[512 * c : 512 * c + 512].astype(F32).reshape(1, 512)
            place += 1


def open_kernel(
    x_ref, lines, wu, wd, wi, x1_ref, h1_ref, a_ref, sp_ref, h2_ref, u_ref,
    wuv, wdv, wiv, x1v, h1v, av, spv, h2v, uv, sems, *, nh, first, recs,
):
    turn = pl.program_id(0)
    rec = first + turn
    move = mover(sems)
    up, down = [], []
    for at in pieces(wu.shape[1]):
        up.append(move(wu.at[:, at], wuv.at[:, at]))
        down.append(move(wd.at[at, :], wdv.at[at, :]))
    wide = [move(wi.at[:, at], wiv.at[:, at]) for at in pieces(wi.shape[1])]
    x0 = x_ref[0].astype(F32)
    n, _ = norm_parts(x0)
    h1 = (n * row(lines, "early_gain") + row(lines, "early_shift")).astype(BF)
    h1v[...] = h1
    sent = [move(h1v, h1_ref.at[rec])]

    def keep(at, a, slope):
        av[:, at] = a
        spv[:, at] = slope
        sent.append(move(av.at[:, at], a_ref.at[rec, :, at]))
        sent.append(move(spv.at[:, at], sp_ref.at[rec, :, at]))

    y = feed(h1, wuv, wdv, lambda f: up[f].wait(), lambda f: down[f].wait(), keep)
    x1 = x0 + 0.5 * y
    x1v[...] = x1
    sent.append(move(x1v, x1_ref.at[rec]))
    n, _ = norm_parts(x1)
    h2 = (n * row(lines, "attend_gain") + row(lines, "attend_shift")).astype(BF)
    h2v[...] = h2
    sent.append(move(h2v, h2_ref.at[rec]))
    for kind, at in enumerate(pieces(wi.shape[1])):

        def write(unit, part):
            uv[unit, kind] = part

        wide[kind].wait()
        put_heads(write, nn(h2, wiv[:, at]), nh)
        sent.append(move(uv.at[:, kind], u_ref.at[:, turn // recs, kind, turn % recs]))
    settle(sent)


def gate_kernel(
    len_ref, o_ref, x1_ref, lines, wo, wc, att_ref, x2_ref, h3_ref, g_ref, ga_ref, gb_ref,
    wov, wcv, attv, x2v, h3v, gv, gav, gbv, sems, *, nh, first,
):
    rec = first + pl.program_id(0)
    move = mover(sems)
    channels = g_ref.shape[2]
    narrow = move(wo, wov)
    linear, gates = [], []
    for at in pieces(channels):
        up = slice(channels + at.start, channels + at.stop)
        linear.append(move(wc.at[:, at], wcv.at[:, at]))
        gates.append(move(wc.at[:, up], wcv.at[:, up]))
    units = o_ref.shape[0]
    rows = x1_ref.shape[1]
    att = take_heads(lambda u: o_ref[u, 0, 0], units, nh)
    attv[...] = att
    sent = [move(attv, att_ref.at[rec])]
    narrow.wait()
    x2 = x1_ref[0] + nn(att, wov[...])
    x2v[...] = x2
    sent.append(move(x2v, x2_ref.at[rec]))
    n, _ = norm_parts(x2)
    h3 = (n * row(lines, "convolve_gain") + row(lines, "convolve_shift")).astype(BF)
    h3v[...] = h3
    sent.append(move(h3v, h3_ref.at[rec]))
    limit = len_ref[rec]
    place = lax.broadcasted_iota(jnp.int32, (rows, 1), 0)
    valid = jnp.where(place < limit, 1.0, 0.0)
    for f, at in enumerate(pieces(channels)):
        linear[f].wait()
        lin = nn(h3, wcv[:, at])
        gates[f].wait()
        gate = nn(h3, wcv[:, channels + at.start : channels + at.stop])
        sig = sigmoid(gate)
        sv = sig * valid
        g = lin * sv
        gv[:, at] = g.astype(BF)
        gav[:, at] = sv.astype(BF)
        gbv[:, at] = (g * (1.0 - sig)).astype(BF)
        for held, out in ((gv, g_ref), (gav, ga_ref), (gbv, gb_ref)):
            sent.append(move(held.at[:, at], out.at[rec, :, at]))
    settle(sent)


def middle_kernel(
    g_ref, halo_ref, x2_ref, cot_ref, dep, lines, wco, wu, wd,
    out_ref, dx3_ref, dg_ref, dhalo_ref, small_ref, ddep_ref, pack_ref,
    gx, cs, inv3, dcx, sp3, h4s, a4s, sp4, dz4s, dy4s, a3s, dy3s, tapped, dws, wcov, wuv, wdv, held, sems, out_sems,
):
    rec = pl.program_id(0)
    rows = x2_ref.shape[1]
    channels = g_ref.shape[2]
    lanes = channels // 128
    taps = dep.shape[0] - 1
    start_small(small_ref)
    start_small(tapped)
    first = pl.multiple_of(rec * rows, 128)
    mine = pl.ds(first, rows)
    tile = 96
    fetched = [(wco, wcov)]
    for at in pieces(wu.shape[1]):
        fetched.append((wu.at[:, at], wuv.at[:, at]))
        fetched.append((wd.at[at, :], wdv.at[at, :]))
    fetched = [pltpu.make_async_copy(*pair, sems.at[k]) for k, pair in enumerate(fetched)]

    @pl.when(rec == 0)
    def _():
        for copy in fetched:
            copy.start()

    def ready(k):
        @pl.when(rec == 0)
        def _():
            fetched[k].wait()


    def conv(c):
        at = part_of(c, 128)
        gx[c, 0:16, :] = halo_ref[0, :, at].astype(F32)
        gx[c, 16:, :] = g_ref[0, :, at].astype(F32)
        for top in range(0, rows, tile):
            sums = dep[0:1, at] * gx[c, top + 2 : top + 2 + tile, :]
            for r in range(1, taps):
                sums = sums + dep[r : r + 1, at] * gx[c, top + 2 + r : top + 2 + r + tile, :]
            cs[top : top + tile, at] = sums

    repeat(lanes, conv)

    def inner(t):
        there = pl.ds(pl.multiple_of(t * 64, 64), 64)
        n, inverse = norm_parts(cs[there, :])
        cs[there, :] = n
        inv3[there, :] = inverse
        w = n * broad_row(lines, "inner_gain", channels) + broad_row(lines, "inner_shift", channels)
        sig = sigmoid(w)
        a3s[pl.ds(first + pl.multiple_of(t * 64, 64), 64), :] = (w * sig).astype(BF)
        sp3[there, :] = (sig * (1.0 + w * (1.0 - sig))).astype(BF)

    repeat(rows // 64, inner)
    ready(0)
    x3 = x2_ref[0] + nn(a3s[mine, :], wcov[...])
    n4, inv4 = norm_parts(x3)
    h4 = (n4 * row(lines, "late_gain") + row(lines, "late_shift")).astype(BF)
    h4s[mine, :] = h4

    def keep(at, a, slope):
        a4s[mine, at] = a
        sp4[:, at] = slope

    y = feed(h4, wuv, wdv, lambda f: ready(1 + 2 * f), lambda f: ready(2 + 2 * f), keep)
    x4 = x3 + 0.5 * y
    n5, inv5 = norm_parts(x4)
    out_ref[0] = (n5 * row(lines, "final_gain") + row(lines, "final_shift")).astype(BF)
    cot = cot_ref[0].astype(F32)
    add_rows(small_ref, 8, cot * n5)
    add_rows(small_ref, 9, cot)
    dx4 = norm_pull(n5, inv5, row(lines, "final_gain"), cot)
    dx3_ref[0] = dx4
    dy4 = (0.5 * dx4).astype(BF)
    dy4s[mine, :] = dy4

    def keep_back(at, dz):
        dz4s[mine, at] = dz

    done = lambda f: None
    dh = feed_back(dy4, wuv, wdv, done, done, lambda f, at: sp4[:, at], keep_back)
    add_rows(small_ref, 6, dh * n4)
    add_rows(small_ref, 7, dh)
    dx3 = dx3_ref[0] + norm_pull(n4, inv4, row(lines, "late_gain"), dh)
    dx3_ref[0] = dx3
    dy3s[mine, :] = dx3.astype(BF)

    def pull(f):
        at = part_of(f)
        dws[:, at] = nt(dy3s[mine, :], wcov[at, :]) * sp3[:, at].astype(F32)

    repeat(channels // 512, pull)

    def inner_back(t):
        there = pl.ds(pl.multiple_of(t * 64, 64), 64)
        dw = dws[there, :]
        n = cs[there, :]
        add_rows(small_ref, 2, dw * n)
        add_rows(small_ref, 4, dw)
        cs[there, :] = norm_pull(n, inv3[there, :], broad_row(lines, "inner_gain", channels), dw)

    repeat(rows // 64, inner_back)

    def conv_back(c):
        at = part_of(c, 128)
        dcx[0:16, :] = jnp.zeros((16, 128), F32)
        dcx[16 : 16 + rows, :] = cs[:, at]
        dcx[16 + rows :, :] = jnp.zeros((16, 128), F32)
        sums = [jnp.zeros((8, 128), F32)] * taps
        for top in range(0, rows, tile):
            dc = dcx[16 + top : 16 + top + tile, :]
            for r in range(taps):
                term = dc * gx[c, top + 2 + r : top + 2 + r + tile, :]
                sums[r] = sums[r] + jnp.sum(term.reshape(tile // 8, 8, 128), axis=0)
        for r in range(taps):
            tapped[c, 8 * r : 8 * r + 8, :] += sums[r]
        for top in range(0, rows + 16, tile):
            size = min(tile, rows + 16 - top)
            sums = dep[0:1, at] * dcx[top + 14 : top + 14 + size, :]
            for r in range(1, taps):
                sums = sums + dep[r : r + 1, at] * dcx[top + 14 - r : top + 14 - r + size, :]
            if top == 0:
                dhalo_ref[0, :, at] = sums[0:16].astype(BF)
                dg_ref[0, 0 : size - 16, at] = sums[16:].astype(BF)
            else:
                dg_ref[0, top - 16 : top - 16 + size, at] = sums.astype(BF)

    repeat(lanes, conv_back)

    @pl.when(rec == pl.num_programs(0) - 1)
    def _():
        def depth(c):
            for r in range(taps):
                ddep_ref[r : r + 1, part_of(c, 128)] = jnp.sum(
                    tapped[c, 8 * r : 8 * r + 8, :], axis=0, keepdims=True
                )

        ddep_ref[taps:, :] = jnp.zeros((1, channels), F32)
        repeat(lanes, depth)
        move = mover(out_sems)
        sent = []

        def send(who, there):
            sent.append(move(held.at[who, :, there], pack_ref.at[who, :, there]))

        place = share_columns(send, held, 0, h4s, dz4s, done)
        place = share_rows(send, held, place, a4s, dy4s, done)
        share_rows(send, held, place, a3s, dy3s, done)
        settle(sent)


def ungate_kernel(
    dg_ref, back_ref, ga_ref, gb_ref, dx3_ref, x2_ref, lines, wc, wo,
    dx2_ref, du_ref, dy2_ref, do_ref, small_ref,
    wcv, wov, gav, gbv, dx3v, x2v, dx2v, duv, dy2v, dov, dgx, sems, *, nh, first, recs,
):
    turn = pl.program_id(0)
    rec = first + turn
    move = mover(sems)
    start_small(small_ref)
    rows = x2v.shape[0]
    channels = gav.shape[1]
    fetched = []
    for at in pieces(channels):
        up = slice(channels + at.start, channels + at.stop)
        fetched.append(
            [
                move(ga_ref.at[rec, :, at], gav.at[:, at]), move(gb_ref.at[rec, :, at], gbv.at[:, at]),
                move(wc.at[:, at], wcv.at[:, at]), move(wc.at[:, up], wcv.at[:, up]),
            ]
        )
    later = [move(x2_ref.at[rec], x2v), move(dx3_ref.at[rec], dx3v), move(wo, wov)]
    dgx[...] = dg_ref[0].astype(F32)
    dgx[rows - 16 :, :] += back_ref[0].astype(F32)
    sent = []
    dh = None
    for f, at in enumerate(pieces(channels)):
        up = slice(channels + at.start, channels + at.stop)
        settle(fetched[f])
        dg = dgx[:, at]
        lin = (dg * gav[:, at].astype(F32)).astype(BF)
        gate = (dg * gbv[:, at].astype(F32)).astype(BF)
        duv[:, at] = lin
        duv[:, up] = gate
        sent.append(move(duv.at[:, at], du_ref.at[rec, :, at]))
        sent.append(move(duv.at[:, up], du_ref.at[rec, :, up]))
        part = nt(lin, wcv[:, at]) + nt(gate, wcv[:, up])
        dh = part if dh is None else dh + part
    settle(later)
    n, inverse = norm_parts(x2v[...])
    add_rows(small_ref, 0, dh * n)
    add_rows(small_ref, 1, dh)
    dx2 = dx3v[...] + norm_pull(n, inverse, row(lines, "convolve_gain"), dh)
    dx2v[...] = dx2
    sent.append(move(dx2v, dx2_ref.at[rec]))
    dy2 = dx2.astype(BF)
    dy2v[...] = dy2
    sent.append(move(dy2v, dy2_ref.at[rec]))

    def write(unit, part):
        dov[unit] = part

    put_heads(write, nt(dy2, wov[...]), nh)
    sent.append(move(dov, do_ref.at[:, turn // recs, turn % recs]))
    settle(sent)


def project_kernel(
    u_ref, x1_ref, dx2_ref, lines, wi, dx1_ref, dy_ref, dp_ref, small_ref,
    wiv, uv, x1v, dx2v, dx1v, dyv, dpv, sems, *, nh, first, recs,
):
    turn = pl.program_id(0)
    rec = first + turn
    move = mover(sems)
    start_small(small_ref)
    fetched = []
    for kind, at in enumerate(pieces(wi.shape[1])):
        fetched.append(move(u_ref.at[:, turn // recs, kind, turn % recs], uv.at[:, kind]))
        fetched.append(move(wi.at[:, at], wiv.at[:, at]))
    later = [move(x1_ref.at[rec], x1v), move(dx2_ref.at[rec], dx2v)]
    sent = []
    dh = None
    for kind, at in enumerate(pieces(wi.shape[1])):
        settle(fetched[2 * kind : 2 * kind + 2])
        dp = take_heads(lambda u: uv[u, kind], u_ref.shape[0], nh)
        dpv[:, at] = dp
        sent.append(move(dpv.at[:, at], dp_ref.at[rec, :, at]))
        part = nt(dp, wiv[:, at])
        dh = part if dh is None else dh + part
    settle(later)
    n, inverse = norm_parts(x1v[...])
    add_rows(small_ref, 0, dh * n)
    add_rows(small_ref, 1, dh)
    dx1 = dx2v[...] + norm_pull(n, inverse, row(lines, "attend_gain"), dh)
    dx1v[...] = dx1
    dyv[...] = (0.5 * dx1).astype(BF)
    sent += [move(dx1v, dx1_ref.at[rec]), move(dyv, dy_ref.at[rec])]
    settle(sent)


def close_kernel(
    dy_ref, dx1_ref, x_ref, sp_ref, lines, wu, wd, out_ref, dz_ref, small_ref,
    wuv, wdv, spv, dx1v, xv, dzv, sems, *, first,
):
    rec = first + pl.program_id(0)
    move = mover(sems)
    start_small(small_ref)
    up, down, slopes = [], [], []
    for at in pieces(wu.shape[1]):
        down.append(move(wd.at[at, :], wdv.at[at, :]))
        slopes.append(move(sp_ref.at[rec, :, at], spv.at[:, at]))
        up.append(move(wu.at[:, at], wuv.at[:, at]))
    later = [move(x_ref.at[rec], xv), move(dx1_ref.at[rec], dx1v)]
    sent = []

    def keep(at, dz):
        dzv[:, at] = dz
        sent.append(move(dzv.at[:, at], dz_ref.at[rec, :, at]))

    def slope(f, at):
        slopes[f].wait()
        return spv[:, at]

    dh = feed_back(dy_ref[0], wuv, wdv, lambda f: up[f].wait(), lambda f: down[f].wait(), slope, keep)
    settle(later)
    n, inverse = norm_parts(xv[...].astype(F32))
    add_rows(small_ref, 0, dh * n)
    add_rows(small_ref, 1, dh)
    out_ref[0] = (dx1v[...] + norm_pull(n, inverse, row(lines, "early_gain"), dh)).astype(BF)
    settle(sent)


def share_kernel(core_ref, *refs, kinds, extra, apart):
    jobs = len(kinds)
    ins = refs[: 2 * jobs]
    more = refs[2 * jobs : 2 * jobs + extra]
    outs = refs[2 * jobs + extra : 2 * jobs + extra + 1 + apart]
    held = refs[2 * jobs + extra + 1 + apart :]
    packed, small, sems = held[2 * jobs :]
    move = mover(sems)
    plan = []
    for k, kind in enumerate(kinds):
        left, right = ins[2 * k : 2 * k + 2]
        left_held, right_held = held[2 * k : 2 * k + 2]
        if kind == "columns":
            first = move(left, left_held)
            parts = [move(right.at[:, at], right_held.at[:, at]) for at in pieces(right.shape[1])]
        else:
            first = move(right, right_held)
            parts = [move(left.at[:, at], left_held.at[:, at]) for at in pieces(left.shape[1])]
        plan.append((left_held, right_held, first, parts))
    sent = []

    def send(who, there):
        if apart:
            for k, out in enumerate(outs):
                core = core_ref[0] if k == 0 else 1 - core_ref[0]
                sent.append(move(packed.at[who, core, there], out.at[who, there]))
        else:
            sent.append(move(packed.at[who, :, there], outs[0].at[who, :, there]))

    place = 0
    for kind, (left, right, first, parts) in zip(kinds, plan):
        first.wait()
        share = share_columns if kind == "columns" else share_rows
        place = share(send, packed, place, left, right, lambda f: parts[f].wait())
    if extra:
        small_shares(more, packed, small, place)
        send(slice(0, packed.shape[0]), slice(place, packed.shape[2]))
    settle(sent)


def small_shares(refs, packed, small, place):
    small_mid, ddep, table = refs[:3]
    batches = (len(refs) - 3) // 3
    count = packed.shape[0] * packed.shape[1]
    small[...] = jnp.zeros_like(small)
    for k in range(3):
        for ref in refs[3 + k * batches : 3 + k * batches + batches]:
            small[2 * k : 2 * k + 2, :] += ref[0:2, :]
    small[6:10, :] = small_mid[6:10, :]
    narrow = 512 // count
    broad = ddep.shape[1] // count
    high = table.shape[0] // count
    packed[:, :, place:, :] = jnp.zeros(packed.shape[:2] + (packed.shape[2] - place, 512), BF)
    blocks = ddep.shape[1] // 512
    inner = [
        jnp.concatenate([small_mid[first + c : first + c + 1, :] for c in range(blocks)], axis=1)
        for first in (2, 4)
    ]
    inner = jnp.concatenate(inner, axis=0)
    for s in range(count):
        packed[s // 2, s % 2, place : place + 16, 0:narrow] = small[
            :, narrow * s : narrow * s + narrow
        ].astype(BF)
        packed[s // 2, s % 2, place + 16 : place + 18, 0:broad] = inner[
            :, broad * s : broad * s + broad
        ].astype(BF)
        packed[s // 2, s % 2, place + 32 : place + 48, 0:broad] = ddep[
            :, broad * s : broad * s + broad
        ].astype(BF)
        packed[s // 2, s % 2, place + 48 : place + 48 + high, 0 : table.shape[1]] = table[
            high * s : high * s + high, :
        ].astype(BF)


def finish_kernel(index_ref, *refs, parts):
    outs = refs[3 * parts : len(refs) - 3]
    sums, proj, last = refs[len(refs) - 3 :]
    for group, held in enumerate((sums, proj, last)):
        for k in range(parts):
            held[index_ref[0] ^ k] = refs[group * parts + k][...]
    (
        e_gain, e_shift, e_up, e_down, a_gain, a_shift, a_in, a_out, table, c_gain, c_shift, c_in, depth,
        i_gain, i_shift, c_out, l_gain, l_shift, l_up, l_down, f_gain, f_shift,
    ) = outs

    def reader(ref):
        def read(first, size):
            if len(ref.shape) == 2:
                return ref[first : first + size, :].astype(F32)
            height = ref.shape[1]
            pieces = []
            while size:
                piece, top = divmod(first, height)
                here = min(size, height - top)
                pieces.append(ref[piece].astype(F32)[top : top + here, :])
                first += here
                size -= here
            return pieces[0] if len(pieces) == 1 else jnp.concatenate(pieces, axis=0)

        return read

    def put(read, place, out):
        height = out.shape[0]
        for f in range(out.shape[1] // 512):
            out[:, 512 * f : 512 * f + 512] = read(place, height)
            place += height
        return place

    sums, proj, last = reader(sums), reader(proj), reader(last)
    put(sums, put(sums, put(sums, put(sums, put(sums, 0, l_up), l_down), c_out), c_in), a_out)
    put(proj, put(proj, 0, a_in), e_down)
    place = put(last, 0, e_up)
    small = last(place, 64)
    for line, out in enumerate(
        (e_gain, e_shift, a_gain, a_shift, c_gain, c_shift, l_gain, l_shift, f_gain, f_shift)
    ):
        out[...] = small[line : line + 1, 0 : out.shape[1]]
    i_gain[...] = small[16:17, 0 : i_gain.shape[1]]
    i_shift[...] = small[17:18, 0 : i_shift.shape[1]]
    depth[...] = small[32 : 32 + depth.shape[0], 0 : depth.shape[1]]
    table[...] = small[48 : 48 + table.shape[0], 0 : table.shape[1]]


def per_rec(array, first=0):
    shape = (1,) + array.shape[1:]
    tail = (0,) * (array.ndim - 1)
    return pl.BlockSpec(shape, lambda r, *_: (r + first,) + tail)


def whole(array):
    zeros = (0,) * array.ndim
    return pl.BlockSpec(array.shape, lambda r, *_: zeros, pipeline_mode=pl.Buffered(1))


def whole_out(array):
    zeros = (0,) * len(array.shape)
    return pl.BlockSpec(array.shape, lambda r, *_: zeros)


def per_unit(array, recs):
    units, rest = array.shape[0], array.shape[2:]
    if len(array.shape) == 6:
        return pl.BlockSpec(
            (units, 1, rest[0], 1) + rest[2:], lambda r, *_: (0, r // recs, 0, r % recs, 0, 0)
        )
    return pl.BlockSpec((units, 1, 1) + rest[1:], lambda r, *_: (0, r // recs, r % recs, 0, 0))


def far(array):
    return pl.BlockSpec(memory_space=pl.ANY)


def spot(shape, kind=F32):
    return jax.ShapeDtypeStruct(shape, kind)


def run(
    kernel, seqs, ins, in_specs, outs, out_specs, scratch=(), prefetch=(), after=(), into=(),
    micros=6,
):
    held = (*after, *into)
    plain = kernel
    place = len(prefetch) + len(ins)

    def kernel(*refs):
        plain(*refs[:place], *refs[place + len(held) :])

    return pl.pallas_call(
        kernel,
        grid_spec=pltpu.PrefetchScalarGridSpec(
            num_scalar_prefetch=len(prefetch),
            grid=(seqs,),
            in_specs=[*in_specs, *(pl.BlockSpec(memory_space=pl.ANY) for _ in held)],
            out_specs=out_specs,
            scratch_shapes=list(scratch),
        ),
        out_shape=outs,
        cost_estimate=cost(micros),
        input_output_aliases={place + len(after) + k: k for k in range(len(into))},
        compiler_params=pltpu.CompilerParams(vmem_limit_bytes=58 * MEGA),
    )(*prefetch, *ins, *held)


def unit_plan(seqs, heads):
    parts = lax.axis_size("tm")
    if parts <= heads:
        return heads // parts, seqs, 1
    return 1, seqs * heads // parts, parts // heads


def distance_hot(seq_total, bucket_count):
    limits = jnp.array(boundaries(seq_total), jnp.int32)
    places = jnp.arange(seq_total, dtype=jnp.int32)
    bucket = jnp.sum((places[:, None] >= limits[None, :]).astype(jnp.int32), axis=1)
    return (bucket[:, None] == jnp.arange(bucket_count, dtype=jnp.int32)[None, :]).astype(FLOAT)


def bias_strip(table, hot, nh, split):
    first = lax.axis_index("tm") // split * nh
    mine = lax.dynamic_slice_in_dim(table, first, nh, 1)
    per = jnp.dot(hot, mine, precision=HIGHEST).T
    pad = 2 * KEYS
    shifted = [
        jnp.pad(per, ((0, 0), (pad + s, 0)), constant_values=NEGATIVE)[:, : pad + hot.shape[0]]
        for s in range(8)
    ]
    return make_strip(jnp.stack(shifted, 1))


def table_grad(diagonals, hot, nh, split, heads):
    per = sum(jnp.pad(diagonals[:, s, KEYS + s :], ((0, 0), (0, s))) for s in range(8))
    mine = jnp.dot(hot.T, per.T, precision=HIGHEST)
    first = lax.axis_index("tm") // split * nh
    return lax.dynamic_update_slice_in_dim(
        jnp.zeros((hot.shape[1], heads), FLOAT), mine, first, 1
    )


def swap(values):
    return lax.all_to_all(values, "tm", 0, 0, tiled=True)


def body(
    frames, cotangent, lengths,
    early_gain, early_shift, early_up, early_down,
    attend_gain, attend_shift, attend_input, attend_output, distance_bias,
    convolve_gain, convolve_shift, convolve_input, depthwise, inner_gain, inner_shift, convolve_output,
    late_gain, late_shift, late_up, late_down, final_gain, final_shift,
):
    seqs, rows, width = frames.shape
    heads = distance_bias.shape[1]
    count = lax.axis_size("rows")
    parts = lax.axis_size("tm")
    hidden = early_up.shape[1]
    channels = convolve_output.shape[0]
    nh, recs, split = unit_plan(seqs, heads)
    units = heads // nh
    batches = seqs if split == 1 else 1
    here = seqs // batches
    recs = recs // batches
    tokens = seqs * rows
    vectors = (
        early_gain, early_shift, attend_gain, attend_shift, convolve_gain, convolve_shift,
        late_gain, late_shift, final_gain, final_shift, inner_gain, inner_shift,
    )
    lines = pl.pallas_call(lines_kernel, out_shape=spot((16, 512)))(*vectors)
    core = (lax.axis_index("rows") % 2).astype(jnp.int32)[None]
    merge = lambda v: v.reshape(tokens, -1)

    def wide(*kinds):
        return spot((units, split, *kinds, recs, rows, 128), BF)

    def held(columns, kind=BF):
        return pltpu.VMEM((rows, columns), kind)

    def like(array):
        return pltpu.VMEM(array.shape, array.dtype)

    def sems(size):
        return pltpu.SemaphoreType.DMA((size,))

    def shares(kinds, ins, height, extra=(), after=(), apart=True):
        shape = (count // 2, 2, height // 512 // count, 512)
        outs = (spot((shape[0],) + shape[2:], BF),) * 2 if apart else (spot(shape, BF),)
        return run(
            functools.partial(share_kernel, kinds=kinds, extra=len(extra), apart=apart), 1, (*ins, *extra),
            [far(v) for v in ins] + [whole(v) for v in extra], outs, [far(v) for v in outs],
            scratch=[like(v) for v in ins] + [pltpu.VMEM(shape, BF), pltpu.VMEM((16, 512), F32), sems(40)],
            after=after, prefetch=(core,),
        )

    def own(columns, kind=BF):
        return spot((seqs, rows, columns), kind)

    kept = ()
    sent = []
    for batch in range(batches):
        ins = (frames, lines, early_up, early_down, attend_input)
        outs = (own(width, F32), own(width), own(hidden), own(hidden), own(width), wide(3))
        *kept, qkv = run(
            functools.partial(open_kernel, nh=nh, first=batch * here, recs=recs), here, ins,
            [per_rec(frames, batch * here), whole(lines)] + [far(v) for v in ins[2:]],
            outs, [far(v) for v in outs],
            scratch=(
                like(early_up), like(early_down), like(attend_input), held(width, F32), held(width), held(hidden),
                held(hidden), held(width), pltpu.VMEM((units, 3, rows, 128), BF), sems(32),
            ),
            into=kept,
        )
        sent.append(swap(qkv.reshape(parts, 3, recs, rows, 128)))
    x1, h1, a1, sp1, h2 = kept
    hot = distance_hot(rows * parts, distance_bias.shape[0])
    strip = bias_strip(distance_bias.astype(FLOAT), hot, nh, split)
    mine = [
        lax.dynamic_slice_in_dim(lengths, batch * here + lax.axis_index("tm") % split * recs, recs, 0)
        for batch in range(batches)
    ]
    attended = [attn_fwd(mine[batch], sent[batch], strip, nh) for batch in range(batches)]

    limits = lengths - lax.axis_index("tm").astype(jnp.int32) * rows
    kept = ()
    for batch in range(batches):
        back = swap(attended[batch][0]).reshape(units, split, recs, rows, 128)
        ins = (back, x1, lines, attend_output, convolve_input)
        outs = (own(width), own(width, F32), own(width), own(channels), own(channels), own(channels))
        kept = run(
            functools.partial(gate_kernel, nh=nh, first=batch * here), here, ins,
            [per_unit(back, recs), per_rec(x1, batch * here), whole(lines)] + [far(v) for v in ins[3:]],
            outs, [far(v) for v in outs], prefetch=(limits,), into=kept,
            scratch=(
                like(attend_output), like(convolve_input), held(width), held(width, F32), held(width),
                held(channels), held(channels), held(channels), sems(32),
            ),
        )
    att, x2, h3, g, ga, gb = kept
    halo = passed_along(g[:, rows - 16 :, :], "tm", 1)

    dep = jnp.pad(depthwise.astype(FLOAT).T, ((0, 1), (0, 0)))
    ins = (g, halo, x2, cotangent, dep, lines, convolve_output, late_up, late_down)
    height = (width * hidden * 2 + channels * width) // 512 // count
    outs = (
        own(width), own(width, F32), own(channels), spot((seqs, 16, channels), BF),
        spot((16, 512)), spot((16, channels)), spot((count // 2, 2, height, 512), BF),
    )
    layer_out, dx3, dg, dhalo, small_mid, ddep, pack_mid = run(
        middle_kernel, seqs, ins,
        [per_rec(v) for v in ins[:4]] + [whole(v) for v in ins[4:6]] + [far(v) for v in ins[6:]],
        outs, [per_rec(v) for v in outs[:4]] + [whole_out(v) for v in outs[4:6]] + [far(outs[6])],
        scratch=(
            pltpu.VMEM((channels // 128, rows + 16, 128), F32), pltpu.VMEM((rows, channels), F32),
            pltpu.VMEM((rows, 1), F32), pltpu.VMEM((rows + 32, 128), F32), pltpu.VMEM((rows, channels), BF),
            pltpu.VMEM((tokens, width), BF), pltpu.VMEM((tokens, hidden), BF), pltpu.VMEM((rows, hidden), BF),
            pltpu.VMEM((tokens, hidden), BF), pltpu.VMEM((tokens, width), BF),
            pltpu.VMEM((tokens, channels), BF), pltpu.VMEM((tokens, width), BF),
            pltpu.VMEM((channels // 128, 128, 128), F32), pltpu.VMEM((rows, channels), F32),
            like(convolve_output), like(late_up), like(late_down), like(outs[6]), sems(16), sems(16),
        ),
        micros=42,
    )
    returned = passed_along(dhalo, "tm", -1)
    sums_mid = offloaded(pack_mid)

    kept = ()
    sent_back = []
    small_gate = []
    for batch in range(batches):
        ins = (dg, returned, ga, gb, dx3, x2, lines, convolve_input, attend_output)
        outs = (own(width, F32), own(2 * channels), own(width), wide(), spot((8, 512)))
        *kept, do, small = run(
            functools.partial(ungate_kernel, nh=nh, first=batch * here, recs=recs), here, ins,
            [per_rec(v, batch * here) for v in ins[:2]] + [far(v) for v in ins[2:6]] + [whole(lines)]
            + [far(v) for v in ins[7:]],
            outs, [far(v) for v in outs[:4]] + [whole_out(outs[4])],
            scratch=(
                like(convolve_input), like(attend_output), held(channels), held(channels), held(width, F32),
                held(width, F32), held(width, F32), held(2 * channels), held(width),
                pltpu.VMEM((units, rows, 128), BF), held(channels, F32), sems(32),
            ),
            into=kept,
        )
        small_gate.append(small)
        sent_back.append(swap(do.reshape(parts, recs, rows, 128)))
    dx2, du, dy2 = kept
    pack_gate = shares(
        ("columns", "columns"), (merge(h3), merge(du), merge(att), merge(dy2)), 2 * channels * width + width * width,
        apart=False,
    )
    own_grads = []
    diagonals = 0.0
    for batch in range(batches):
        out, lse = attended[batch]
        grad, diagonal = attn_bwd(mine[batch], sent[batch], sent_back[batch], out, lse, strip, nh)
        diagonals = diagonals + diagonal
        own_grads.append(swap(grad).reshape(units, split, 3, recs, rows, 128))
    sums_gate = offloaded(pack_gate[0])
    grad_table = table_grad(diagonals, hot, nh, split, heads)

    kept = ()
    kept_two = ()
    small_proj = []
    small_first = []
    for batch in range(batches):
        ins = (own_grads[batch], x1, dx2, lines, attend_input)
        outs = (own(width, F32), own(width), own(3 * width), spot((8, 512)))
        if batch == batches - 1:
            part_rest = time_sum(jnp.concatenate([sums_mid, sums_gate], axis=0))
        *kept, small = run(
            functools.partial(project_kernel, nh=nh, first=batch * here, recs=recs), here, ins,
            [far(v) for v in ins[:3]] + [whole(lines), far(attend_input)],
            outs, [far(v) for v in outs[:3]] + [whole_out(outs[3])],
            scratch=(
                like(attend_input), pltpu.VMEM((units, 3, rows, 128), BF), held(width, F32), held(width, F32),
                held(width, F32), held(width), held(3 * width), sems(32),
            ),
            into=kept, after=(sums_mid,) if batch == batches - 1 else (),
        )
        small_proj.append(small)
        dx1, dy1, dp = kept
        if batch == batches - 1:
            pack_proj = shares(
                ("columns", "rows"), (merge(h2), merge(dp), merge(a1), merge(dy1)), width * hidden + width * 3 * width,
                apart=False,
            )
            sums_proj = offloaded(pack_proj[0])
            before = ()
        else:
            before = ()
        ins = (dy1, dx1, frames, sp1, lines, early_up, early_down)
        dx0_spot = own(width)
        outs = (dx0_spot, own(hidden), spot((8, 512)))
        *kept_two, small = run(
            functools.partial(close_kernel, first=batch * here), here, ins,
            [per_rec(dy1, batch * here)] + [far(v) for v in ins[1:4]] + [whole(lines)] + [far(v) for v in ins[5:]],
            outs, [per_rec(dx0_spot, batch * here), far(outs[1]), whole_out(outs[2])],
            scratch=(
                like(early_up), like(early_down), held(hidden), held(width, F32), held(width), held(hidden), sems(32),
            ),
            into=kept_two, after=before,
        )
        small_first.append(small)
    dx0, dz1 = kept_two
    pack_last = shares(
        ("columns",), (merge(h1), merge(dz1)), width * hidden + 64 * 512 * count,
        extra=(small_mid, ddep, grad_table, *small_first, *small_proj, *small_gate), after=(part_rest,),
    )
    part_last = along_chips(along_time(between_cores(*pack_last)))
    part_proj = time_sum_by_steps(sums_proj)
    totals = (part_rest, *others(part_rest), part_proj, *others(part_proj), part_last, *others(part_last))
    return (layer_out, dx0) + finish(
        totals, count, parts, width, hidden, channels, depthwise.shape[1], distance_bias.shape
    )


def offloaded(packed):
    sent = packed.reshape(-1, packed.shape[3])
    return lax.psum_scatter(sent, "rows", scatter_dimension=0, tiled=True)


def with_others(mine):
    parts = lax.axis_size("tm")
    return lax.all_to_all(jnp.broadcast_to(mine, (parts,) + mine.shape), "tm", 0, 0, tiled=True)


def total(blocks):
    return jnp.sum(blocks.astype(FLOAT), axis=0).astype(BF)


def between_cores(keep, send):
    devices = range(lax.axis_size("rows"))
    got = lax.ppermute(send, "rows", [(i, i ^ 1) for i in devices])
    return (keep.astype(FLOAT) + got.astype(FLOAT)).astype(BF)


def time_sum(share):
    parts = lax.axis_size("tm")
    blocks = share.reshape((parts, share.shape[0] // parts) + share.shape[1:])
    return total(lax.all_to_all(blocks, "tm", 0, 0, tiled=True))


def time_sum_by_steps(share):
    parts = lax.axis_size("tm")
    me = lax.axis_index("tm")
    blocks = share.reshape((parts, share.shape[0] // parts) + share.shape[1:])
    pick = lambda k: lax.dynamic_index_in_dim(blocks, me ^ k, 0, keepdims=False)
    sums = pick(0).astype(FLOAT)
    for k in range(1, parts):
        got = lax.ppermute(pick(k), "tm", [(i, i ^ k) for i in range(parts)])
        sums = sums + got.astype(FLOAT)
    return sums.astype(BF)


def others(mine):
    parts = lax.axis_size("tm")
    return [lax.ppermute(mine, "tm", [(i, i ^ k) for i in range(parts)]) for k in range(1, parts)]


def along_time(half):
    chips, height, width = half.shape
    parts = lax.axis_size("tm")
    blocks = jnp.transpose(half.reshape(chips, parts, height // parts, width), (1, 0, 2, 3))
    return total(lax.all_to_all(blocks, "tm", 0, 0, tiled=True))


def along_chips(part):
    devices = range(lax.axis_size("rows"))
    groups = [[i for i in devices if i % 2 == core] for core in range(2)]
    return total(lax.all_to_all(part, "rows", 0, 0, axis_index_groups=groups, tiled=True))


def finish(totals, count, parts, width, hidden, channels, taps, table_shape):
    share = width // count
    line = (1, share)
    broad = (1, channels // count)
    shapes = (
        line, line, (share, hidden), (hidden // count, width), line, line, (share, 3 * width), (share, width),
        (table_shape[0] // count, table_shape[1]), line, line, (share, 2 * channels), (taps, channels // count),
        broad, broad, (channels // count, width), line, line, (share, hidden), (hidden // count, width), line, line,
    )
    outs = tuple(spot(shape) for shape in shapes)
    me = lax.axis_index("tm").astype(jnp.int32)[None]
    got = list(
        run(
            functools.partial(finish_kernel, parts=parts), 1, totals, [whole(v) for v in totals],
            outs, [whole_out(v) for v in outs], prefetch=(me,), micros=3,
            scratch=[pltpu.VMEM((parts,) + v.shape, BF) for v in totals[::parts]],
        )
    )
    got[12] = got[12].T
    for place, shape in enumerate(shapes):
        if shape[0] == 1:
            got[place] = got[place].reshape(-1)
    return tuple(got)


def solution(mesh):
    placed = (
        P("rows", "tm", None),
        P("rows", "tm", None),
        P("rows"),
        P(),
        P(),
        P(),
        P(),
        P(),
        P(),
        P(),
        P(),
        P(),
        P(),
        P(),
        P(),
        P(),
        P(),
        P(),
        P(),
        P(),
        P(),
        P(),
        P(),
        P(),
        P(),
    )
    return jax.shard_map(
        body,
        mesh=mesh,
        in_specs=placed,
        out_specs=(
            P("rows", "tm", None),
            P("rows", "tm", None),
            P("rows"),
            P("rows"),
            P("rows", None),
            P("rows", None),
            P("rows"),
            P("rows"),
            P("rows", None),
            P("rows", None),
            P("rows", None),
            P("rows"),
            P("rows"),
            P("rows", None),
            P("rows", None),
            P("rows"),
            P("rows"),
            P("rows", None),
            P("rows"),
            P("rows"),
            P("rows", None),
            P("rows", None),
            P("rows"),
            P("rows"),
        ),
        check_vma=False,
    )
```

```python
import functools

import jax
import jax.numpy as jnp
from jax import lax
from jax.experimental import pallas as pl
from jax.experimental.pallas import tpu as pltpu
from jax.sharding import PartitionSpec as P

EPSILON = 1e-05
NEGATIVE = -1e30
HIGHEST = lax.Precision.HIGHEST
BFLOAT = jnp.bfloat16
FLOAT = jnp.float32
NEG = NEGATIVE
F32 = FLOAT
BF = BFLOAT


MEGA = 2**20
SCALE = 1


def cost(micros):
    micros = micros * SCALE
    return pl.CostEstimate(
        flops=int(micros * 1.1e9), bytes_accessed=int(micros * 3.6e6), transcendentals=0
    )


def passed_along(block, axis, distance):
    devices = range(lax.axis_size(axis))
    route = [(i - distance, i) for i in devices if i - distance in devices]
    return lax.ppermute(block, axis, route)


def boundaries(seq_total):
    edges_list = list(range(1, 16))
    for exponent in range(16):
        edges_list.append(int(16.0 * (seq_total / 16.0) ** (exponent / 16.0)))
    return edges_list


KEYS = 256
QUERIES = 512


def nt(a, b):
    return lax.dot_general(a, b, (((1,), (1,)), ((), ())), preferred_element_type=F32)


def nn(a, b):
    return lax.dot_general(a, b, (((1,), (0,)), ((), ())), preferred_element_type=F32)


def strip_kernel(base_ref, out_ref):
    heads, keys, _ = out_ref.shape
    for h in range(heads):
        base = base_ref[h]
        for g in range(keys // 8):
            out_ref[h, 8 * g : 8 * g + 8, :] = pltpu.roll(base, 8 * g, 1)[:, keys:] if g else base[:, keys:]


def make_strip(base):
    heads, _, wide = base.shape
    return pl.pallas_call(
        strip_kernel,
        out_shape=jax.ShapeDtypeStruct((heads, KEYS, wide - KEYS), F32),
        compiler_params=pltpu.CompilerParams(vmem_limit_bytes=58 * MEGA),
        cost_estimate=cost(3),
    )(base)


def head_lanes(shape, h):
    lane = lax.broadcasted_iota(jnp.int32, shape, 1)
    return (lane >= 64 * h) & (lane < 64 * h + 64), lane == ((64 * h + 64) % 128)


def masked_queries(q, h):
    mine, spare = head_lanes(q.shape, h)
    return jnp.where(mine, q, jnp.where(spare, 1.0, 0.0)).astype(BF)


def masked_keys(k, h, first, length):
    mine, spare = head_lanes(k.shape, h)
    beyond = first + lax.broadcasted_iota(jnp.int32, k.shape, 0) >= length
    return jnp.where(mine, k, jnp.where(spare & beyond, NEG, 0.0)).astype(BF)


def block_of(index, size):
    return pl.ds(pl.multiple_of(index * size, 128), size)


def loop(first, last, step):
    def turn(index, carried):
        step(index)
        return carried

    lax.fori_loop(first, last, turn, 0)


def attend_kernel(len_ref, x_ref, bias_ref, o_ref, lse_ref, kh, vt, qh, acc, ot, strip_ref, sem, *, nh):
    parts, rows = x_ref.shape[0], x_ref.shape[3]
    total = parts * rows
    length = len_ref[pl.program_id(0)]
    bias = pltpu.make_async_copy(bias_ref, strip_ref, sem.at[0])
    bias.start()

    def prepare(t):
        at = block_of(t, rows)
        q = x_ref[t, 0, 0].astype(F32) * 0.125
        k = x_ref[t, 1, 0].astype(F32)
        v = x_ref[t, 2, 0].astype(F32).T.astype(BF)
        for h in range(nh):
            qh[h, at, :] = masked_queries(q, h)
            kh[h, at, :] = masked_keys(k, h, t * rows, length)
            vt[h, 0:64, at] = v[64 * h : 64 * h + 64]
            ones = lax.broadcasted_iota(jnp.int32, (16, rows), 0) == 0
            vt[h, 64:80, at] = jnp.where(ones, 1.0, 0.0).astype(BF)

    loop(0, parts, prepare)
    bias.wait()

    def queries(qb):
        at = block_of(qb, QUERIES)
        for h in range(nh):
            acc[h] = jnp.zeros((80, QUERIES), F32)

        def keys(kb, peaks):
            there = block_of(kb, QUERIES)
            after = []
            for h in range(nh):
                scores = []
                for half in range(QUERIES // KEYS):
                    first = kb * QUERIES + half * KEYS
                    off = pl.ds(pl.multiple_of(KEYS + qb * QUERIES - first, 128), QUERIES)
                    k = kh[h, pl.ds(pl.multiple_of(first, 128), KEYS), :]
                    scores.append(nt(k, qh[h, at, :]) + strip_ref[h, :, off])
                peak = peaks[h]
                for s in scores:
                    peak = jnp.maximum(peak, jnp.max(s, axis=0, keepdims=True))
                p = jnp.concatenate([jnp.exp(s - peak).astype(BF) for s in scores], axis=0)
                acc[h] = acc[h] * jnp.exp(peaks[h] - peak) + nn(vt[h, :, there], p)
                after.append(peak)
            return tuple(after)

        last = jnp.minimum(qb + 1, (length + QUERIES - 1) // QUERIES)
        peaks = lax.fori_loop(
            0, last, keys, tuple(jnp.full((1, QUERIES), NEG, F32) for _ in range(nh))
        )
        for h in range(nh):
            sums = acc[h, 64:65, :]
            lse_ref[0, h, :, at] = peaks[h] + jnp.log(sums)
            ot[64 * h : 64 * h + 64, at] = acc[h, 0:64, :] / sums
        if nh == 1:
            ot[64:128, at] = jnp.zeros((64, QUERIES), F32)

    loop(0, total // QUERIES, queries)

    def give(t):
        o_ref[t, 0] = ot[:, block_of(t, rows)].T.astype(BF)

    loop(0, parts, give)


def attn_fwd(lengths, x, strip, nh):
    parts, _, recs, rows, wide = x.shape
    total = parts * rows
    return pl.pallas_call(
        functools.partial(attend_kernel, nh=nh),
        grid_spec=pltpu.PrefetchScalarGridSpec(
            num_scalar_prefetch=1,
            grid=(recs,),
            in_specs=[
                pl.BlockSpec((parts, 3, 1, rows, wide), lambda r, l: (0, 0, r, 0, 0)), pl.BlockSpec(memory_space=pl.ANY),
            ],
            out_specs=[
                pl.BlockSpec((parts, 1, rows, wide), lambda r, l: (0, r, 0, 0)),
                pl.BlockSpec((1, nh, 1, total), lambda r, l: (r, 0, 0, 0)),
            ],
            scratch_shapes=[
                pltpu.VMEM((nh, total, wide), BF), pltpu.VMEM((nh, 80, total), BF),
                pltpu.VMEM((nh, total, wide), BF), pltpu.VMEM((nh, 80, QUERIES), F32),
                pltpu.VMEM((wide, total), F32), pltpu.VMEM(strip.shape, F32), pltpu.SemaphoreType.DMA((1,)),
            ],
        ),
        out_shape=[
            jax.ShapeDtypeStruct((parts, recs, rows, wide), BF),
            jax.ShapeDtypeStruct((recs, nh, 1, total), F32),
        ],
        compiler_params=pltpu.CompilerParams(vmem_limit_bytes=58 * MEGA),
        cost_estimate=cost(11),
    )(lengths, x, strip)


def attend_back_kernel(
    len_ref, x_ref, do_ref, o_ref, lse_ref, bias_ref, dx_ref, db_ref,
    kh, vh, qh, qs, dos, kt, dqt, delta, dk, dv, dks, dvs, dbs, strip_ref, sem, *, nh,
):
    parts, rows = x_ref.shape[0], x_ref.shape[3]
    total = parts * rows
    length = len_ref[pl.program_id(0)]
    blocks = (length + KEYS - 1) // KEYS
    bias = pltpu.make_async_copy(bias_ref, strip_ref, sem.at[0])
    bias.start()

    @pl.when(pl.program_id(0) == 0)
    def _():
        dbs[...] = jnp.zeros_like(dbs)

    dqt[...] = jnp.zeros_like(dqt)

    def prepare(t):
        at = block_of(t, rows)
        q = x_ref[t, 0, 0].astype(F32) * 0.125
        k = x_ref[t, 1, 0].astype(F32)
        v = x_ref[t, 2, 0].astype(F32)
        do = do_ref[t, 0]
        qs[at, :] = q.astype(BF)
        dos[at, :] = do
        kt[:, at] = k.T.astype(BF)
        product = (do.astype(F32) * o_ref[t, 0].astype(F32)).T
        for h in range(nh):
            qh[h, at, :] = masked_queries(q, h)
            kh[h, at, :] = masked_keys(k, h, t * rows, length)
            vh[h, at, :] = jnp.where(head_lanes(v.shape, h)[0], v, 0.0).astype(BF)
            delta[h, :, at] = jnp.sum(product[64 * h : 64 * h + 64], axis=0, keepdims=True)

    loop(0, parts, prepare)
    bias.wait()

    def keys(kb):
        there = block_of(kb, KEYS)
        dk[...] = jnp.zeros_like(dk)
        dv[...] = jnp.zeros_like(dv)

        def queries(qb):
            at = block_of(qb, QUERIES)
            off = pl.ds(pl.multiple_of(KEYS + qb * QUERIES - kb * KEYS, 128), QUERIES)
            for h in range(nh):
                s = nt(kh[h, there, :], qh[h, at, :]) + strip_ref[h, :, off]
                p = jnp.exp(s - lse_ref[0, h, :, at])
                ds = p * (nt(vh[h, there, :], dos[at, :]) - delta[h, :, at])
                low = ds.astype(BF)
                dv[h] += nn(p.astype(BF), dos[at, :])
                dk[h] += nn(low, qs[at, :])
                dqt[64 * h : 64 * h + 64, at] += nn(kt[64 * h : 64 * h + 64, there], low)
                dbs[h, :, off] += ds

        loop(kb * KEYS // QUERIES, total // QUERIES, queries)
        first, _ = head_lanes((KEYS, 128), 0)
        dks[there, :] = (jnp.where(first, dk[0], dk[1]) if nh == 2 else dk[0]).astype(BF)
        dvs[there, :] = (jnp.where(first, dv[0], dv[1]) if nh == 2 else dv[0]).astype(BF)

    loop(0, blocks, keys)

    def nothing(kb):
        dks[block_of(kb, KEYS), :] = jnp.zeros((KEYS, 128), BF)
        dvs[block_of(kb, KEYS), :] = jnp.zeros((KEYS, 128), BF)

    loop(blocks, total // KEYS, nothing)

    def give(t):
        at = block_of(t, rows)
        dx_ref[t, 0, 0] = (dqt[:, at] * 0.125).T.astype(BF)
        dx_ref[t, 1, 0] = dks[at, :]
        dx_ref[t, 2, 0] = dvs[at, :]

    loop(0, parts, give)

    @pl.when(pl.program_id(0) == pl.num_programs(0) - 1)
    def _():
        wide = dbs.shape[2]
        for h in range(nh):
            sums = dbs[h, 0:8, :]
            for g in range(1, KEYS // 8):
                sums = sums + pltpu.roll(dbs[h, 8 * g : 8 * g + 8, :], wide - 8 * g, 1)
            db_ref[h] = sums


def attn_bwd(lengths, x, do, o, lse, strip, nh):
    parts, _, recs, rows, wide = x.shape
    total = parts * rows
    several = pltpu.VMEM((nh, total, wide), BF)
    single = pltpu.VMEM((total, wide), BF)
    part = pltpu.VMEM((nh, KEYS, wide), F32)
    return pl.pallas_call(
        functools.partial(attend_back_kernel, nh=nh),
        grid_spec=pltpu.PrefetchScalarGridSpec(
            num_scalar_prefetch=1,
            grid=(recs,),
            in_specs=[
                pl.BlockSpec((parts, 3, 1, rows, wide), lambda r, l: (0, 0, r, 0, 0)),
                pl.BlockSpec((parts, 1, rows, wide), lambda r, l: (0, r, 0, 0)),
                pl.BlockSpec((parts, 1, rows, wide), lambda r, l: (0, r, 0, 0)),
                pl.BlockSpec((1, nh, 1, total), lambda r, l: (r, 0, 0, 0)),
                pl.BlockSpec(memory_space=pl.ANY),
            ],
            out_specs=[
                pl.BlockSpec((parts, 3, 1, rows, wide), lambda r, l: (0, 0, r, 0, 0)),
                pl.BlockSpec((nh, 8, strip.shape[2]), lambda r, l: (0, 0, 0)),
            ],
            scratch_shapes=[
                several, several, several, single, single, pltpu.VMEM((wide, total), BF),
                pltpu.VMEM((wide, total), F32), pltpu.VMEM((nh, 1, total), F32), part, part, single, single,
                pltpu.VMEM(strip.shape, F32), pltpu.VMEM(strip.shape, F32), pltpu.SemaphoreType.DMA((1,)),
            ],
        ),
        out_shape=[
            jax.ShapeDtypeStruct((parts, 3, recs, rows, wide), BF),
            jax.ShapeDtypeStruct((nh, 8, strip.shape[2]), F32),
        ],
        compiler_params=pltpu.CompilerParams(vmem_limit_bytes=58 * MEGA),
        cost_estimate=cost(15),
    )(lengths, x, do, o, lse, strip)


def tn(a, b):
    return lax.dot_general(a, b, (((0,), (0,)), ((), ())), preferred_element_type=F32)


def sigmoid(v):
    return 0.5 * jnp.tanh(0.5 * v) + 0.5


LINES = {
    "early_gain": 0, "early_shift": 1, "attend_gain": 2, "attend_shift": 3, "convolve_gain": 4, "convolve_shift": 5,
    "late_gain": 6, "late_shift": 7, "final_gain": 8, "final_shift": 9, "inner_gain": 10,
}


def row(ref, name):
    place = LINES[name]
    return ref[place : place + 1, :]


def broad_row(ref, name, width):
    blocks = width // 512
    place = LINES["inner_gain"] + (blocks if name == "inner_shift" else 0)
    return jnp.concatenate([ref[place + c : place + c + 1, :] for c in range(blocks)], axis=1)


def part_of(index, size=512):
    return pl.ds(pl.multiple_of(index * size, 128), size)


def repeat(count, step):
    def turn(index, carried):
        step(index)
        return carried

    lax.fori_loop(0, count, turn, 0)


def mover(sems):
    spent = []

    def move(source, target):
        copy = pltpu.make_async_copy(source, target, sems.at[len(spent)])
        spent.append(copy)
        copy.start()
        return copy

    return move


def pieces(width):
    return [slice(first, first + 512) for first in range(0, width, 512)]


def settle(copies):
    for copy in copies:
        copy.wait()


class Lane:
    def __init__(self, sems, first, parts, make):
        self.sems, self.first, self.parts, self.make = sems, first, parts, make
        self.each = len(make(0))

    def copies(self, part):
        place = self.first + part * self.each
        return [
            pltpu.make_async_copy(source, target, self.sems.at[place + k])
            for k, (source, target) in enumerate(self.make(part))
        ]

    def start(self, part=0):
        for copy in self.copies(part):
            copy.start()

    def wait(self, part=0):
        for copy in self.copies(part):
            copy.wait()

    def start_all(self):
        for part in range(self.parts):
            self.start(part)

    def wait_all(self):
        repeat(self.parts, self.wait)


def lanes(sems):
    spent = [0]

    def lane(parts, make):
        made = Lane(sems, spent[0], parts, make)
        spent[0] += parts * made.each
        return made

    return lane


def one(*pairs):
    return 1, lambda part: list(pairs)


def feed(h, wu, wd, up, down, keep):
    y = None
    for f in range(wu.shape[1] // 512):
        at = slice(512 * f, 512 * f + 512)
        up(f)
        z = nn(h, wu[:, at])
        sig = sigmoid(z)
        a = (z * sig).astype(BF)
        keep(f, at, a, (sig * (1.0 + z * (1.0 - sig))).astype(BF))
        down(f)
        part = nn(a, wd[at, :])
        y = part if y is None else y + part
    return y


def feed_back(dy, wu, wd, up, down, slope, keep):
    dh = None
    for f in range(wu.shape[1] // 512):
        at = slice(512 * f, 512 * f + 512)
        down(f)
        dz = (nt(dy, wd[at, :]) * slope(f, at).astype(F32)).astype(BF)
        keep(f, at, dz)
        up(f)
        part = nt(dz, wu[:, at])
        dh = part if dh is None else dh + part
    return dh


def over_rows(rows, step):
    step(slice(0, rows))


def share_columns(held, place, left, right, ready, send):
    height = left.shape[1] // (held.shape[0] * held.shape[1])

    def step(f):
        ready(f)
        block = tn(left[...], right[:, part_of(f)]).astype(BF)
        there = pl.ds(pl.multiple_of(place + f * height, 16), height)
        held[:, :, there, :] = block.reshape(held.shape[:2] + (height, 512))
        send(f, pl.ds(0, held.shape[0]), there)

    repeat(right.shape[1] // 512, step)


def share_rows(held, place, left, right, ready, send):
    height = left.shape[1] // (held.shape[0] * held.shape[1])
    each = 512 // (held.shape[1] * height)

    def step(f):
        ready(f)
        block = tn(left[:, part_of(f)], right[...]).astype(BF)
        who, there = pl.ds(each * f, each), pl.ds(place, height)
        held[who, :, there, :] = block.reshape(each, held.shape[1], height, 512)
        send(f, who, there)

    repeat(left.shape[1] // 512, step)


def columns_of(held, place, left, right):
    height = left.shape[1] // (held.shape[0] * held.shape[1])
    return lambda f: (pl.ds(0, held.shape[0]), pl.ds(pl.multiple_of(place + f * height, 16), height))


def rows_of(held, place, left, right):
    height = left.shape[1] // (held.shape[0] * held.shape[1])
    each = 512 // (held.shape[1] * height)
    return lambda f: (pl.ds(each * f, each), pl.ds(place, height))


def spread_columns(send, held, place, left, right, ready):
    count = held.shape[0] * held.shape[1]
    height = left.shape[1] // count
    for f, at in enumerate(pieces(right.shape[1])):
        ready(f)
        there = slice(place, place + height)
        block = tn(left[...], right[:, at]).astype(BF)
        held[:, :, there, :] = block.reshape(held.shape[:2] + (height, 512))
        send(slice(0, held.shape[0]), there)
        place += height
    return place


def spread_rows(send, held, place, left, right, ready):
    height = left.shape[1] // (held.shape[0] * held.shape[1])
    each = 512 // (held.shape[1] * height)
    for f, at in enumerate(pieces(left.shape[1])):
        ready(f)
        who, there = slice(each * f, each * f + each), slice(place, place + height)
        block = tn(left[:, at], right[...]).astype(BF)
        held[who, :, there, :] = block.reshape(each, held.shape[1], height, 512)
        send(who, there)
    return place + height


def norm_parts(v):
    center = v - jnp.mean(v, axis=-1, keepdims=True)
    inverse = lax.rsqrt(jnp.mean(center * center, axis=-1, keepdims=True) + EPSILON)
    return center * inverse, inverse


def norm_pull(n, inverse, gain, grad):
    dn = grad * gain
    return (
        dn - jnp.mean(dn, axis=-1, keepdims=True) - n * jnp.mean(dn * n, axis=-1, keepdims=True)
    ) * inverse


def add_rows(ref, place, values):
    total = jnp.sum(values, axis=0, keepdims=True)
    for c in range(values.shape[1] // 512):
        ref[place + c : place + c + 1, :] += total[:, 512 * c : 512 * c + 512]


def start_small(ref):
    @pl.when(pl.program_id(0) == 0)
    def _():
        ref[...] = jnp.zeros_like(ref)


def put_heads(write, value, nh):
    for pair in range(value.shape[1] // 128):
        part = value[:, 128 * pair : 128 * pair + 128]
        if nh == 2:
            write(pair, part.astype(BF))
        else:
            low = lax.broadcasted_iota(jnp.int32, part.shape, 1) < 64
            write(2 * pair, jnp.where(low, part, 0.0).astype(BF))
            write(2 * pair + 1, jnp.where(low, pltpu.roll(part, 64, 1), 0.0).astype(BF))


def take_heads(read, units, nh):
    if nh == 2:
        return jnp.concatenate([read(u) for u in range(units)], axis=1)
    pairs = [
        (read(2 * u).astype(F32) + pltpu.roll(read(2 * u + 1).astype(F32), 64, 1)).astype(BF)
        for u in range(units // 2)
    ]
    return jnp.concatenate(pairs, axis=1)


def lines_kernel(*refs):
    out = refs[-1]
    out[...] = jnp.zeros_like(out)
    place = 0
    for ref in refs[:-1]:
        for c in range(ref.shape[0] // 512):
            out[place : place + 1, :] = ref[512 * c : 512 * c + 512].astype(F32).reshape(1, 512)
            place += 1


def open_kernel(
    x_ref, lines_ref, wu_ref, wd_ref, wi_ref, x1_ref, h1_ref, a_ref, sp_ref, h2_ref, u_ref,
    x, lines, wu, wd, wi, x1, h1, a1, sp, h2, u, total, sems, *, nh, first, recs,
):
    turn = pl.program_id(0)
    rec = first + turn
    rows = x.shape[0]
    parts = wu.shape[1] // 512
    lane = lanes(sems)
    ahead = lane(*one((x_ref.at[rec], x), (lines_ref, lines)))
    up = lane(parts, lambda f: [(wu_ref.at[:, part_of(f)], wu.at[:, part_of(f)])])
    down = lane(parts, lambda f: [(wd_ref.at[part_of(f), :], wd.at[part_of(f), :])])
    wide = lane(3, lambda f: [(wi_ref.at[:, part_of(f)], wi.at[:, part_of(f)])])
    out_h1 = lane(*one((h1, h1_ref.at[rec])))
    out_hidden = lane(
        parts,
        lambda f: [
            (a1.at[:, part_of(f)], a_ref.at[rec, :, part_of(f)]),
            (sp.at[:, part_of(f)], sp_ref.at[rec, :, part_of(f)]),
        ],
    )
    out_x1 = lane(*one((x1, x1_ref.at[rec]), (h2, h2_ref.at[rec])))
    out_u = lane(3, lambda f: [(u.at[f], u_ref.at[:, turn // recs, f, turn % recs])])
    ahead.start()
    for f in range(parts):
        up.start(f)
        down.start(f)
    wide.start_all()
    ahead.wait()

    def normal(at):
        n, _ = norm_parts(x[at, :].astype(F32))
        h1[at, :] = (n * row(lines, "early_gain") + row(lines, "early_shift")).astype(BF)

    over_rows(rows, normal)
    out_h1.start()

    def keep(f, at, a, slope):
        a1[:, at] = a
        sp[:, at] = slope
        out_hidden.start(f)

    total[...] = feed(h1[...], wu, wd, up.wait, down.wait, keep)

    def second(at):
        value = x[at, :].astype(F32) + 0.5 * total[at, :]
        x1[at, :] = value
        n, _ = norm_parts(value)
        h2[at, :] = (n * row(lines, "attend_gain") + row(lines, "attend_shift")).astype(BF)

    over_rows(rows, second)
    out_x1.start()

    def project(kind):
        wide.wait(kind)

        def write(unit, part):
            u[kind, unit] = part

        put_heads(write, nn(h2[...], wi[:, part_of(kind)]), nh)
        out_u.start(kind)

    repeat(3, project)
    for out in (out_h1, out_hidden, out_x1, out_u):
        out.wait_all()


def gate_kernel(
    len_ref, o_ref, x1_ref, lines_ref, wo_ref, wc_ref, att_ref, x2_ref, h3_ref, g_ref, ga_ref, gb_ref,
    o, x1, lines, wo, wc, att, x2, h3, g, ga, gb, sems, *, nh, first, recs,
):
    turn = pl.program_id(0)
    rec = first + turn
    rows = x1.shape[0]
    channels = g.shape[1]
    parts = channels // 512
    lane = lanes(sems)
    ahead = lane(*one((o_ref.at[:, turn // recs, turn % recs], o), (wo_ref, wo)))
    then = lane(*one((x1_ref.at[rec], x1), (lines_ref, lines)))
    wide = lane(
        parts,
        lambda f: [
            (wc_ref.at[:, part_of(f)], wc.at[:, part_of(f)]),
            (wc_ref.at[:, part_of(f + parts)], wc.at[:, part_of(f + parts)]),
        ],
    )
    out_att = lane(*one((att, att_ref.at[rec])))
    out_x2 = lane(*one((x2, x2_ref.at[rec]), (h3, h3_ref.at[rec])))
    out_g = lane(
        parts,
        lambda f: [
            (held.at[:, part_of(f)], out.at[rec, :, part_of(f)])
            for held, out in ((g, g_ref), (ga, ga_ref), (gb, gb_ref))
        ],
    )
    ahead.start()
    then.start()
    wide.start_all()
    ahead.wait()
    att[...] = take_heads(lambda unit: o[unit], o.shape[0], nh)
    out_att.start()
    then.wait()
    x2[...] = x1[...] + nn(att[...], wo[...])

    def normal(at):
        n, _ = norm_parts(x2[at, :])
        h3[at, :] = (n * row(lines, "convolve_gain") + row(lines, "convolve_shift")).astype(BF)

    over_rows(rows, normal)
    out_x2.start()
    limit = len_ref[rec]
    place = lax.broadcasted_iota(jnp.int32, (rows, 1), 0)
    valid = jnp.where(place < limit, 1.0, 0.0)

    def step(f):
        at = part_of(f)
        wide.wait(f)
        lin = nn(h3[...], wc[:, at])
        sig = sigmoid(nn(h3[...], wc[:, part_of(f + parts)]))
        sv = sig * valid
        value = lin * sv
        g[:, at] = value.astype(BF)
        ga[:, at] = sv.astype(BF)
        gb[:, at] = (value * (1.0 - sig)).astype(BF)
        out_g.start(f)

    repeat(parts, step)
    for out in (out_att, out_x2, out_g):
        out.wait_all()


def middle_kernel(
    g_ref, halo_ref, x2_ref, cot_ref, dep, lines, wco, wu, wd,
    out_ref, dx3_ref, dg_ref, dhalo_ref, small_ref, ddep_ref, pack_ref,
    gx, cs, inv3, dcx, sp3, h4s, a4s, sp4, dz4s, dy4s, a3s, dy3s, tapped, dws, wcov, wuv, wdv, held, sems, out_sems,
):
    rec = pl.program_id(0)
    rows = x2_ref.shape[1]
    channels = g_ref.shape[2]
    strips = channels // 128
    taps = dep.shape[0] - 1
    start_small(small_ref)
    start_small(tapped)
    first = pl.multiple_of(rec * rows, 128)
    mine = pl.ds(first, rows)
    tile = 96
    fetched = [(wco, wcov)]
    for at in pieces(wu.shape[1]):
        fetched.append((wu.at[:, at], wuv.at[:, at]))
        fetched.append((wd.at[at, :], wdv.at[at, :]))
    fetched = [pltpu.make_async_copy(*pair, sems.at[k]) for k, pair in enumerate(fetched)]

    @pl.when(rec == 0)
    def _():
        for copy in fetched:
            copy.start()

    def ready(k):
        @pl.when(rec == 0)
        def _():
            fetched[k].wait()


    def conv(c):
        at = part_of(c, 128)
        gx[c, 0:16, :] = halo_ref[0, :, at].astype(F32)
        gx[c, 16:, :] = g_ref[0, :, at].astype(F32)
        for top in range(0, rows, tile):
            sums = dep[0:1, at] * gx[c, top + 2 : top + 2 + tile, :]
            for r in range(1, taps):
                sums = sums + dep[r : r + 1, at] * gx[c, top + 2 + r : top + 2 + r + tile, :]
            cs[top : top + tile, at] = sums

    repeat(strips, conv)

    def inner(t):
        there = pl.ds(pl.multiple_of(t * 64, 64), 64)
        n, inverse = norm_parts(cs[there, :])
        cs[there, :] = n
        inv3[there, :] = inverse
        w = n * broad_row(lines, "inner_gain", channels) + broad_row(lines, "inner_shift", channels)
        sig = sigmoid(w)
        a3s[pl.ds(first + pl.multiple_of(t * 64, 64), 64), :] = (w * sig).astype(BF)
        sp3[there, :] = (sig * (1.0 + w * (1.0 - sig))).astype(BF)

    repeat(rows // 64, inner)
    ready(0)
    x3 = x2_ref[0] + nn(a3s[mine, :], wcov[...])
    n4, inv4 = norm_parts(x3)
    h4 = (n4 * row(lines, "late_gain") + row(lines, "late_shift")).astype(BF)
    h4s[mine, :] = h4

    def keep(f, at, a, slope):
        a4s[mine, at] = a
        sp4[:, at] = slope

    y = feed(h4, wuv, wdv, lambda f: ready(1 + 2 * f), lambda f: ready(2 + 2 * f), keep)
    x4 = x3 + 0.5 * y
    n5, inv5 = norm_parts(x4)
    out_ref[0] = (n5 * row(lines, "final_gain") + row(lines, "final_shift")).astype(BF)
    cot = cot_ref[0].astype(F32)
    add_rows(small_ref, 8, cot * n5)
    add_rows(small_ref, 9, cot)
    dx4 = norm_pull(n5, inv5, row(lines, "final_gain"), cot)
    dx3_ref[0] = dx4
    dy4 = (0.5 * dx4).astype(BF)
    dy4s[mine, :] = dy4

    def keep_back(f, at, dz):
        dz4s[mine, at] = dz

    done = lambda f: None
    dh = feed_back(dy4, wuv, wdv, done, done, lambda f, at: sp4[:, at], keep_back)
    add_rows(small_ref, 6, dh * n4)
    add_rows(small_ref, 7, dh)
    dx3 = dx3_ref[0] + norm_pull(n4, inv4, row(lines, "late_gain"), dh)
    dx3_ref[0] = dx3
    dy3s[mine, :] = dx3.astype(BF)

    def pull(f):
        at = part_of(f)
        dws[:, at] = nt(dy3s[mine, :], wcov[at, :]) * sp3[:, at].astype(F32)

    repeat(channels // 512, pull)

    def inner_back(t):
        there = pl.ds(pl.multiple_of(t * 64, 64), 64)
        dw = dws[there, :]
        n = cs[there, :]
        add_rows(small_ref, 2, dw * n)
        add_rows(small_ref, 4, dw)
        cs[there, :] = norm_pull(n, inv3[there, :], broad_row(lines, "inner_gain", channels), dw)

    repeat(rows // 64, inner_back)

    def conv_back(c):
        at = part_of(c, 128)
        dcx[0:16, :] = jnp.zeros((16, 128), F32)
        dcx[16 : 16 + rows, :] = cs[:, at]
        dcx[16 + rows :, :] = jnp.zeros((16, 128), F32)
        sums = [jnp.zeros((8, 128), F32)] * taps
        for top in range(0, rows, tile):
            dc = dcx[16 + top : 16 + top + tile, :]
            for r in range(taps):
                term = dc * gx[c, top + 2 + r : top + 2 + r + tile, :]
                sums[r] = sums[r] + jnp.sum(term.reshape(tile // 8, 8, 128), axis=0)
        for r in range(taps):
            tapped[c, 8 * r : 8 * r + 8, :] += sums[r]
        for top in range(0, rows + 16, tile):
            size = min(tile, rows + 16 - top)
            sums = dep[0:1, at] * dcx[top + 14 : top + 14 + size, :]
            for r in range(1, taps):
                sums = sums + dep[r : r + 1, at] * dcx[top + 14 - r : top + 14 - r + size, :]
            if top == 0:
                dhalo_ref[0, :, at] = sums[0:16].astype(BF)
                dg_ref[0, 0 : size - 16, at] = sums[16:].astype(BF)
            else:
                dg_ref[0, top - 16 : top - 16 + size, at] = sums.astype(BF)

    repeat(strips, conv_back)

    @pl.when(rec == pl.num_programs(0) - 1)
    def _():
        def depth(c):
            for r in range(taps):
                ddep_ref[r : r + 1, part_of(c, 128)] = jnp.sum(
                    tapped[c, 8 * r : 8 * r + 8, :], axis=0, keepdims=True
                )

        ddep_ref[taps:, :] = jnp.zeros((1, channels), F32)
        repeat(strips, depth)
        move = mover(out_sems)
        sent = []

        def send(who, there):
            sent.append(move(held.at[who, :, there], pack_ref.at[who, :, there]))

        place = spread_columns(send, held, 0, h4s, dz4s, done)
        place = spread_rows(send, held, place, a4s, dy4s, done)
        spread_rows(send, held, place, a3s, dy3s, done)
        settle(sent)


def share(kind, lane, held, outs, core, place, left, right, ready):
    columns = kind == "columns"
    parts = (right if columns else left).shape[1] // 512
    where = (columns_of if columns else rows_of)(held, place, left, right)

    def make(f):
        who, there = where(f)
        if core is None:
            return [(held.at[who, :, there], outs[0].at[who, :, there])]
        return [(held.at[who, c, there], out.at[who, there]) for c, out in zip((core, 1 - core), outs)]

    out = lane(parts, make)
    (share_columns if columns else share_rows)(
        held, place, left, right, ready, lambda f, who, there: out.start(f)
    )
    height = left.shape[1] // (held.shape[0] * held.shape[1])
    return place + height * (parts if columns else 1), out


def ungate_kernel(
    dg_ref, back_ref, ga_ref, gb_ref, dx3_ref, x2_ref, lines_ref, wc_ref, wo_ref,
    dx2_ref, du_ref, dy2_ref, do_ref, small_ref,
    dg, back, lines, wc, wo, ga, gb, dx3, x2, dx2, du, dy2, do, small, dgx, total, sems, *, nh, first, recs,
):
    turn = pl.program_id(0)
    rec = first + turn
    rows = x2.shape[0]
    channels = ga.shape[1]
    parts = channels // 512
    lane = lanes(sems)
    ahead = lane(*one((back_ref.at[rec], back)))
    fetch = lane(
        parts,
        lambda f: [
            (dg_ref.at[rec, :, part_of(f)], dg.at[:, part_of(f)]),
            (ga_ref.at[rec, :, part_of(f)], ga.at[:, part_of(f)]),
            (gb_ref.at[rec, :, part_of(f)], gb.at[:, part_of(f)]),
            (wc_ref.at[:, part_of(f)], wc.at[:, part_of(f)]),
            (wc_ref.at[:, part_of(f + parts)], wc.at[:, part_of(f + parts)]),
        ],
    )
    then = lane(*one((x2_ref.at[rec], x2), (dx3_ref.at[rec], dx3), (lines_ref, lines), (wo_ref, wo)))
    out_du = lane(
        parts,
        lambda f: [
            (du.at[:, part_of(f)], du_ref.at[rec, :, part_of(f)]),
            (du.at[:, part_of(f + parts)], du_ref.at[rec, :, part_of(f + parts)]),
        ],
    )
    out_dx2 = lane(*one((dx2, dx2_ref.at[rec]), (dy2, dy2_ref.at[rec]), (small, small_ref)))
    out_do = lane(*one((do, do_ref.at[:, turn // recs, turn % recs])))
    ahead.start()
    fetch.start_all()
    then.start()
    start_small(small)
    total[...] = jnp.zeros_like(total)
    ahead.wait()

    def step(f):
        at = part_of(f)
        up = part_of(f + parts)
        fetch.wait(f)
        dgx[...] = dg[:, at].astype(F32)
        dgx[rows - 16 :, :] += back[:, at].astype(F32)
        value = dgx[...]
        lin = (value * ga[:, at].astype(F32)).astype(BF)
        gate = (value * gb[:, at].astype(F32)).astype(BF)
        du[:, at] = lin
        du[:, up] = gate
        out_du.start(f)
        total[...] += nt(lin, wc[:, at]) + nt(gate, wc[:, up])

    repeat(parts, step)
    then.wait()

    def pull(at):
        n, inverse = norm_parts(x2[at, :])
        dh = total[at, :]
        add_rows(small, 0, dh * n)
        add_rows(small, 1, dh)
        value = dx3[at, :] + norm_pull(n, inverse, row(lines, "convolve_gain"), dh)
        dx2[at, :] = value
        dy2[at, :] = value.astype(BF)

    over_rows(rows, pull)
    out_dx2.start()

    def write(unit, part):
        do[unit] = part

    put_heads(write, nt(dy2[...], wo[...]), nh)
    out_do.start()
    for out in (out_du, out_dx2, out_do):
        out.wait_all()


def project_kernel(
    u_ref, x1_ref, dx2_ref, lines_ref, wi_ref, dx1_ref, dy_ref, dp_ref, small_ref,
    lines, wi, u, x1, dx2, dx1, dy, dp, small, total, sems, *, nh, first, recs,
):
    turn = pl.program_id(0)
    rec = first + turn
    rows = x1.shape[0]
    lane = lanes(sems)
    fetch = lane(
        3,
        lambda f: [
            (u_ref.at[:, turn // recs, f, turn % recs], u.at[f]), (wi_ref.at[:, part_of(f)], wi.at[:, part_of(f)]),
        ],
    )
    then = lane(*one((x1_ref.at[rec], x1), (dx2_ref.at[rec], dx2), (lines_ref, lines)))
    out_dp = lane(3, lambda f: [(dp.at[:, part_of(f)], dp_ref.at[rec, :, part_of(f)])])
    out_dx1 = lane(*one((dx1, dx1_ref.at[rec]), (dy, dy_ref.at[rec]), (small, small_ref)))
    fetch.start_all()
    then.start()
    start_small(small)
    total[...] = jnp.zeros_like(total)

    def step(kind):
        at = part_of(kind)
        fetch.wait(kind)
        value = take_heads(lambda unit: u[kind, unit], u.shape[1], nh)
        dp[:, at] = value
        out_dp.start(kind)
        total[...] += nt(value, wi[:, at])

    repeat(3, step)
    then.wait()

    def pull(at):
        n, inverse = norm_parts(x1[at, :])
        dh = total[at, :]
        add_rows(small, 0, dh * n)
        add_rows(small, 1, dh)
        value = dx2[at, :] + norm_pull(n, inverse, row(lines, "attend_gain"), dh)
        dx1[at, :] = value
        dy[at, :] = (0.5 * value).astype(BF)

    over_rows(rows, pull)
    out_dx1.start()
    for out in (out_dp, out_dx1):
        out.wait_all()


def close_kernel(
    dy_ref, dx1_ref, x_ref, sp_ref, lines_ref, wu_ref, wd_ref, out_ref, dz_ref, small_ref,
    dy, lines, wu, wd, sp, dx1, x, dz, out, small, total, sems, *, first,
):
    rec = first + pl.program_id(0)
    rows = x.shape[0]
    parts = wu.shape[1] // 512
    lane = lanes(sems)
    ahead = lane(*one((dy_ref.at[rec], dy)))
    down = lane(
        parts,
        lambda f: [
            (wd_ref.at[part_of(f), :], wd.at[part_of(f), :]), (sp_ref.at[rec, :, part_of(f)], sp.at[:, part_of(f)]),
        ],
    )
    up = lane(parts, lambda f: [(wu_ref.at[:, part_of(f)], wu.at[:, part_of(f)])])
    then = lane(*one((x_ref.at[rec], x), (dx1_ref.at[rec], dx1), (lines_ref, lines)))
    out_dz = lane(parts, lambda f: [(dz.at[:, part_of(f)], dz_ref.at[rec, :, part_of(f)])])
    out_dx = lane(*one((out, out_ref.at[rec]), (small, small_ref)))
    ahead.start()
    for f in range(parts):
        down.start(f)
        up.start(f)
    then.start()
    start_small(small)
    ahead.wait()

    def keep(f, at, value):
        dz[:, at] = value
        out_dz.start(f)

    total[...] = feed_back(dy[...], wu, wd, up.wait, down.wait, lambda f, at: sp[:, at], keep)
    then.wait()

    def pull(at):
        n, inverse = norm_parts(x[at, :].astype(F32))
        dh = total[at, :]
        add_rows(small, 0, dh * n)
        add_rows(small, 1, dh)
        out[at, :] = (dx1[at, :] + norm_pull(n, inverse, row(lines, "early_gain"), dh)).astype(BF)

    over_rows(rows, pull)
    out_dx.start()
    for lane_out in (out_dz, out_dx):
        lane_out.wait_all()


def share_kernel(core_ref, *refs, kinds, extra, apart):
    jobs = len(kinds)
    ins = refs[: 2 * jobs]
    more = refs[2 * jobs : 2 * jobs + extra]
    outs = refs[2 * jobs + extra : 2 * jobs + extra + 1 + apart]
    held = refs[2 * jobs + extra + 1 + apart :]
    packed, small, sems = held[2 * jobs :]
    core = core_ref[0] if apart else None
    lane = lanes(sems)
    plan = []
    for k, kind in enumerate(kinds):
        left, right = ins[2 * k : 2 * k + 2]
        left_held, right_held = held[2 * k : 2 * k + 2]
        if kind == "columns":
            first = lane(*one((left, left_held)))
            source, target = right, right_held
        else:
            first = lane(*one((right, right_held)))
            source, target = left, left_held
        parts = lane(
            source.shape[1] // 512,
            lambda f, source=source, target=target: [(source.at[:, part_of(f)], target.at[:, part_of(f)])],
        )
        first.start()
        parts.start_all()
        plan.append((left_held, right_held, first, parts))
    waits = []
    place = 0
    for kind, (left, right, first, parts) in zip(kinds, plan):
        first.wait()
        place, out = share(kind, lane, packed, outs, core, place, left, right, parts.wait)
        waits.append(out)
    if extra:
        small_shares(more, packed, small, place)
        there = pl.ds(place, packed.shape[2] - place)
        out = lane(
            *one(*[(packed.at[:, c, there], target.at[:, there]) for c, target in zip((core, 1 - core), outs)])
        )
        out.start()
        waits.append(out)
    for out in waits:
        out.wait_all()


def small_shares(refs, packed, small, place):
    small_mid, ddep, table = refs[:3]
    batches = (len(refs) - 3) // 3
    count = packed.shape[0] * packed.shape[1]
    small[...] = jnp.zeros_like(small)
    for k in range(3):
        for ref in refs[3 + k * batches : 3 + k * batches + batches]:
            small[2 * k : 2 * k + 2, :] += ref[0:2, :]
    small[6:10, :] = small_mid[6:10, :]
    narrow = 512 // count
    broad = ddep.shape[1] // count
    high = table.shape[0] // count
    packed[:, :, place:, :] = jnp.zeros(packed.shape[:2] + (packed.shape[2] - place, 512), BF)
    blocks = ddep.shape[1] // 512
    inner = [
        jnp.concatenate([small_mid[first + c : first + c + 1, :] for c in range(blocks)], axis=1)
        for first in (2, 4)
    ]
    inner = jnp.concatenate(inner, axis=0)
    for s in range(count):
        there = slice(place, place + 16)
        packed[s // 2, s % 2, there, 0:narrow] = small[:, narrow * s : narrow * s + narrow].astype(BF)
        packed[s // 2, s % 2, place : place + 2, 128 : 128 + broad] = inner[
            :, broad * s : broad * s + broad
        ].astype(BF)
        packed[s // 2, s % 2, there, 256 : 256 + broad] = ddep[:, broad * s : broad * s + broad].astype(BF)
        packed[s // 2, s % 2, place : place + high, 384 : 384 + table.shape[1]] = table[
            high * s : high * s + high, :
        ].astype(BF)


def finish_kernel(index_ref, *refs, parts):
    outs = refs[3 * parts : len(refs) - 3]
    sums, proj, last = refs[len(refs) - 3 :]
    for group, held in enumerate((sums, proj, last)):
        for k in range(parts):
            held[index_ref[0] ^ k] = refs[group * parts + k][...]
    (
        e_gain, e_shift, e_up, e_down, a_gain, a_shift, a_in, a_out, table, c_gain, c_shift, c_in, depth,
        i_gain, i_shift, c_out, l_gain, l_shift, l_up, l_down, f_gain, f_shift,
    ) = outs

    def reader(ref):
        def read(first, size):
            if len(ref.shape) == 2:
                return ref[first : first + size, :].astype(F32)
            height = ref.shape[1]
            pieces = []
            while size:
                piece, top = divmod(first, height)
                here = min(size, height - top)
                pieces.append(ref[piece].astype(F32)[top : top + here, :])
                first += here
                size -= here
            return pieces[0] if len(pieces) == 1 else jnp.concatenate(pieces, axis=0)

        return read

    def put(read, place, out):
        height = out.shape[0]
        for f in range(out.shape[1] // 512):
            out[:, 512 * f : 512 * f + 512] = read(place, height)
            place += height
        return place

    sums, proj, last = reader(sums), reader(proj), reader(last)
    put(sums, put(sums, put(sums, put(sums, put(sums, 0, l_up), l_down), c_out), c_in), a_out)
    put(proj, put(proj, 0, a_in), e_down)
    place = put(last, 0, e_up)
    small = last(place, 16)
    for line, out in enumerate(
        (e_gain, e_shift, a_gain, a_shift, c_gain, c_shift, l_gain, l_shift, f_gain, f_shift)
    ):
        out[...] = small[line : line + 1, 0 : out.shape[1]]
    i_gain[...] = small[0:1, 128 : 128 + i_gain.shape[1]]
    i_shift[...] = small[1:2, 128 : 128 + i_shift.shape[1]]
    depth[...] = small[0 : depth.shape[0], 256 : 256 + depth.shape[1]]
    table[...] = small[0 : table.shape[0], 384 : 384 + table.shape[1]]


def per_rec(array, first=0):
    shape = (1,) + array.shape[1:]
    tail = (0,) * (array.ndim - 1)
    return pl.BlockSpec(shape, lambda r, *_: (r + first,) + tail)


def whole(array):
    zeros = (0,) * array.ndim
    return pl.BlockSpec(array.shape, lambda r, *_: zeros, pipeline_mode=pl.Buffered(1))


def whole_out(array):
    zeros = (0,) * len(array.shape)
    return pl.BlockSpec(array.shape, lambda r, *_: zeros)


def per_unit(array, recs):
    units, rest = array.shape[0], array.shape[2:]
    if len(array.shape) == 6:
        return pl.BlockSpec(
            (units, 1, rest[0], 1) + rest[2:], lambda r, *_: (0, r // recs, 0, r % recs, 0, 0)
        )
    return pl.BlockSpec((units, 1, 1) + rest[1:], lambda r, *_: (0, r // recs, r % recs, 0, 0))


def far(array):
    return pl.BlockSpec(memory_space=pl.ANY)


def spot(shape, kind=F32):
    return jax.ShapeDtypeStruct(shape, kind)


def run(
    kernel, seqs, ins, in_specs, outs, out_specs, scratch=(), prefetch=(), after=(), into=(),
    micros=6,
):
    held = (*after, *into)
    plain = kernel
    place = len(prefetch) + len(ins)

    def kernel(*refs):
        plain(*refs[:place], *refs[place + len(held) :])

    return pl.pallas_call(
        kernel,
        grid_spec=pltpu.PrefetchScalarGridSpec(
            num_scalar_prefetch=len(prefetch),
            grid=(seqs,),
            in_specs=[*in_specs, *(pl.BlockSpec(memory_space=pl.ANY) for _ in held)],
            out_specs=out_specs,
            scratch_shapes=list(scratch),
        ),
        out_shape=outs,
        cost_estimate=cost(micros),
        input_output_aliases={place + len(after) + k: k for k in range(len(into))},
        compiler_params=pltpu.CompilerParams(vmem_limit_bytes=58 * MEGA),
    )(*prefetch, *ins, *held)


def unit_plan(seqs, heads):
    parts = lax.axis_size("tm")
    if parts <= heads:
        return heads // parts, seqs, 1
    return 1, seqs * heads // parts, parts // heads


def distance_hot(seq_total, bucket_count):
    limits = jnp.array(boundaries(seq_total), jnp.int32)
    places = jnp.arange(seq_total, dtype=jnp.int32)
    bucket = jnp.sum((places[:, None] >= limits[None, :]).astype(jnp.int32), axis=1)
    return (bucket[:, None] == jnp.arange(bucket_count, dtype=jnp.int32)[None, :]).astype(FLOAT)


def bias_strip(table, hot, nh, split):
    first = lax.axis_index("tm") // split * nh
    mine = lax.dynamic_slice_in_dim(table, first, nh, 1)
    per = jnp.dot(hot, mine, precision=HIGHEST).T
    pad = 2 * KEYS
    shifted = [
        jnp.pad(per, ((0, 0), (pad + s, 0)), constant_values=NEGATIVE)[:, : pad + hot.shape[0]]
        for s in range(8)
    ]
    return make_strip(jnp.stack(shifted, 1))


def table_grad(diagonals, hot, nh, split, heads):
    per = sum(jnp.pad(diagonals[:, s, KEYS + s :], ((0, 0), (0, s))) for s in range(8))
    mine = jnp.dot(hot.T, per.T, precision=HIGHEST)
    first = lax.axis_index("tm") // split * nh
    return lax.dynamic_update_slice_in_dim(
        jnp.zeros((hot.shape[1], heads), FLOAT), mine, first, 1
    )


def swap(values):
    return lax.all_to_all(values, "tm", 0, 0, tiled=True)


def body(
    frames, cotangent, lengths,
    early_gain, early_shift, early_up, early_down,
    attend_gain, attend_shift, attend_input, attend_output, distance_bias,
    convolve_gain, convolve_shift, convolve_input, depthwise, inner_gain, inner_shift, convolve_output,
    late_gain, late_shift, late_up, late_down, final_gain, final_shift,
):
    seqs, rows, width = frames.shape
    heads = distance_bias.shape[1]
    count = lax.axis_size("rows")
    parts = lax.axis_size("tm")
    hidden = early_up.shape[1]
    channels = convolve_output.shape[0]
    nh, recs, split = unit_plan(seqs, heads)
    units = heads // nh
    batches = seqs if split == 1 else 1
    here = seqs // batches
    recs = recs // batches
    tokens = seqs * rows
    vectors = (
        early_gain, early_shift, attend_gain, attend_shift, convolve_gain, convolve_shift,
        late_gain, late_shift, final_gain, final_shift, inner_gain, inner_shift,
    )
    lines = pl.pallas_call(lines_kernel, out_shape=spot((16, 512)))(*vectors)
    core = (lax.axis_index("rows") % 2).astype(jnp.int32)[None]
    merge = lambda v: v.reshape(tokens, -1)

    def wide(*kinds):
        return spot((units, split, *kinds, recs, rows, 128), BF)

    def held(columns, kind=BF):
        return pltpu.VMEM((rows, columns), kind)

    def like(array):
        return pltpu.VMEM(array.shape, array.dtype)

    def sems(size):
        return pltpu.SemaphoreType.DMA((size,))

    def shares(kinds, ins, height, extra=(), after=(), apart=True):
        shape = (count // 2, 2, height // 512 // count, 512)
        outs = (spot((shape[0],) + shape[2:], BF),) * 2 if apart else (spot(shape, BF),)
        return run(
            functools.partial(share_kernel, kinds=kinds, extra=len(extra), apart=apart), 1, (*ins, *extra),
            [far(v) for v in ins] + [whole(v) for v in extra], outs, [far(v) for v in outs],
            scratch=[like(v) for v in ins] + [pltpu.VMEM(shape, BF), pltpu.VMEM((16, 512), F32), sems(40)],
            after=after, prefetch=(core,),
        )

    def own(columns, kind=BF):
        return spot((seqs, rows, columns), kind)

    kept = ()
    sent = []
    for batch in range(batches):
        ins = (frames, lines, early_up, early_down, attend_input)
        outs = (own(width, F32), own(width), own(hidden), own(hidden), own(width), wide(3))
        *kept, qkv = run(
            functools.partial(open_kernel, nh=nh, first=batch * here, recs=recs), here, ins,
            [far(v) for v in ins], outs, [far(v) for v in outs],
            scratch=(
                held(width), like(lines), like(early_up), like(early_down), like(attend_input), held(width, F32),
                held(width), held(hidden), held(hidden), held(width), pltpu.VMEM((3, units, rows, 128), BF),
                held(width, F32), sems(40),
            ),
            into=kept,
        )
        sent.append(swap(qkv.reshape(parts, 3, recs, rows, 128)))
    x1, h1, a1, sp1, h2 = kept
    hot = distance_hot(rows * parts, distance_bias.shape[0])
    strip = bias_strip(distance_bias.astype(FLOAT), hot, nh, split)
    mine = [
        lax.dynamic_slice_in_dim(lengths, batch * here + lax.axis_index("tm") % split * recs, recs, 0)
        for batch in range(batches)
    ]
    attended = [attn_fwd(mine[batch], sent[batch], strip, nh) for batch in range(batches)]

    limits = lengths - lax.axis_index("tm").astype(jnp.int32) * rows
    kept = ()
    for batch in range(batches):
        back = swap(attended[batch][0]).reshape(units, split, recs, rows, 128)
        ins = (back, x1, lines, attend_output, convolve_input)
        outs = (own(width), own(width, F32), own(width), own(channels), own(channels), own(channels))
        kept = run(
            functools.partial(gate_kernel, nh=nh, first=batch * here, recs=recs), here, ins,
            [far(v) for v in ins], outs, [far(v) for v in outs], prefetch=(limits,), into=kept,
            scratch=(
                pltpu.VMEM((units, rows, 128), BF), held(width, F32), like(lines), like(attend_output),
                like(convolve_input), held(width), held(width, F32), held(width),
                held(channels), held(channels), held(channels), sems(40),
            ),
        )
    att, x2, h3, g, ga, gb = kept
    halo = passed_along(g[:, rows - 16 :, :], "tm", 1)

    dep = jnp.pad(depthwise.astype(FLOAT).T, ((0, 1), (0, 0)))
    ins = (g, halo, x2, cotangent, dep, lines, convolve_output, late_up, late_down)
    height = (width * hidden * 2 + channels * width) // 512 // count
    outs = (
        own(width), own(width, F32), own(channels), spot((seqs, 16, channels), BF),
        spot((16, 512)), spot((16, channels)), spot((count // 2, 2, height, 512), BF),
    )
    layer_out, dx3, dg, dhalo, small_mid, ddep, pack_mid = run(
        middle_kernel, seqs, ins,
        [per_rec(v) for v in ins[:4]] + [whole(v) for v in ins[4:6]] + [far(v) for v in ins[6:]],
        outs, [per_rec(v) for v in outs[:4]] + [whole_out(v) for v in outs[4:6]] + [far(outs[6])],
        scratch=(
            pltpu.VMEM((channels // 128, rows + 16, 128), F32), pltpu.VMEM((rows, channels), F32),
            pltpu.VMEM((rows, 1), F32), pltpu.VMEM((rows + 32, 128), F32), pltpu.VMEM((rows, channels), BF),
            pltpu.VMEM((tokens, width), BF), pltpu.VMEM((tokens, hidden), BF), pltpu.VMEM((rows, hidden), BF),
            pltpu.VMEM((tokens, hidden), BF), pltpu.VMEM((tokens, width), BF),
            pltpu.VMEM((tokens, channels), BF), pltpu.VMEM((tokens, width), BF),
            pltpu.VMEM((channels // 128, 128, 128), F32), pltpu.VMEM((rows, channels), F32),
            like(convolve_output), like(late_up), like(late_down), like(outs[6]), sems(16), sems(16),
        ),
        micros=200,
    )
    returned = passed_along(dhalo, "tm", -1)
    sums_mid = offloaded(pack_mid)

    kept = ()
    sent_back = []
    small_gate = []
    for batch in range(batches):
        ins = (dg, returned, ga, gb, dx3, x2, lines, convolve_input, attend_output)
        outs = (own(width, F32), own(2 * channels), own(width), wide(), spot((8, 512)))
        *kept, do, small = run(
            functools.partial(ungate_kernel, nh=nh, first=batch * here, recs=recs), here, ins,
            [far(v) for v in ins], outs, [far(v) for v in outs],
            scratch=(
                held(channels), pltpu.VMEM((16, channels), BF), like(lines), like(convolve_input), like(attend_output),
                held(channels), held(channels), held(width, F32), held(width, F32), held(width, F32),
                held(2 * channels), held(width), pltpu.VMEM((units, rows, 128), BF), pltpu.VMEM((8, 512), F32),
                held(512, F32), held(width, F32), sems(40),
            ),
            into=kept,
        )
        small_gate.append(small)
        sent_back.append(swap(do.reshape(parts, recs, rows, 128)))
    dx2, du, dy2 = kept
    pack_gate = shares(
        ("columns", "columns"), (merge(h3), merge(du), merge(att), merge(dy2)), 2 * channels * width + width * width,
        apart=False,
    )
    own_grads = []
    diagonals = 0.0
    for batch in range(batches):
        out, lse = attended[batch]
        grad, diagonal = attn_bwd(mine[batch], sent[batch], sent_back[batch], out, lse, strip, nh)
        diagonals = diagonals + diagonal
        own_grads.append(swap(grad).reshape(units, split, 3, recs, rows, 128))
    sums_gate = offloaded(pack_gate[0])
    grad_table = table_grad(diagonals, hot, nh, split, heads)

    kept = ()
    kept_two = ()
    small_proj = []
    small_first = []
    for batch in range(batches):
        ins = (own_grads[batch], x1, dx2, lines, attend_input)
        outs = (own(width, F32), own(width), own(3 * width), spot((8, 512)))
        if batch == batches - 1:
            part_rest = time_sum(jnp.concatenate([sums_mid, sums_gate], axis=0))
        *kept, small = run(
            functools.partial(project_kernel, nh=nh, first=batch * here, recs=recs), here, ins,
            [far(v) for v in ins], outs, [far(v) for v in outs],
            scratch=(
                like(lines), like(attend_input), pltpu.VMEM((3, units, rows, 128), BF), held(width, F32),
                held(width, F32), held(width, F32), held(width), held(3 * width), pltpu.VMEM((8, 512), F32),
                held(width, F32), sems(40),
            ),
            into=kept, after=(sums_mid,) if batch == batches - 1 else (),
        )
        small_proj.append(small)
        dx1, dy1, dp = kept
        if batch == batches - 1:
            pack_proj = shares(
                ("columns", "rows"), (merge(h2), merge(dp), merge(a1), merge(dy1)), width * hidden + width * 3 * width,
                apart=False,
            )
            sums_proj = offloaded(pack_proj[0])
            before = ()
        else:
            before = ()
        ins = (dy1, dx1, frames, sp1, lines, early_up, early_down)
        outs = (own(width), own(hidden), spot((8, 512)))
        *kept_two, small = run(
            functools.partial(close_kernel, first=batch * here), here, ins,
            [far(v) for v in ins], outs, [far(v) for v in outs],
            scratch=(
                held(width), like(lines), like(early_up), like(early_down), held(hidden), held(width, F32),
                held(width), held(hidden), held(width), pltpu.VMEM((8, 512), F32), held(width, F32), sems(40),
            ),
            into=kept_two, after=before,
        )
        small_first.append(small)
    dx0, dz1 = kept_two
    pack_last = shares(
        ("columns",), (merge(h1), merge(dz1)), width * hidden + 32 * 512 * count,
        extra=(small_mid, ddep, grad_table, *small_first, *small_proj, *small_gate), after=(part_rest,),
    )
    part_last = along_chips(along_time(between_cores(*pack_last)))
    part_proj = time_sum_by_steps(sums_proj)
    totals = (part_rest, *others(part_rest), part_proj, *others(part_proj), part_last, *others(part_last))
    return (layer_out, dx0) + finish(
        totals, count, parts, width, hidden, channels, depthwise.shape[1], distance_bias.shape
    )


def offloaded(packed):
    sent = packed.reshape(-1, packed.shape[3])
    return lax.psum_scatter(sent, "rows", scatter_dimension=0, tiled=True)


def with_others(mine):
    parts = lax.axis_size("tm")
    return lax.all_to_all(jnp.broadcast_to(mine, (parts,) + mine.shape), "tm", 0, 0, tiled=True)


def total(blocks):
    return jnp.sum(blocks.astype(FLOAT), axis=0).astype(BF)


def between_cores(keep, send):
    devices = range(lax.axis_size("rows"))
    got = lax.ppermute(send, "rows", [(i, i ^ 1) for i in devices])
    return (keep.astype(FLOAT) + got.astype(FLOAT)).astype(BF)


def time_sum(share):
    parts = lax.axis_size("tm")
    blocks = share.reshape((parts, share.shape[0] // parts) + share.shape[1:])
    return total(lax.all_to_all(blocks, "tm", 0, 0, tiled=True))


def time_sum_by_steps(share):
    parts = lax.axis_size("tm")
    me = lax.axis_index("tm")
    blocks = share.reshape((parts, share.shape[0] // parts) + share.shape[1:])
    pick = lambda k: lax.dynamic_index_in_dim(blocks, me ^ k, 0, keepdims=False)
    sums = pick(0).astype(FLOAT)
    for k in range(1, parts):
        got = lax.ppermute(pick(k), "tm", [(i, i ^ k) for i in range(parts)])
        sums = sums + got.astype(FLOAT)
    return sums.astype(BF)


def others(mine):
    parts = lax.axis_size("tm")
    return [lax.ppermute(mine, "tm", [(i, i ^ k) for i in range(parts)]) for k in range(1, parts)]


def along_time(half):
    chips, height, width = half.shape
    parts = lax.axis_size("tm")
    blocks = jnp.transpose(half.reshape(chips, parts, height // parts, width), (1, 0, 2, 3))
    return total(lax.all_to_all(blocks, "tm", 0, 0, tiled=True))


def along_chips(part):
    devices = range(lax.axis_size("rows"))
    groups = [[i for i in devices if i % 2 == core] for core in range(2)]
    return total(lax.all_to_all(part, "rows", 0, 0, axis_index_groups=groups, tiled=True))


def finish(totals, count, parts, width, hidden, channels, taps, table_shape):
    share = width // count
    line = (1, share)
    broad = (1, channels // count)
    shapes = (
        line, line, (share, hidden), (hidden // count, width), line, line, (share, 3 * width), (share, width),
        (table_shape[0] // count, table_shape[1]), line, line, (share, 2 * channels), (taps, channels // count),
        broad, broad, (channels // count, width), line, line, (share, hidden), (hidden // count, width), line, line,
    )
    outs = tuple(spot(shape) for shape in shapes)
    me = lax.axis_index("tm").astype(jnp.int32)[None]
    got = list(
        run(
            functools.partial(finish_kernel, parts=parts), 1, totals, [whole(v) for v in totals],
            outs, [whole_out(v) for v in outs], prefetch=(me,), micros=3,
            scratch=[pltpu.VMEM((parts,) + v.shape, BF) for v in totals[::parts]],
        )
    )
    got[12] = got[12].T
    for place, shape in enumerate(shapes):
        if shape[0] == 1:
            got[place] = got[place].reshape(-1)
    return tuple(got)


def solution(mesh):
    placed = (
        P("rows", "tm", None),
        P("rows", "tm", None),
        P("rows"),
        P(),
        P(),
        P(),
        P(),
        P(),
        P(),
        P(),
        P(),
        P(),
        P(),
        P(),
        P(),
        P(),
        P(),
        P(),
        P(),
        P(),
        P(),
        P(),
        P(),
        P(),
        P(),
    )
    return jax.shard_map(
        body,
        mesh=mesh,
        in_specs=placed,
        out_specs=(
            P("rows", "tm", None),
            P("rows", "tm", None),
            P("rows"),
            P("rows"),
            P("rows", None),
            P("rows", None),
            P("rows"),
            P("rows"),
            P("rows", None),
            P("rows", None),
            P("rows", None),
            P("rows"),
            P("rows"),
            P("rows", None),
            P("rows", None),
            P("rows"),
            P("rows"),
            P("rows", None),
            P("rows"),
            P("rows"),
            P("rows", None),
            P("rows", None),
            P("rows"),
            P("rows"),
        ),
        check_vma=False,
    )
```

```python
import functools

import jax
import jax.numpy as jnp
from jax import lax
from jax.experimental import pallas as pl
from jax.experimental.pallas import tpu as pltpu
from jax.sharding import PartitionSpec as P

EPSILON = 1e-05
NEGATIVE = -1e30
HIGHEST = lax.Precision.HIGHEST
BFLOAT = jnp.bfloat16
FLOAT = jnp.float32
NEG = NEGATIVE
F32 = FLOAT
BF = BFLOAT


MEGA = 2**20
SCALE = 1


def cost(micros):
    micros = micros * SCALE
    return pl.CostEstimate(
        flops=int(micros * 1.1e9), bytes_accessed=int(micros * 3.6e6), transcendentals=0
    )


def passed_along(block, axis, distance):
    devices = range(lax.axis_size(axis))
    route = [(i - distance, i) for i in devices if i - distance in devices]
    return lax.ppermute(block, axis, route)


def boundaries(seq_total):
    edges_list = list(range(1, 16))
    for exponent in range(16):
        edges_list.append(int(16.0 * (seq_total / 16.0) ** (exponent / 16.0)))
    return edges_list


KEYS = 256
QUERIES = 512


def nt(a, b):
    return lax.dot_general(a, b, (((1,), (1,)), ((), ())), preferred_element_type=F32)


def nn(a, b):
    return lax.dot_general(a, b, (((1,), (0,)), ((), ())), preferred_element_type=F32)


def strip_kernel(base_ref, out_ref):
    heads, keys, _ = out_ref.shape
    for h in range(heads):
        base = base_ref[h]
        for g in range(keys // 8):
            out_ref[h, 8 * g : 8 * g + 8, :] = pltpu.roll(base, 8 * g, 1)[:, keys:] if g else base[:, keys:]


def make_strip(base):
    heads, _, wide = base.shape
    return pl.pallas_call(
        strip_kernel,
        out_shape=jax.ShapeDtypeStruct((heads, KEYS, wide - KEYS), F32),
        compiler_params=pltpu.CompilerParams(vmem_limit_bytes=58 * MEGA),
        cost_estimate=cost(3),
    )(base)


def head_lanes(shape, h):
    lane = lax.broadcasted_iota(jnp.int32, shape, 1)
    return (lane >= 64 * h) & (lane < 64 * h + 64), lane == ((64 * h + 64) % 128)


def masked_queries(q, h):
    mine, spare = head_lanes(q.shape, h)
    return jnp.where(mine, q, jnp.where(spare, 1.0, 0.0)).astype(BF)


def masked_keys(k, h, first, length):
    mine, spare = head_lanes(k.shape, h)
    beyond = first + lax.broadcasted_iota(jnp.int32, k.shape, 0) >= length
    return jnp.where(mine, k, jnp.where(spare & beyond, NEG, 0.0)).astype(BF)


def block_of(index, size):
    return pl.ds(pl.multiple_of(index * size, 128), size)


def loop(first, last, step):
    def turn(index, carried):
        step(index)
        return carried

    lax.fori_loop(first, last, turn, 0)


def attend_kernel(len_ref, x_ref, bias_ref, o_ref, lse_ref, kh, vt, qh, acc, ot, strip_ref, sem, *, nh):
    parts, rows = x_ref.shape[0], x_ref.shape[3]
    total = parts * rows
    length = len_ref[pl.program_id(0)]
    bias = pltpu.make_async_copy(bias_ref, strip_ref, sem.at[0])
    bias.start()

    def prepare(t):
        at = block_of(t, rows)
        q = x_ref[t, 0, 0].astype(F32) * 0.125
        k = x_ref[t, 1, 0].astype(F32)
        v = x_ref[t, 2, 0].astype(F32).T.astype(BF)
        for h in range(nh):
            qh[h, at, :] = masked_queries(q, h)
            kh[h, at, :] = masked_keys(k, h, t * rows, length)
            vt[h, 0:64, at] = v[64 * h : 64 * h + 64]
            ones = lax.broadcasted_iota(jnp.int32, (16, rows), 0) == 0
            vt[h, 64:80, at] = jnp.where(ones, 1.0, 0.0).astype(BF)

    loop(0, parts, prepare)
    bias.wait()

    def queries(qb):
        at = block_of(qb, QUERIES)
        for h in range(nh):
            acc[h] = jnp.zeros((80, QUERIES), F32)

        def keys(kb, peaks):
            there = block_of(kb, QUERIES)
            after = []
            for h in range(nh):
                scores = []
                for half in range(QUERIES // KEYS):
                    first = kb * QUERIES + half * KEYS
                    off = pl.ds(pl.multiple_of(KEYS + qb * QUERIES - first, 128), QUERIES)
                    k = kh[h, pl.ds(pl.multiple_of(first, 128), KEYS), :]
                    scores.append(nt(k, qh[h, at, :]) + strip_ref[h, :, off])
                peak = peaks[h]
                for s in scores:
                    peak = jnp.maximum(peak, jnp.max(s, axis=0, keepdims=True))
                p = jnp.concatenate([jnp.exp(s - peak).astype(BF) for s in scores], axis=0)
                acc[h] = acc[h] * jnp.exp(peaks[h] - peak) + nn(vt[h, :, there], p)
                after.append(peak)
            return tuple(after)

        last = jnp.minimum(qb + 1, (length + QUERIES - 1) // QUERIES)
        peaks = lax.fori_loop(
            0, last, keys, tuple(jnp.full((1, QUERIES), NEG, F32) for _ in range(nh))
        )
        for h in range(nh):
            sums = acc[h, 64:65, :]
            lse_ref[0, h, :, at] = peaks[h] + jnp.log(sums)
            ot[64 * h : 64 * h + 64, at] = acc[h, 0:64, :] / sums
        if nh == 1:
            ot[64:128, at] = jnp.zeros((64, QUERIES), F32)

    loop(0, total // QUERIES, queries)

    def give(t):
        o_ref[t, 0] = ot[:, block_of(t, rows)].T.astype(BF)

    loop(0, parts, give)


def attn_fwd(lengths, x, strip, nh):
    parts, _, recs, rows, wide = x.shape
    total = parts * rows
    return pl.pallas_call(
        functools.partial(attend_kernel, nh=nh),
        grid_spec=pltpu.PrefetchScalarGridSpec(
            num_scalar_prefetch=1,
            grid=(recs,),
            in_specs=[
                pl.BlockSpec((parts, 3, 1, rows, wide), lambda r, l: (0, 0, r, 0, 0)), pl.BlockSpec(memory_space=pl.ANY),
            ],
            out_specs=[
                pl.BlockSpec((parts, 1, rows, wide), lambda r, l: (0, r, 0, 0)),
                pl.BlockSpec((1, nh, 1, total), lambda r, l: (r, 0, 0, 0)),
            ],
            scratch_shapes=[
                pltpu.VMEM((nh, total, wide), BF), pltpu.VMEM((nh, 80, total), BF),
                pltpu.VMEM((nh, total, wide), BF), pltpu.VMEM((nh, 80, QUERIES), F32),
                pltpu.VMEM((wide, total), F32), pltpu.VMEM(strip.shape, F32), pltpu.SemaphoreType.DMA((1,)),
            ],
        ),
        out_shape=[
            jax.ShapeDtypeStruct((parts, recs, rows, wide), BF),
            jax.ShapeDtypeStruct((recs, nh, 1, total), F32),
        ],
        compiler_params=pltpu.CompilerParams(vmem_limit_bytes=58 * MEGA),
        cost_estimate=cost(11),
    )(lengths, x, strip)


def attend_back_kernel(
    len_ref, x_ref, do_ref, o_ref, lse_ref, bias_ref, dx_ref, db_ref,
    kh, vh, qh, qs, dos, kt, dqt, delta, dk, dv, dks, dvs, dbs, strip_ref, sem, *, nh,
):
    parts, rows = x_ref.shape[0], x_ref.shape[3]
    total = parts * rows
    length = len_ref[pl.program_id(0)]
    blocks = (length + KEYS - 1) // KEYS
    bias = pltpu.make_async_copy(bias_ref, strip_ref, sem.at[0])
    bias.start()

    @pl.when(pl.program_id(0) == 0)
    def _():
        dbs[...] = jnp.zeros_like(dbs)

    dqt[...] = jnp.zeros_like(dqt)

    def prepare(t):
        at = block_of(t, rows)
        q = x_ref[t, 0, 0].astype(F32) * 0.125
        k = x_ref[t, 1, 0].astype(F32)
        v = x_ref[t, 2, 0].astype(F32)
        do = do_ref[t, 0]
        qs[at, :] = q.astype(BF)
        dos[at, :] = do
        kt[:, at] = k.T.astype(BF)
        product = (do.astype(F32) * o_ref[t, 0].astype(F32)).T
        for h in range(nh):
            qh[h, at, :] = masked_queries(q, h)
            kh[h, at, :] = masked_keys(k, h, t * rows, length)
            vh[h, at, :] = jnp.where(head_lanes(v.shape, h)[0], v, 0.0).astype(BF)
            delta[h, :, at] = jnp.sum(product[64 * h : 64 * h + 64], axis=0, keepdims=True)

    loop(0, parts, prepare)
    bias.wait()

    def keys(kb):
        there = block_of(kb, KEYS)
        dk[...] = jnp.zeros_like(dk)
        dv[...] = jnp.zeros_like(dv)

        def queries(qb):
            at = block_of(qb, QUERIES)
            off = pl.ds(pl.multiple_of(KEYS + qb * QUERIES - kb * KEYS, 128), QUERIES)
            for h in range(nh):
                s = nt(kh[h, there, :], qh[h, at, :]) + strip_ref[h, :, off]
                p = jnp.exp(s - lse_ref[0, h, :, at])
                ds = p * (nt(vh[h, there, :], dos[at, :]) - delta[h, :, at])
                low = ds.astype(BF)
                dv[h] += nn(p.astype(BF), dos[at, :])
                dk[h] += nn(low, qs[at, :])
                dqt[64 * h : 64 * h + 64, at] += nn(kt[64 * h : 64 * h + 64, there], low)
                dbs[h, :, off] += ds

        loop(kb * KEYS // QUERIES, total // QUERIES, queries)
        first, _ = head_lanes((KEYS, 128), 0)
        dks[there, :] = (jnp.where(first, dk[0], dk[1]) if nh == 2 else dk[0]).astype(BF)
        dvs[there, :] = (jnp.where(first, dv[0], dv[1]) if nh == 2 else dv[0]).astype(BF)

    loop(0, blocks, keys)

    def nothing(kb):
        dks[block_of(kb, KEYS), :] = jnp.zeros((KEYS, 128), BF)
        dvs[block_of(kb, KEYS), :] = jnp.zeros((KEYS, 128), BF)

    loop(blocks, total // KEYS, nothing)

    def give(t):
        at = block_of(t, rows)
        dx_ref[t, 0, 0] = (dqt[:, at] * 0.125).T.astype(BF)
        dx_ref[t, 1, 0] = dks[at, :]
        dx_ref[t, 2, 0] = dvs[at, :]

    loop(0, parts, give)

    @pl.when(pl.program_id(0) == pl.num_programs(0) - 1)
    def _():
        wide = dbs.shape[2]
        for h in range(nh):
            sums = dbs[h, 0:8, :]
            for g in range(1, KEYS // 8):
                sums = sums + pltpu.roll(dbs[h, 8 * g : 8 * g + 8, :], wide - 8 * g, 1)
            db_ref[h] = sums


def attn_bwd(lengths, x, do, o, lse, strip, nh):
    parts, _, recs, rows, wide = x.shape
    total = parts * rows
    several = pltpu.VMEM((nh, total, wide), BF)
    single = pltpu.VMEM((total, wide), BF)
    part = pltpu.VMEM((nh, KEYS, wide), F32)
    return pl.pallas_call(
        functools.partial(attend_back_kernel, nh=nh),
        grid_spec=pltpu.PrefetchScalarGridSpec(
            num_scalar_prefetch=1,
            grid=(recs,),
            in_specs=[
                pl.BlockSpec((parts, 3, 1, rows, wide), lambda r, l: (0, 0, r, 0, 0)),
                pl.BlockSpec((parts, 1, rows, wide), lambda r, l: (0, r, 0, 0)),
                pl.BlockSpec((parts, 1, rows, wide), lambda r, l: (0, r, 0, 0)),
                pl.BlockSpec((1, nh, 1, total), lambda r, l: (r, 0, 0, 0)),
                pl.BlockSpec(memory_space=pl.ANY),
            ],
            out_specs=[
                pl.BlockSpec((parts, 3, 1, rows, wide), lambda r, l: (0, 0, r, 0, 0)),
                pl.BlockSpec((nh, 8, strip.shape[2]), lambda r, l: (0, 0, 0)),
            ],
            scratch_shapes=[
                several, several, several, single, single, pltpu.VMEM((wide, total), BF),
                pltpu.VMEM((wide, total), F32), pltpu.VMEM((nh, 1, total), F32), part, part, single, single,
                pltpu.VMEM(strip.shape, F32), pltpu.VMEM(strip.shape, F32), pltpu.SemaphoreType.DMA((1,)),
            ],
        ),
        out_shape=[
            jax.ShapeDtypeStruct((parts, 3, recs, rows, wide), BF),
            jax.ShapeDtypeStruct((nh, 8, strip.shape[2]), F32),
        ],
        compiler_params=pltpu.CompilerParams(vmem_limit_bytes=58 * MEGA),
        cost_estimate=cost(15),
    )(lengths, x, do, o, lse, strip)


def tn(a, b):
    return lax.dot_general(a, b, (((0,), (0,)), ((), ())), preferred_element_type=F32)


def sigmoid(v):
    return 0.5 * jnp.tanh(0.5 * v) + 0.5


LINES = {
    "early_gain": 0, "early_shift": 1, "attend_gain": 2, "attend_shift": 3, "convolve_gain": 4, "convolve_shift": 5,
    "late_gain": 6, "late_shift": 7, "final_gain": 8, "final_shift": 9, "inner_gain": 10,
}


def row(ref, name):
    place = LINES[name]
    return ref[place : place + 1, :]


def broad_row(ref, name, width):
    blocks = width // 512
    place = LINES["inner_gain"] + (blocks if name == "inner_shift" else 0)
    return jnp.concatenate([ref[place + c : place + c + 1, :] for c in range(blocks)], axis=1)


def part_of(index, size=512):
    return pl.ds(pl.multiple_of(index * size, 128), size)


def repeat(count, step):
    def turn(index, carried):
        step(index)
        return carried

    lax.fori_loop(0, count, turn, 0)


def mover(sems):
    spent = []

    def move(source, target):
        copy = pltpu.make_async_copy(source, target, sems.at[len(spent)])
        spent.append(copy)
        copy.start()
        return copy

    return move


def pieces(width):
    return [slice(first, first + 512) for first in range(0, width, 512)]


def settle(copies):
    for copy in copies:
        copy.wait()


class Lane:
    def __init__(self, sems, first, parts, make):
        self.sems, self.first, self.parts, self.make = sems, first, parts, make
        self.each = len(make(0))

    def copies(self, part):
        place = self.first + part * self.each
        return [
            pltpu.make_async_copy(source, target, self.sems.at[place + k])
            for k, (source, target) in enumerate(self.make(part))
        ]

    def start(self, part=0):
        for copy in self.copies(part):
            copy.start()

    def wait(self, part=0):
        for copy in self.copies(part):
            copy.wait()

    def start_all(self):
        for part in range(self.parts):
            self.start(part)

    def wait_all(self):
        repeat(self.parts, self.wait)


def lanes(sems):
    spent = [0]

    def lane(parts, make):
        made = Lane(sems, spent[0], parts, make)
        spent[0] += parts * made.each
        return made

    return lane


def one(*pairs):
    return 1, lambda part: list(pairs)


def feed(h, wu, wd, up, down, keep):
    y = None
    for f in range(wu.shape[1] // 512):
        at = slice(512 * f, 512 * f + 512)
        up(f)
        z = nn(h, wu[:, at])
        sig = sigmoid(z)
        a = (z * sig).astype(BF)
        keep(f, at, a, (sig * (1.0 + z * (1.0 - sig))).astype(BF))
        down(f)
        part = nn(a, wd[at, :])
        y = part if y is None else y + part
    return y


def feed_back(dy, wu, wd, up, down, slope, keep):
    dh = None
    for f in range(wu.shape[1] // 512):
        at = slice(512 * f, 512 * f + 512)
        down(f)
        dz = (nt(dy, wd[at, :]) * slope(f, at).astype(F32)).astype(BF)
        keep(f, at, dz)
        up(f)
        part = nt(dz, wu[:, at])
        dh = part if dh is None else dh + part
    return dh


def over_rows(rows, step):
    step(slice(0, rows))


def over_tiles(rows, step):
    def tile(t):
        step(part_of(t, 128))

    repeat(rows // 128, tile)


def share_columns(held, place, left, right, ready, send):
    height = left.shape[1] // (held.shape[0] * held.shape[1])

    def step(f):
        ready(f)
        block = tn(left[...], right[:, part_of(f)]).astype(BF)
        there = pl.ds(pl.multiple_of(place + f * height, 16), height)
        held[:, :, there, :] = block.reshape(held.shape[:2] + (height, 512))
        send(f, pl.ds(0, held.shape[0]), there)

    repeat(right.shape[1] // 512, step)


def share_rows(held, place, left, right, ready, send):
    height = left.shape[1] // (held.shape[0] * held.shape[1])
    each = 512 // (held.shape[1] * height)

    def step(f):
        ready(f)
        block = tn(left[:, part_of(f)], right[...]).astype(BF)
        who, there = pl.ds(each * f, each), pl.ds(place, height)
        held[who, :, there, :] = block.reshape(each, held.shape[1], height, 512)
        send(f, who, there)

    repeat(left.shape[1] // 512, step)


def columns_of(held, place, left, right):
    height = left.shape[1] // (held.shape[0] * held.shape[1])
    return lambda f: (pl.ds(0, held.shape[0]), pl.ds(pl.multiple_of(place + f * height, 16), height))


def rows_of(held, place, left, right):
    height = left.shape[1] // (held.shape[0] * held.shape[1])
    each = 512 // (held.shape[1] * height)
    return lambda f: (pl.ds(each * f, each), pl.ds(place, height))


def spread_columns(send, held, place, left, right, ready):
    count = held.shape[0] * held.shape[1]
    height = left.shape[1] // count
    for f, at in enumerate(pieces(right.shape[1])):
        ready(f)
        there = slice(place, place + height)
        block = tn(left[...], right[:, at]).astype(BF)
        held[:, :, there, :] = block.reshape(held.shape[:2] + (height, 512))
        send(slice(0, held.shape[0]), there)
        place += height
    return place


def spread_rows(send, held, place, left, right, ready):
    height = left.shape[1] // (held.shape[0] * held.shape[1])
    each = 512 // (held.shape[1] * height)
    for f, at in enumerate(pieces(left.shape[1])):
        ready(f)
        who, there = slice(each * f, each * f + each), slice(place, place + height)
        block = tn(left[:, at], right[...]).astype(BF)
        held[who, :, there, :] = block.reshape(each, held.shape[1], height, 512)
        send(who, there)
    return place + height


def norm_parts(v):
    center = v - jnp.mean(v, axis=-1, keepdims=True)
    inverse = lax.rsqrt(jnp.mean(center * center, axis=-1, keepdims=True) + EPSILON)
    return center * inverse, inverse


def norm_pull(n, inverse, gain, grad):
    dn = grad * gain
    return (
        dn - jnp.mean(dn, axis=-1, keepdims=True) - n * jnp.mean(dn * n, axis=-1, keepdims=True)
    ) * inverse


def add_rows(ref, place, values):
    total = jnp.sum(values, axis=0, keepdims=True)
    for c in range(values.shape[1] // 512):
        ref[place + c : place + c + 1, :] += total[:, 512 * c : 512 * c + 512]


def start_small(ref):
    @pl.when(pl.program_id(0) == 0)
    def _():
        ref[...] = jnp.zeros_like(ref)


def put_heads(write, value, nh):
    for pair in range(value.shape[1] // 128):
        part = value[:, 128 * pair : 128 * pair + 128]
        if nh == 2:
            write(pair, part.astype(BF))
        else:
            low = lax.broadcasted_iota(jnp.int32, part.shape, 1) < 64
            write(2 * pair, jnp.where(low, part, 0.0).astype(BF))
            write(2 * pair + 1, jnp.where(low, pltpu.roll(part, 64, 1), 0.0).astype(BF))


def take_heads(read, units, nh):
    if nh == 2:
        return jnp.concatenate([read(u) for u in range(units)], axis=1)
    pairs = [
        (read(2 * u).astype(F32) + pltpu.roll(read(2 * u + 1).astype(F32), 64, 1)).astype(BF)
        for u in range(units // 2)
    ]
    return jnp.concatenate(pairs, axis=1)


def lines_kernel(*refs):
    out = refs[-1]
    out[...] = jnp.zeros_like(out)
    place = 0
    for ref in refs[:-1]:
        for c in range(ref.shape[0] // 512):
            out[place : place + 1, :] = ref[512 * c : 512 * c + 512].astype(F32).reshape(1, 512)
            place += 1


def open_kernel(
    x_ref, g1_ref, s1_ref, g2_ref, s2_ref, wu_ref, wd_ref, wi_ref, x1_ref, h1_ref, a_ref, sp_ref, h2_ref, u_ref,
    x, g1, s1, g2, s2, wu, wd, wi, x1, h1, a1, sp, h2, u, total, sems, *, nh, first, recs,
):
    turn = pl.program_id(0)
    rec = first + turn
    rows = x.shape[0]
    parts = wu.shape[1] // 512
    lane = lanes(sems)
    ahead = lane(*one((x_ref.at[rec], x), (g1_ref, g1), (s1_ref, s1), (g2_ref, g2), (s2_ref, s2)))
    line = lambda ref: ref[...].astype(F32).reshape(1, 512)
    up = lane(parts, lambda f: [(wu_ref.at[:, part_of(f)], wu.at[:, part_of(f)])])
    down = lane(parts, lambda f: [(wd_ref.at[part_of(f), :], wd.at[part_of(f), :])])
    wide = lane(3, lambda f: [(wi_ref.at[:, part_of(f)], wi.at[:, part_of(f)])])
    out_h1 = lane(*one((h1, h1_ref.at[rec])))
    out_hidden = lane(
        parts,
        lambda f: [
            (a1.at[:, part_of(f)], a_ref.at[rec, :, part_of(f)]),
            (sp.at[:, part_of(f)], sp_ref.at[rec, :, part_of(f)]),
        ],
    )
    out_x1 = lane(*one((x1, x1_ref.at[rec]), (h2, h2_ref.at[rec])))
    out_u = lane(3, lambda f: [(u.at[f], u_ref.at[:, turn // recs, f, turn % recs])])
    ahead.start()
    for f in range(parts):
        up.start(f)
        down.start(f)
    wide.start_all()
    ahead.wait()

    def normal(at):
        n, _ = norm_parts(x[at, :].astype(F32))
        h1[at, :] = (n * line(g1) + line(s1)).astype(BF)

    over_rows(rows, normal)
    out_h1.start()

    def keep(f, at, a, slope):
        a1[:, at] = a
        sp[:, at] = slope
        out_hidden.start(f)

    total[...] = feed(h1[...], wu, wd, up.wait, down.wait, keep)

    def second(at):
        value = x[at, :].astype(F32) + 0.5 * total[at, :]
        x1[at, :] = value
        n, _ = norm_parts(value)
        h2[at, :] = (n * line(g2) + line(s2)).astype(BF)

    over_rows(rows, second)
    out_x1.start()

    def project(kind):
        wide.wait(kind)

        def write(unit, part):
            u[kind, unit] = part

        put_heads(write, nn(h2[...], wi[:, part_of(kind)]), nh)
        out_u.start(kind)

    repeat(3, project)
    for out in (out_h1, out_hidden, out_x1, out_u):
        out.wait_all()


def gate_kernel(
    len_ref, o_ref, x1_ref, lines_ref, wo_ref, wc_ref, att_ref, x2_ref, h3_ref, g_ref, ga_ref, gb_ref,
    o, x1, lines, wo, wc, att, x2, h3, g, ga, gb, sems, *, nh, first, recs,
):
    turn = pl.program_id(0)
    rec = first + turn
    rows = x1.shape[0]
    channels = g.shape[1]
    parts = channels // 512
    lane = lanes(sems)
    ahead = lane(*one((o_ref.at[:, turn // recs, turn % recs], o), (wo_ref, wo)))
    then = lane(*one((x1_ref.at[rec], x1), (lines_ref, lines)))
    wide = lane(
        parts,
        lambda f: [
            (wc_ref.at[:, part_of(f)], wc.at[:, part_of(f)]),
            (wc_ref.at[:, part_of(f + parts)], wc.at[:, part_of(f + parts)]),
        ],
    )
    out_att = lane(*one((att, att_ref.at[rec])))
    out_x2 = lane(*one((x2, x2_ref.at[rec]), (h3, h3_ref.at[rec])))
    out_g = lane(
        parts,
        lambda f: [
            (held.at[:, part_of(f)], out.at[rec, :, part_of(f)])
            for held, out in ((g, g_ref), (ga, ga_ref), (gb, gb_ref))
        ],
    )
    ahead.start()
    then.start()
    wide.start_all()
    ahead.wait()
    att[...] = take_heads(lambda unit: o[unit], o.shape[0], nh)
    out_att.start()
    then.wait()
    x2[...] = x1[...] + nn(att[...], wo[...])

    def normal(at):
        n, _ = norm_parts(x2[at, :])
        h3[at, :] = (n * row(lines, "convolve_gain") + row(lines, "convolve_shift")).astype(BF)

    over_tiles(rows, normal)
    out_x2.start()
    limit = len_ref[rec]
    place = lax.broadcasted_iota(jnp.int32, (rows, 1), 0)
    valid = jnp.where(place < limit, 1.0, 0.0)

    def step(f):
        at = part_of(f)
        wide.wait(f)
        lin = nn(h3[...], wc[:, at])
        sig = sigmoid(nn(h3[...], wc[:, part_of(f + parts)]))
        sv = sig * valid
        value = lin * sv
        g[:, at] = value.astype(BF)
        ga[:, at] = sv.astype(BF)
        gb[:, at] = (value * (1.0 - sig)).astype(BF)
        out_g.start(f)

    repeat(parts, step)
    for out in (out_att, out_x2, out_g):
        out.wait_all()


def middle_kernel(
    g_ref, halo_ref, x2_ref, cot_ref, dep, lines, wco, wu, wd,
    out_ref, dx3_ref, dg_ref, dhalo_ref, small_ref, ddep_ref, pack_ref,
    gx, cs, inv3, dcx, sp3, h4s, a4s, sp4, dz4s, dy4s, a3s, dy3s, tapped, dws, wcov, wuv, wdv, held, sems, out_sems,
):
    rec = pl.program_id(0)
    rows = x2_ref.shape[1]
    channels = g_ref.shape[2]
    strips = channels // 128
    taps = dep.shape[0] - 1
    start_small(small_ref)
    start_small(tapped)
    first = pl.multiple_of(rec * rows, 128)
    mine = pl.ds(first, rows)
    tile = 96
    fetched = [(wco, wcov)]
    for at in pieces(wu.shape[1]):
        fetched.append((wu.at[:, at], wuv.at[:, at]))
        fetched.append((wd.at[at, :], wdv.at[at, :]))
    fetched = [pltpu.make_async_copy(*pair, sems.at[k]) for k, pair in enumerate(fetched)]

    @pl.when(rec == 0)
    def _():
        for copy in fetched:
            copy.start()

    def ready(k):
        @pl.when(rec == 0)
        def _():
            fetched[k].wait()


    def conv(c):
        at = part_of(c, 128)
        gx[c, 0:16, :] = halo_ref[0, :, at].astype(F32)
        gx[c, 16:, :] = g_ref[0, :, at].astype(F32)
        for top in range(0, rows, tile):
            sums = dep[0:1, at] * gx[c, top + 2 : top + 2 + tile, :]
            for r in range(1, taps):
                sums = sums + dep[r : r + 1, at] * gx[c, top + 2 + r : top + 2 + r + tile, :]
            cs[top : top + tile, at] = sums

    repeat(strips, conv)

    def inner(t):
        there = pl.ds(pl.multiple_of(t * 64, 64), 64)
        n, inverse = norm_parts(cs[there, :])
        cs[there, :] = n
        inv3[there, :] = inverse
        w = n * broad_row(lines, "inner_gain", channels) + broad_row(lines, "inner_shift", channels)
        sig = sigmoid(w)
        a3s[pl.ds(first + pl.multiple_of(t * 64, 64), 64), :] = (w * sig).astype(BF)
        sp3[there, :] = (sig * (1.0 + w * (1.0 - sig))).astype(BF)

    repeat(rows // 64, inner)
    ready(0)
    x3 = x2_ref[0] + nn(a3s[mine, :], wcov[...])
    n4, inv4 = norm_parts(x3)
    h4 = (n4 * row(lines, "late_gain") + row(lines, "late_shift")).astype(BF)
    h4s[mine, :] = h4

    def keep(f, at, a, slope):
        a4s[mine, at] = a
        sp4[:, at] = slope

    y = feed(h4, wuv, wdv, lambda f: ready(1 + 2 * f), lambda f: ready(2 + 2 * f), keep)
    x4 = x3 + 0.5 * y
    n5, inv5 = norm_parts(x4)
    out_ref[0] = (n5 * row(lines, "final_gain") + row(lines, "final_shift")).astype(BF)
    cot = cot_ref[0].astype(F32)
    add_rows(small_ref, 8, cot * n5)
    add_rows(small_ref, 9, cot)
    dx4 = norm_pull(n5, inv5, row(lines, "final_gain"), cot)
    dx3_ref[0] = dx4
    dy4 = (0.5 * dx4).astype(BF)
    dy4s[mine, :] = dy4

    def keep_back(f, at, dz):
        dz4s[mine, at] = dz

    done = lambda f: None
    dh = feed_back(dy4, wuv, wdv, done, done, lambda f, at: sp4[:, at], keep_back)
    add_rows(small_ref, 6, dh * n4)
    add_rows(small_ref, 7, dh)
    dx3 = dx3_ref[0] + norm_pull(n4, inv4, row(lines, "late_gain"), dh)
    dx3_ref[0] = dx3
    dy3s[mine, :] = dx3.astype(BF)

    def pull(f):
        at = part_of(f)
        dws[:, at] = nt(dy3s[mine, :], wcov[at, :]) * sp3[:, at].astype(F32)

    repeat(channels // 512, pull)

    def inner_back(t):
        there = pl.ds(pl.multiple_of(t * 64, 64), 64)
        dw = dws[there, :]
        n = cs[there, :]
        add_rows(small_ref, 2, dw * n)
        add_rows(small_ref, 4, dw)
        cs[there, :] = norm_pull(n, inv3[there, :], broad_row(lines, "inner_gain", channels), dw)

    repeat(rows // 64, inner_back)

    def conv_back(c):
        at = part_of(c, 128)
        dcx[0:16, :] = jnp.zeros((16, 128), F32)
        dcx[16 : 16 + rows, :] = cs[:, at]
        dcx[16 + rows :, :] = jnp.zeros((16, 128), F32)
        sums = [jnp.zeros((8, 128), F32)] * taps
        for top in range(0, rows, tile):
            dc = dcx[16 + top : 16 + top + tile, :]
            for r in range(taps):
                term = dc * gx[c, top + 2 + r : top + 2 + r + tile, :]
                sums[r] = sums[r] + jnp.sum(term.reshape(tile // 8, 8, 128), axis=0)
        for r in range(taps):
            tapped[c, 8 * r : 8 * r + 8, :] += sums[r]
        for top in range(0, rows + 16, tile):
            size = min(tile, rows + 16 - top)
            sums = dep[0:1, at] * dcx[top + 14 : top + 14 + size, :]
            for r in range(1, taps):
                sums = sums + dep[r : r + 1, at] * dcx[top + 14 - r : top + 14 - r + size, :]
            if top == 0:
                dhalo_ref[0, :, at] = sums[0:16].astype(BF)
                dg_ref[0, 0 : size - 16, at] = sums[16:].astype(BF)
            else:
                dg_ref[0, top - 16 : top - 16 + size, at] = sums.astype(BF)

    repeat(strips, conv_back)

    @pl.when(rec == pl.num_programs(0) - 1)
    def _():
        def depth(c):
            for r in range(taps):
                ddep_ref[r : r + 1, part_of(c, 128)] = jnp.sum(
                    tapped[c, 8 * r : 8 * r + 8, :], axis=0, keepdims=True
                )

        ddep_ref[taps:, :] = jnp.zeros((1, channels), F32)
        repeat(strips, depth)
        move = mover(out_sems)
        sent = []

        def send(who, there):
            sent.append(move(held.at[who, :, there], pack_ref.at[who, :, there]))

        place = spread_columns(send, held, 0, h4s, dz4s, done)
        place = spread_rows(send, held, place, a4s, dy4s, done)
        spread_rows(send, held, place, a3s, dy3s, done)
        settle(sent)


def share(kind, lane, held, outs, core, place, left, right, ready):
    columns = kind == "columns"
    parts = (right if columns else left).shape[1] // 512
    where = (columns_of if columns else rows_of)(held, place, left, right)

    def make(f):
        who, there = where(f)
        if core is None:
            return [(held.at[who, :, there], outs[0].at[who, :, there])]
        return [(held.at[who, c, there], out.at[who, there]) for c, out in zip((core, 1 - core), outs)]

    out = lane(parts, make)
    (share_columns if columns else share_rows)(
        held, place, left, right, ready, lambda f, who, there: out.start(f)
    )
    height = left.shape[1] // (held.shape[0] * held.shape[1])
    return place + height * (parts if columns else 1), out


def ungate_kernel(
    dg_ref, back_ref, ga_ref, gb_ref, dx3_ref, x2_ref, lines_ref, wc_ref, wo_ref,
    dx2_ref, du_ref, dy2_ref, do_ref, small_ref,
    dg, back, lines, wc, wo, ga, gb, dx3, x2, dx2, du, dy2, do, small, dgx, total, sems, *, nh, first, recs,
):
    turn = pl.program_id(0)
    rec = first + turn
    rows = x2.shape[0]
    channels = ga.shape[1]
    parts = channels // 512
    lane = lanes(sems)
    ahead = lane(*one((back_ref.at[rec], back)))
    fetch = lane(
        parts,
        lambda f: [
            (dg_ref.at[rec, :, part_of(f)], dg.at[:, part_of(f)]),
            (ga_ref.at[rec, :, part_of(f)], ga.at[:, part_of(f)]),
            (gb_ref.at[rec, :, part_of(f)], gb.at[:, part_of(f)]),
            (wc_ref.at[:, part_of(f)], wc.at[:, part_of(f)]),
            (wc_ref.at[:, part_of(f + parts)], wc.at[:, part_of(f + parts)]),
        ],
    )
    then = lane(*one((x2_ref.at[rec], x2), (dx3_ref.at[rec], dx3), (lines_ref, lines), (wo_ref, wo)))
    out_du = lane(
        parts,
        lambda f: [
            (du.at[:, part_of(f)], du_ref.at[rec, :, part_of(f)]),
            (du.at[:, part_of(f + parts)], du_ref.at[rec, :, part_of(f + parts)]),
        ],
    )
    out_dx2 = lane(*one((dx2, dx2_ref.at[rec]), (dy2, dy2_ref.at[rec]), (small, small_ref)))
    out_do = lane(*one((do, do_ref.at[:, turn // recs, turn % recs])))
    ahead.start()
    fetch.start_all()
    then.start()
    start_small(small)
    total[...] = jnp.zeros_like(total)
    ahead.wait()

    def step(f):
        at = part_of(f)
        up = part_of(f + parts)
        fetch.wait(f)
        dgx[...] = dg[:, at].astype(F32)
        dgx[rows - 16 :, :] += back[:, at].astype(F32)
        value = dgx[...]
        lin = (value * ga[:, at].astype(F32)).astype(BF)
        gate = (value * gb[:, at].astype(F32)).astype(BF)
        du[:, at] = lin
        du[:, up] = gate
        out_du.start(f)
        total[...] += nt(lin, wc[:, at]) + nt(gate, wc[:, up])

    repeat(parts, step)
    then.wait()

    def pull(at):
        n, inverse = norm_parts(x2[at, :])
        dh = total[at, :]
        add_rows(small, 0, dh * n)
        add_rows(small, 1, dh)
        value = dx3[at, :] + norm_pull(n, inverse, row(lines, "convolve_gain"), dh)
        dx2[at, :] = value
        dy2[at, :] = value.astype(BF)

    over_rows(rows, pull)
    out_dx2.start()

    def write(unit, part):
        do[unit] = part

    put_heads(write, nt(dy2[...], wo[...]), nh)
    out_do.start()
    for out in (out_du, out_dx2, out_do):
        out.wait_all()


def project_kernel(
    u_ref, x1_ref, dx2_ref, lines_ref, wi_ref, dx1_ref, dy_ref, dp_ref, small_ref,
    lines, wi, u, x1, dx2, dx1, dy, dp, small, total, sems, *, nh, first, recs,
):
    turn = pl.program_id(0)
    rec = first + turn
    rows = x1.shape[0]
    lane = lanes(sems)
    fetch = lane(
        3,
        lambda f: [
            (u_ref.at[:, turn // recs, f, turn % recs], u.at[f]), (wi_ref.at[:, part_of(f)], wi.at[:, part_of(f)]),
        ],
    )
    then = lane(*one((x1_ref.at[rec], x1), (dx2_ref.at[rec], dx2), (lines_ref, lines)))
    out_dp = lane(3, lambda f: [(dp.at[:, part_of(f)], dp_ref.at[rec, :, part_of(f)])])
    out_dx1 = lane(*one((dx1, dx1_ref.at[rec]), (dy, dy_ref.at[rec]), (small, small_ref)))
    fetch.start_all()
    then.start()
    start_small(small)
    total[...] = jnp.zeros_like(total)

    def step(kind):
        at = part_of(kind)
        fetch.wait(kind)
        value = take_heads(lambda unit: u[kind, unit], u.shape[1], nh)
        dp[:, at] = value
        out_dp.start(kind)
        total[...] += nt(value, wi[:, at])

    repeat(3, step)
    then.wait()

    def pull(at):
        n, inverse = norm_parts(x1[at, :])
        dh = total[at, :]
        add_rows(small, 0, dh * n)
        add_rows(small, 1, dh)
        value = dx2[at, :] + norm_pull(n, inverse, row(lines, "attend_gain"), dh)
        dx1[at, :] = value
        dy[at, :] = (0.5 * value).astype(BF)

    over_rows(rows, pull)
    out_dx1.start()
    for out in (out_dp, out_dx1):
        out.wait_all()


def close_kernel(
    dy_ref, dx1_ref, x_ref, sp_ref, lines_ref, wu_ref, wd_ref, out_ref, dz_ref, small_ref,
    dy, lines, wu, wd, sp, dx1, x, dz, out, small, total, sems, *, first,
):
    rec = first + pl.program_id(0)
    rows = x.shape[0]
    parts = wu.shape[1] // 512
    lane = lanes(sems)
    ahead = lane(*one((dy_ref.at[rec], dy)))
    down = lane(
        parts,
        lambda f: [
            (wd_ref.at[part_of(f), :], wd.at[part_of(f), :]), (sp_ref.at[rec, :, part_of(f)], sp.at[:, part_of(f)]),
        ],
    )
    up = lane(parts, lambda f: [(wu_ref.at[:, part_of(f)], wu.at[:, part_of(f)])])
    then = lane(*one((x_ref.at[rec], x), (dx1_ref.at[rec], dx1), (lines_ref, lines)))
    out_dz = lane(parts, lambda f: [(dz.at[:, part_of(f)], dz_ref.at[rec, :, part_of(f)])])
    out_dx = lane(*one((out, out_ref.at[rec]), (small, small_ref)))
    ahead.start()
    for f in range(parts):
        down.start(f)
        up.start(f)
    then.start()
    start_small(small)
    ahead.wait()

    def keep(f, at, value):
        dz[:, at] = value
        out_dz.start(f)

    total[...] = feed_back(dy[...], wu, wd, up.wait, down.wait, lambda f, at: sp[:, at], keep)
    then.wait()

    def pull(at):
        n, inverse = norm_parts(x[at, :].astype(F32))
        dh = total[at, :]
        add_rows(small, 0, dh * n)
        add_rows(small, 1, dh)
        out[at, :] = (dx1[at, :] + norm_pull(n, inverse, row(lines, "early_gain"), dh)).astype(BF)

    over_rows(rows, pull)
    out_dx.start()
    for lane_out in (out_dz, out_dx):
        lane_out.wait_all()


def share_kernel(core_ref, *refs, kinds, extra, apart):
    jobs = len(kinds)
    ins = refs[: 2 * jobs]
    more = refs[2 * jobs : 2 * jobs + extra]
    outs = refs[2 * jobs + extra : 2 * jobs + extra + 1 + apart]
    held = refs[2 * jobs + extra + 1 + apart :]
    packed, small, sems = held[2 * jobs :]
    core = core_ref[0] if apart else None
    lane = lanes(sems)
    plan = []
    for k, kind in enumerate(kinds):
        left, right = ins[2 * k : 2 * k + 2]
        left_held, right_held = held[2 * k : 2 * k + 2]
        if kind == "columns":
            first = lane(*one((left, left_held)))
            source, target = right, right_held
        else:
            first = lane(*one((right, right_held)))
            source, target = left, left_held
        parts = lane(
            source.shape[1] // 512,
            lambda f, source=source, target=target: [(source.at[:, part_of(f)], target.at[:, part_of(f)])],
        )
        first.start()
        parts.start_all()
        plan.append((left_held, right_held, first, parts))
    waits = []
    place = 0
    for kind, (left, right, first, parts) in zip(kinds, plan):
        first.wait()
        place, out = share(kind, lane, packed, outs, core, place, left, right, parts.wait)
        waits.append(out)
    if extra:
        small_shares(more, packed, small, place)
        there = pl.ds(place, packed.shape[2] - place)
        out = lane(
            *one(*[(packed.at[:, c, there], target.at[:, there]) for c, target in zip((core, 1 - core), outs)])
        )
        out.start()
        waits.append(out)
    for out in waits:
        out.wait_all()


def small_shares(refs, packed, small, place):
    small_mid, ddep, table = refs[:3]
    batches = (len(refs) - 3) // 3
    count = packed.shape[0] * packed.shape[1]
    small[...] = jnp.zeros_like(small)
    for k in range(3):
        for ref in refs[3 + k * batches : 3 + k * batches + batches]:
            small[2 * k : 2 * k + 2, :] += ref[0:2, :]
    small[6:10, :] = small_mid[6:10, :]
    narrow = 512 // count
    broad = ddep.shape[1] // count
    high = table.shape[0] // count
    packed[:, :, place:, :] = jnp.zeros(packed.shape[:2] + (packed.shape[2] - place, 512), BF)
    blocks = ddep.shape[1] // 512
    inner = [
        jnp.concatenate([small_mid[first + c : first + c + 1, :] for c in range(blocks)], axis=1)
        for first in (2, 4)
    ]
    inner = jnp.concatenate(inner, axis=0)
    for s in range(count):
        there = slice(place, place + 16)
        packed[s // 2, s % 2, there, 0:narrow] = small[:, narrow * s : narrow * s + narrow].astype(BF)
        packed[s // 2, s % 2, place : place + 2, 128 : 128 + broad] = inner[
            :, broad * s : broad * s + broad
        ].astype(BF)
        packed[s // 2, s % 2, there, 256 : 256 + broad] = ddep[:, broad * s : broad * s + broad].astype(BF)
        packed[s // 2, s % 2, place : place + high, 384 : 384 + table.shape[1]] = table[
            high * s : high * s + high, :
        ].astype(BF)


def finish_kernel(index_ref, *refs, parts):
    outs = refs[3 * parts : len(refs) - 3]
    sums, proj, last = refs[len(refs) - 3 :]
    for group, held in enumerate((sums, proj, last)):
        for k in range(parts):
            held[index_ref[0] ^ k] = refs[group * parts + k][...]
    (
        e_gain, e_shift, e_up, e_down, a_gain, a_shift, a_in, a_out, table, c_gain, c_shift, c_in, depth,
        i_gain, i_shift, c_out, l_gain, l_shift, l_up, l_down, f_gain, f_shift,
    ) = outs

    def reader(ref):
        def read(first, size):
            if len(ref.shape) == 2:
                return ref[first : first + size, :].astype(F32)
            height = ref.shape[1]
            pieces = []
            while size:
                piece, top = divmod(first, height)
                here = min(size, height - top)
                pieces.append(ref[piece].astype(F32)[top : top + here, :])
                first += here
                size -= here
            return pieces[0] if len(pieces) == 1 else jnp.concatenate(pieces, axis=0)

        return read

    def put(read, place, out):
        height = out.shape[0]
        for f in range(out.shape[1] // 512):
            out[:, 512 * f : 512 * f + 512] = read(place, height)
            place += height
        return place

    sums, proj, last = reader(sums), reader(proj), reader(last)
    put(sums, put(sums, put(sums, put(sums, put(sums, 0, l_up), l_down), c_out), c_in), a_out)
    put(proj, put(proj, 0, a_in), e_down)
    place = put(last, 0, e_up)
    small = last(place, 16)
    for line, out in enumerate(
        (e_gain, e_shift, a_gain, a_shift, c_gain, c_shift, l_gain, l_shift, f_gain, f_shift)
    ):
        out[...] = small[line : line + 1, 0 : out.shape[1]]
    i_gain[...] = small[0:1, 128 : 128 + i_gain.shape[1]]
    i_shift[...] = small[1:2, 128 : 128 + i_shift.shape[1]]
    depth[...] = small[0 : depth.shape[0], 256 : 256 + depth.shape[1]]
    table[...] = small[0 : table.shape[0], 384 : 384 + table.shape[1]]


def per_rec(array, first=0):
    shape = (1,) + array.shape[1:]
    tail = (0,) * (array.ndim - 1)
    return pl.BlockSpec(shape, lambda r, *_: (r + first,) + tail)


def whole(array):
    zeros = (0,) * array.ndim
    return pl.BlockSpec(array.shape, lambda r, *_: zeros, pipeline_mode=pl.Buffered(1))


def whole_out(array):
    zeros = (0,) * len(array.shape)
    return pl.BlockSpec(array.shape, lambda r, *_: zeros)


def per_unit(array, recs):
    units, rest = array.shape[0], array.shape[2:]
    if len(array.shape) == 6:
        return pl.BlockSpec(
            (units, 1, rest[0], 1) + rest[2:], lambda r, *_: (0, r // recs, 0, r % recs, 0, 0)
        )
    return pl.BlockSpec((units, 1, 1) + rest[1:], lambda r, *_: (0, r // recs, r % recs, 0, 0))


def far(array):
    return pl.BlockSpec(memory_space=pl.ANY)


def spot(shape, kind=F32):
    return jax.ShapeDtypeStruct(shape, kind)


def run(
    kernel, seqs, ins, in_specs, outs, out_specs, scratch=(), prefetch=(), after=(), into=(),
    micros=6,
):
    held = (*after, *into)
    plain = kernel
    place = len(prefetch) + len(ins)

    def kernel(*refs):
        plain(*refs[:place], *refs[place + len(held) :])

    return pl.pallas_call(
        kernel,
        grid_spec=pltpu.PrefetchScalarGridSpec(
            num_scalar_prefetch=len(prefetch),
            grid=(seqs,),
            in_specs=[*in_specs, *(pl.BlockSpec(memory_space=pl.ANY) for _ in held)],
            out_specs=out_specs,
            scratch_shapes=list(scratch),
        ),
        out_shape=outs,
        cost_estimate=cost(micros),
        input_output_aliases={place + len(after) + k: k for k in range(len(into))},
        compiler_params=pltpu.CompilerParams(vmem_limit_bytes=58 * MEGA),
    )(*prefetch, *ins, *held)


def unit_plan(seqs, heads):
    parts = lax.axis_size("tm")
    if parts <= heads:
        return heads // parts, seqs, 1
    return 1, seqs * heads // parts, parts // heads


def distance_hot(seq_total, bucket_count):
    limits = jnp.array(boundaries(seq_total), jnp.int32)
    places = jnp.arange(seq_total, dtype=jnp.int32)
    bucket = jnp.sum((places[:, None] >= limits[None, :]).astype(jnp.int32), axis=1)
    return (bucket[:, None] == jnp.arange(bucket_count, dtype=jnp.int32)[None, :]).astype(FLOAT)


def bias_strip(table, hot, nh, split):
    first = lax.axis_index("tm") // split * nh
    mine = lax.dynamic_slice_in_dim(table, first, nh, 1)
    per = jnp.dot(hot, mine, precision=HIGHEST).T
    pad = 2 * KEYS
    shifted = [
        jnp.pad(per, ((0, 0), (pad + s, 0)), constant_values=NEGATIVE)[:, : pad + hot.shape[0]]
        for s in range(8)
    ]
    return make_strip(jnp.stack(shifted, 1))


def table_grad(diagonals, hot, nh, split, heads):
    per = sum(jnp.pad(diagonals[:, s, KEYS + s :], ((0, 0), (0, s))) for s in range(8))
    mine = jnp.dot(hot.T, per.T, precision=HIGHEST)
    first = lax.axis_index("tm") // split * nh
    return lax.dynamic_update_slice_in_dim(
        jnp.zeros((hot.shape[1], heads), FLOAT), mine, first, 1
    )


def swap(values):
    return lax.all_to_all(values, "tm", 0, 0, tiled=True)


def body(
    frames, cotangent, lengths,
    early_gain, early_shift, early_up, early_down,
    attend_gain, attend_shift, attend_input, attend_output, distance_bias,
    convolve_gain, convolve_shift, convolve_input, depthwise, inner_gain, inner_shift, convolve_output,
    late_gain, late_shift, late_up, late_down, final_gain, final_shift,
):
    seqs, rows, width = frames.shape
    heads = distance_bias.shape[1]
    count = lax.axis_size("rows")
    parts = lax.axis_size("tm")
    hidden = early_up.shape[1]
    channels = convolve_output.shape[0]
    nh, recs, split = unit_plan(seqs, heads)
    units = heads // nh
    batches = seqs if split == 1 else 1
    here = seqs // batches
    recs = recs // batches
    tokens = seqs * rows
    vectors = (
        early_gain, early_shift, attend_gain, attend_shift, convolve_gain, convolve_shift,
        late_gain, late_shift, final_gain, final_shift, inner_gain, inner_shift,
    )
    lines = pl.pallas_call(lines_kernel, out_shape=spot((16, 512)))(*vectors)
    core = (lax.axis_index("rows") % 2).astype(jnp.int32)[None]
    merge = lambda v: v.reshape(tokens, -1)

    def wide(*kinds):
        return spot((units, split, *kinds, recs, rows, 128), BF)

    def held(columns, kind=BF):
        return pltpu.VMEM((rows, columns), kind)

    def like(array):
        return pltpu.VMEM(array.shape, array.dtype)

    def sems(size):
        return pltpu.SemaphoreType.DMA((size,))

    def shares(kinds, ins, height, extra=(), after=(), apart=True):
        shape = (count // 2, 2, height // 512 // count, 512)
        outs = (spot((shape[0],) + shape[2:], BF),) * 2 if apart else (spot(shape, BF),)
        return run(
            functools.partial(share_kernel, kinds=kinds, extra=len(extra), apart=apart), 1, (*ins, *extra),
            [far(v) for v in ins] + [whole(v) for v in extra], outs, [far(v) for v in outs],
            scratch=[like(v) for v in ins] + [pltpu.VMEM(shape, BF), pltpu.VMEM((16, 512), F32), sems(40)],
            after=after, prefetch=(core,),
        )

    def own(columns, kind=BF):
        return spot((seqs, rows, columns), kind)

    kept = ()
    sent = []
    for batch in range(batches):
        ins = (
            frames, early_gain, early_shift, attend_gain, attend_shift, early_up, early_down, attend_input,
        )
        outs = (own(width, F32), own(width), own(hidden), own(hidden), own(width), wide(3))
        *kept, qkv = run(
            functools.partial(open_kernel, nh=nh, first=batch * here, recs=recs), here, ins,
            [far(v) for v in ins], outs, [far(v) for v in outs],
            scratch=(
                held(width), like(early_gain), like(early_shift), like(attend_gain), like(attend_shift),
                like(early_up), like(early_down), like(attend_input), held(width, F32),
                held(width), held(hidden), held(hidden), held(width), pltpu.VMEM((3, units, rows, 128), BF),
                held(width, F32), sems(40),
            ),
            into=kept,
        )
        sent.append(swap(qkv.reshape(parts, 3, recs, rows, 128)))
    x1, h1, a1, sp1, h2 = kept
    hot = distance_hot(rows * parts, distance_bias.shape[0])
    strip = bias_strip(distance_bias.astype(FLOAT), hot, nh, split)
    mine = [
        lax.dynamic_slice_in_dim(lengths, batch * here + lax.axis_index("tm") % split * recs, recs, 0)
        for batch in range(batches)
    ]
    attended = [attn_fwd(mine[batch], sent[batch], strip, nh) for batch in range(batches)]

    limits = lengths - lax.axis_index("tm").astype(jnp.int32) * rows
    kept = ()
    for batch in range(batches):
        back = swap(attended[batch][0]).reshape(units, split, recs, rows, 128)
        ins = (back, x1, lines, attend_output, convolve_input)
        outs = (own(width), own(width, F32), own(width), own(channels), own(channels), own(channels))
        kept = run(
            functools.partial(gate_kernel, nh=nh, first=batch * here, recs=recs), here, ins,
            [far(v) for v in ins], outs, [far(v) for v in outs], prefetch=(limits,), into=kept,
            scratch=(
                pltpu.VMEM((units, rows, 128), BF), held(width, F32), like(lines), like(attend_output),
                like(convolve_input), held(width), held(width, F32), held(width),
                held(channels), held(channels), held(channels), sems(40),
            ),
        )
    att, x2, h3, g, ga, gb = kept
    halo = passed_along(g[:, rows - 16 :, :], "tm", 1)

    dep = jnp.pad(depthwise.astype(FLOAT).T, ((0, 1), (0, 0)))
    ins = (g, halo, x2, cotangent, dep, lines, convolve_output, late_up, late_down)
    height = (width * hidden * 2 + channels * width) // 512 // count
    outs = (
        own(width), own(width, F32), own(channels), spot((seqs, 16, channels), BF),
        spot((16, 512)), spot((16, channels)), spot((count // 2, 2, height, 512), BF),
    )
    layer_out, dx3, dg, dhalo, small_mid, ddep, pack_mid = run(
        middle_kernel, seqs, ins,
        [per_rec(v) for v in ins[:4]] + [whole(v) for v in ins[4:6]] + [far(v) for v in ins[6:]],
        outs, [per_rec(v) for v in outs[:4]] + [whole_out(v) for v in outs[4:6]] + [far(outs[6])],
        scratch=(
            pltpu.VMEM((channels // 128, rows + 16, 128), F32), pltpu.VMEM((rows, channels), F32),
            pltpu.VMEM((rows, 1), F32), pltpu.VMEM((rows + 32, 128), F32), pltpu.VMEM((rows, channels), BF),
            pltpu.VMEM((tokens, width), BF), pltpu.VMEM((tokens, hidden), BF), pltpu.VMEM((rows, hidden), BF),
            pltpu.VMEM((tokens, hidden), BF), pltpu.VMEM((tokens, width), BF),
            pltpu.VMEM((tokens, channels), BF), pltpu.VMEM((tokens, width), BF),
            pltpu.VMEM((channels // 128, 128, 128), F32), pltpu.VMEM((rows, channels), F32),
            like(convolve_output), like(late_up), like(late_down), like(outs[6]), sems(16), sems(16),
        ),
        micros=200,
    )
    returned = passed_along(dhalo, "tm", -1)
    sums_mid = offloaded(pack_mid)

    kept = ()
    sent_back = []
    small_gate = []
    for batch in range(batches):
        ins = (dg, returned, ga, gb, dx3, x2, lines, convolve_input, attend_output)
        outs = (own(width, F32), own(2 * channels), own(width), wide(), spot((8, 512)))
        *kept, do, small = run(
            functools.partial(ungate_kernel, nh=nh, first=batch * here, recs=recs), here, ins,
            [far(v) for v in ins], outs, [far(v) for v in outs],
            scratch=(
                held(channels), pltpu.VMEM((16, channels), BF), like(lines), like(convolve_input), like(attend_output),
                held(channels), held(channels), held(width, F32), held(width, F32), held(width, F32),
                held(2 * channels), held(width), pltpu.VMEM((units, rows, 128), BF), pltpu.VMEM((8, 512), F32),
                held(512, F32), held(width, F32), sems(40),
            ),
            into=kept,
        )
        small_gate.append(small)
        sent_back.append(swap(do.reshape(parts, recs, rows, 128)))
    dx2, du, dy2 = kept
    pack_gate = shares(
        ("columns", "columns"), (merge(h3), merge(du), merge(att), merge(dy2)), 2 * channels * width + width * width,
        apart=False,
    )
    own_grads = []
    diagonals = 0.0
    for batch in range(batches):
        out, lse = attended[batch]
        grad, diagonal = attn_bwd(mine[batch], sent[batch], sent_back[batch], out, lse, strip, nh)
        diagonals = diagonals + diagonal
        own_grads.append(swap(grad).reshape(units, split, 3, recs, rows, 128))
    sums_gate = offloaded(pack_gate[0])
    grad_table = table_grad(diagonals, hot, nh, split, heads)

    kept = ()
    kept_two = ()
    small_proj = []
    small_first = []
    for batch in range(batches):
        ins = (own_grads[batch], x1, dx2, lines, attend_input)
        outs = (own(width, F32), own(width), own(3 * width), spot((8, 512)))
        if batch == batches - 1:
            part_rest = time_sum(jnp.concatenate([sums_mid, sums_gate], axis=0))
        *kept, small = run(
            functools.partial(project_kernel, nh=nh, first=batch * here, recs=recs), here, ins,
            [far(v) for v in ins], outs, [far(v) for v in outs],
            scratch=(
                like(lines), like(attend_input), pltpu.VMEM((3, units, rows, 128), BF), held(width, F32),
                held(width, F32), held(width, F32), held(width), held(3 * width), pltpu.VMEM((8, 512), F32),
                held(width, F32), sems(40),
            ),
            into=kept, after=(sums_mid,) if batch == batches - 1 else (),
        )
        small_proj.append(small)
        dx1, dy1, dp = kept
        if batch == batches - 1:
            pack_proj = shares(
                ("columns", "rows"), (merge(h2), merge(dp), merge(a1), merge(dy1)), width * hidden + width * 3 * width,
                apart=False,
            )
            sums_proj = offloaded(pack_proj[0])
            before = ()
        else:
            before = ()
        ins = (dy1, dx1, frames, sp1, lines, early_up, early_down)
        outs = (own(width), own(hidden), spot((8, 512)))
        *kept_two, small = run(
            functools.partial(close_kernel, first=batch * here), here, ins,
            [far(v) for v in ins], outs, [far(v) for v in outs],
            scratch=(
                held(width), like(lines), like(early_up), like(early_down), held(hidden), held(width, F32),
                held(width), held(hidden), held(width), pltpu.VMEM((8, 512), F32), held(width, F32), sems(40),
            ),
            into=kept_two, after=before,
        )
        small_first.append(small)
    dx0, dz1 = kept_two
    pack_last = shares(
        ("columns",), (merge(h1), merge(dz1)), width * hidden + 32 * 512 * count,
        extra=(small_mid, ddep, grad_table, *small_first, *small_proj, *small_gate), after=(part_rest,),
    )
    part_last = along_chips(along_time(between_cores(*pack_last)))
    part_proj = time_sum_by_steps(sums_proj)
    totals = (part_rest, *others(part_rest), part_proj, *others(part_proj), part_last, *others(part_last))
    return (layer_out, dx0) + finish(
        totals, count, parts, width, hidden, channels, depthwise.shape[1], distance_bias.shape
    )


def offloaded(packed):
    sent = packed.reshape(-1, packed.shape[3])
    return lax.psum_scatter(sent, "rows", scatter_dimension=0, tiled=True)


def with_others(mine):
    parts = lax.axis_size("tm")
    return lax.all_to_all(jnp.broadcast_to(mine, (parts,) + mine.shape), "tm", 0, 0, tiled=True)


def total(blocks):
    return jnp.sum(blocks.astype(FLOAT), axis=0).astype(BF)


def between_cores(keep, send):
    devices = range(lax.axis_size("rows"))
    got = lax.ppermute(send, "rows", [(i, i ^ 1) for i in devices])
    return (keep.astype(FLOAT) + got.astype(FLOAT)).astype(BF)


def time_sum(share):
    parts = lax.axis_size("tm")
    blocks = share.reshape((parts, share.shape[0] // parts) + share.shape[1:])
    return total(lax.all_to_all(blocks, "tm", 0, 0, tiled=True))


def time_sum_by_steps(share):
    parts = lax.axis_size("tm")
    me = lax.axis_index("tm")
    blocks = share.reshape((parts, share.shape[0] // parts) + share.shape[1:])
    pick = lambda k: lax.dynamic_index_in_dim(blocks, me ^ k, 0, keepdims=False)
    sums = pick(0).astype(FLOAT)
    for k in range(1, parts):
        got = lax.ppermute(pick(k), "tm", [(i, i ^ k) for i in range(parts)])
        sums = sums + got.astype(FLOAT)
    return sums.astype(BF)


def others(mine):
    parts = lax.axis_size("tm")
    return [lax.ppermute(mine, "tm", [(i, i ^ k) for i in range(parts)]) for k in range(1, parts)]


def along_time(half):
    chips, height, width = half.shape
    parts = lax.axis_size("tm")
    blocks = jnp.transpose(half.reshape(chips, parts, height // parts, width), (1, 0, 2, 3))
    return total(lax.all_to_all(blocks, "tm", 0, 0, tiled=True))


def along_chips(part):
    devices = range(lax.axis_size("rows"))
    groups = [[i for i in devices if i % 2 == core] for core in range(2)]
    return total(lax.all_to_all(part, "rows", 0, 0, axis_index_groups=groups, tiled=True))


def finish(totals, count, parts, width, hidden, channels, taps, table_shape):
    share = width // count
    line = (1, share)
    broad = (1, channels // count)
    shapes = (
        line, line, (share, hidden), (hidden // count, width), line, line, (share, 3 * width), (share, width),
        (table_shape[0] // count, table_shape[1]), line, line, (share, 2 * channels), (taps, channels // count),
        broad, broad, (channels // count, width), line, line, (share, hidden), (hidden // count, width), line, line,
    )
    outs = tuple(spot(shape) for shape in shapes)
    me = lax.axis_index("tm").astype(jnp.int32)[None]
    got = list(
        run(
            functools.partial(finish_kernel, parts=parts), 1, totals, [whole(v) for v in totals],
            outs, [whole_out(v) for v in outs], prefetch=(me,), micros=3,
            scratch=[pltpu.VMEM((parts,) + v.shape, BF) for v in totals[::parts]],
        )
    )
    got[12] = got[12].T
    for place, shape in enumerate(shapes):
        if shape[0] == 1:
            got[place] = got[place].reshape(-1)
    return tuple(got)


def solution(mesh):
    placed = (
        P("rows", "tm", None),
        P("rows", "tm", None),
        P("rows"),
        P(),
        P(),
        P(),
        P(),
        P(),
        P(),
        P(),
        P(),
        P(),
        P(),
        P(),
        P(),
        P(),
        P(),
        P(),
        P(),
        P(),
        P(),
        P(),
        P(),
        P(),
        P(),
    )
    return jax.shard_map(
        body,
        mesh=mesh,
        in_specs=placed,
        out_specs=(
            P("rows", "tm", None),
            P("rows", "tm", None),
            P("rows"),
            P("rows"),
            P("rows", None),
            P("rows", None),
            P("rows"),
            P("rows"),
            P("rows", None),
            P("rows", None),
            P("rows", None),
            P("rows"),
            P("rows"),
            P("rows", None),
            P("rows", None),
            P("rows"),
            P("rows"),
            P("rows", None),
            P("rows"),
            P("rows"),
            P("rows", None),
            P("rows", None),
            P("rows"),
            P("rows"),
        ),
        check_vma=False,
    )
```

```python
import functools

import jax
import jax.numpy as jnp
from jax import lax
from jax.experimental import pallas as pl
from jax.experimental.pallas import tpu as pltpu
from jax.sharding import PartitionSpec as P

EPSILON = 1e-05
NEGATIVE = -1e30
HIGHEST = lax.Precision.HIGHEST
BFLOAT = jnp.bfloat16
FLOAT = jnp.float32
NEG = NEGATIVE
F32 = FLOAT
BF = BFLOAT


MEGA = 2**20
SCALE = 1


def cost(micros):
    micros = micros * SCALE
    return pl.CostEstimate(
        flops=int(micros * 1.1e9), bytes_accessed=int(micros * 3.6e6), transcendentals=0
    )


def passed_along(block, axis, distance):
    devices = range(lax.axis_size(axis))
    route = [(i - distance, i) for i in devices if i - distance in devices]
    return lax.ppermute(block, axis, route)


def boundaries(seq_total):
    edges_list = list(range(1, 16))
    for exponent in range(16):
        edges_list.append(int(16.0 * (seq_total / 16.0) ** (exponent / 16.0)))
    return edges_list


KEYS = 256
QUERIES = 512


def nt(a, b):
    return lax.dot_general(a, b, (((1,), (1,)), ((), ())), preferred_element_type=F32)


def nn(a, b):
    return lax.dot_general(a, b, (((1,), (0,)), ((), ())), preferred_element_type=F32)


def strip_kernel(base_ref, out_ref):
    heads, keys, _ = out_ref.shape
    for h in range(heads):
        base = base_ref[h]
        for g in range(keys // 8):
            out_ref[h, 8 * g : 8 * g + 8, :] = pltpu.roll(base, 8 * g, 1)[:, keys:] if g else base[:, keys:]


def make_strip(base):
    heads, _, wide = base.shape
    return pl.pallas_call(
        strip_kernel,
        out_shape=jax.ShapeDtypeStruct((heads, KEYS, wide - KEYS), F32),
        compiler_params=pltpu.CompilerParams(vmem_limit_bytes=58 * MEGA),
        cost_estimate=cost(3),
    )(base)


def head_lanes(shape, h):
    lane = lax.broadcasted_iota(jnp.int32, shape, 1)
    return (lane >= 64 * h) & (lane < 64 * h + 64), lane == ((64 * h + 64) % 128)


def masked_queries(q, h):
    mine, spare = head_lanes(q.shape, h)
    return jnp.where(mine, q, jnp.where(spare, 1.0, 0.0)).astype(BF)


def masked_keys(k, h, first, length):
    mine, spare = head_lanes(k.shape, h)
    beyond = first + lax.broadcasted_iota(jnp.int32, k.shape, 0) >= length
    return jnp.where(mine, k, jnp.where(spare & beyond, NEG, 0.0)).astype(BF)


def block_of(index, size):
    return pl.ds(pl.multiple_of(index * size, 128), size)


def loop(first, last, step):
    def turn(index, carried):
        step(index)
        return carried

    lax.fori_loop(first, last, turn, 0)


def attend_kernel(len_ref, x_ref, bias_ref, o_ref, lse_ref, kh, vt, qh, acc, ot, strip_ref, sem, *, nh):
    parts, rows = x_ref.shape[0], x_ref.shape[3]
    total = parts * rows
    length = len_ref[pl.program_id(0)]
    bias = pltpu.make_async_copy(bias_ref, strip_ref, sem.at[0])
    bias.start()

    def prepare(t):
        at = block_of(t, rows)
        q = x_ref[t, 0, 0].astype(F32) * 0.125
        k = x_ref[t, 1, 0].astype(F32)
        v = x_ref[t, 2, 0].astype(F32).T.astype(BF)
        for h in range(nh):
            qh[h, at, :] = masked_queries(q, h)
            kh[h, at, :] = masked_keys(k, h, t * rows, length)
            vt[h, 0:64, at] = v[64 * h : 64 * h + 64]
            ones = lax.broadcasted_iota(jnp.int32, (16, rows), 0) == 0
            vt[h, 64:80, at] = jnp.where(ones, 1.0, 0.0).astype(BF)

    loop(0, parts, prepare)
    bias.wait()

    def queries(qb):
        at = block_of(qb, QUERIES)
        for h in range(nh):
            acc[h] = jnp.zeros((80, QUERIES), F32)

        def keys(kb, peaks):
            there = block_of(kb, QUERIES)
            after = []
            for h in range(nh):
                scores = []
                for half in range(QUERIES // KEYS):
                    first = kb * QUERIES + half * KEYS
                    off = pl.ds(pl.multiple_of(KEYS + qb * QUERIES - first, 128), QUERIES)
                    k = kh[h, pl.ds(pl.multiple_of(first, 128), KEYS), :]
                    scores.append(nt(k, qh[h, at, :]) + strip_ref[h, :, off])
                peak = peaks[h]
                for s in scores:
                    peak = jnp.maximum(peak, jnp.max(s, axis=0, keepdims=True))
                p = jnp.concatenate([jnp.exp(s - peak).astype(BF) for s in scores], axis=0)
                acc[h] = acc[h] * jnp.exp(peaks[h] - peak) + nn(vt[h, :, there], p)
                after.append(peak)
            return tuple(after)

        last = jnp.minimum(qb + 1, (length + QUERIES - 1) // QUERIES)
        peaks = lax.fori_loop(
            0, last, keys, tuple(jnp.full((1, QUERIES), NEG, F32) for _ in range(nh))
        )
        for h in range(nh):
            sums = acc[h, 64:65, :]
            lse_ref[0, h, :, at] = peaks[h] + jnp.log(sums)
            ot[64 * h : 64 * h + 64, at] = acc[h, 0:64, :] / sums
        if nh == 1:
            ot[64:128, at] = jnp.zeros((64, QUERIES), F32)

    loop(0, total // QUERIES, queries)

    def give(t):
        o_ref[t, 0] = ot[:, block_of(t, rows)].T.astype(BF)

    loop(0, parts, give)


def attn_fwd(lengths, x, strip, nh):
    parts, _, recs, rows, wide = x.shape
    total = parts * rows
    return pl.pallas_call(
        functools.partial(attend_kernel, nh=nh),
        grid_spec=pltpu.PrefetchScalarGridSpec(
            num_scalar_prefetch=1,
            grid=(recs,),
            in_specs=[
                pl.BlockSpec((parts, 3, 1, rows, wide), lambda r, l: (0, 0, r, 0, 0)), pl.BlockSpec(memory_space=pl.ANY),
            ],
            out_specs=[
                pl.BlockSpec((parts, 1, rows, wide), lambda r, l: (0, r, 0, 0)),
                pl.BlockSpec((1, nh, 1, total), lambda r, l: (r, 0, 0, 0)),
            ],
            scratch_shapes=[
                pltpu.VMEM((nh, total, wide), BF), pltpu.VMEM((nh, 80, total), BF),
                pltpu.VMEM((nh, total, wide), BF), pltpu.VMEM((nh, 80, QUERIES), F32),
                pltpu.VMEM((wide, total), F32), pltpu.VMEM(strip.shape, F32), pltpu.SemaphoreType.DMA((1,)),
            ],
        ),
        out_shape=[
            jax.ShapeDtypeStruct((parts, recs, rows, wide), BF),
            jax.ShapeDtypeStruct((recs, nh, 1, total), F32),
        ],
        compiler_params=pltpu.CompilerParams(vmem_limit_bytes=58 * MEGA),
        cost_estimate=cost(11),
    )(lengths, x, strip)


def attend_back_kernel(
    len_ref, x_ref, do_ref, o_ref, lse_ref, bias_ref, dx_ref, db_ref,
    kh, vh, qh, qs, dos, kt, dqt, delta, dk, dv, dks, dvs, dbs, strip_ref, sem, *, nh,
):
    parts, rows = x_ref.shape[0], x_ref.shape[3]
    total = parts * rows
    length = len_ref[pl.program_id(0)]
    blocks = (length + KEYS - 1) // KEYS
    bias = pltpu.make_async_copy(bias_ref, strip_ref, sem.at[0])
    bias.start()

    @pl.when(pl.program_id(0) == 0)
    def _():
        dbs[...] = jnp.zeros_like(dbs)

    dqt[...] = jnp.zeros_like(dqt)

    def prepare(t):
        at = block_of(t, rows)
        q = x_ref[t, 0, 0].astype(F32) * 0.125
        k = x_ref[t, 1, 0].astype(F32)
        v = x_ref[t, 2, 0].astype(F32)
        do = do_ref[t, 0]
        qs[at, :] = q.astype(BF)
        dos[at, :] = do
        kt[:, at] = k.T.astype(BF)
        product = (do.astype(F32) * o_ref[t, 0].astype(F32)).T
        for h in range(nh):
            qh[h, at, :] = masked_queries(q, h)
            kh[h, at, :] = masked_keys(k, h, t * rows, length)
            vh[h, at, :] = jnp.where(head_lanes(v.shape, h)[0], v, 0.0).astype(BF)
            delta[h, :, at] = jnp.sum(product[64 * h : 64 * h + 64], axis=0, keepdims=True)

    loop(0, parts, prepare)
    bias.wait()

    def keys(kb):
        there = block_of(kb, KEYS)
        dk[...] = jnp.zeros_like(dk)
        dv[...] = jnp.zeros_like(dv)

        def queries(qb):
            at = block_of(qb, QUERIES)
            off = pl.ds(pl.multiple_of(KEYS + qb * QUERIES - kb * KEYS, 128), QUERIES)
            for h in range(nh):
                s = nt(kh[h, there, :], qh[h, at, :]) + strip_ref[h, :, off]
                p = jnp.exp(s - lse_ref[0, h, :, at])
                ds = p * (nt(vh[h, there, :], dos[at, :]) - delta[h, :, at])
                low = ds.astype(BF)
                dv[h] += nn(p.astype(BF), dos[at, :])
                dk[h] += nn(low, qs[at, :])
                dqt[64 * h : 64 * h + 64, at] += nn(kt[64 * h : 64 * h + 64, there], low)
                dbs[h, :, off] += ds

        loop(kb * KEYS // QUERIES, total // QUERIES, queries)
        first, _ = head_lanes((KEYS, 128), 0)
        dks[there, :] = (jnp.where(first, dk[0], dk[1]) if nh == 2 else dk[0]).astype(BF)
        dvs[there, :] = (jnp.where(first, dv[0], dv[1]) if nh == 2 else dv[0]).astype(BF)

    loop(0, blocks, keys)

    def nothing(kb):
        dks[block_of(kb, KEYS), :] = jnp.zeros((KEYS, 128), BF)
        dvs[block_of(kb, KEYS), :] = jnp.zeros((KEYS, 128), BF)

    loop(blocks, total // KEYS, nothing)

    def give(t):
        at = block_of(t, rows)
        dx_ref[t, 0, 0] = (dqt[:, at] * 0.125).T.astype(BF)
        dx_ref[t, 1, 0] = dks[at, :]
        dx_ref[t, 2, 0] = dvs[at, :]

    loop(0, parts, give)

    @pl.when(pl.program_id(0) == pl.num_programs(0) - 1)
    def _():
        wide = dbs.shape[2]
        for h in range(nh):
            sums = dbs[h, 0:8, :]
            for g in range(1, KEYS // 8):
                sums = sums + pltpu.roll(dbs[h, 8 * g : 8 * g + 8, :], wide - 8 * g, 1)
            db_ref[h] = sums


def attn_bwd(lengths, x, do, o, lse, strip, nh):
    parts, _, recs, rows, wide = x.shape
    total = parts * rows
    several = pltpu.VMEM((nh, total, wide), BF)
    single = pltpu.VMEM((total, wide), BF)
    part = pltpu.VMEM((nh, KEYS, wide), F32)
    return pl.pallas_call(
        functools.partial(attend_back_kernel, nh=nh),
        grid_spec=pltpu.PrefetchScalarGridSpec(
            num_scalar_prefetch=1,
            grid=(recs,),
            in_specs=[
                pl.BlockSpec((parts, 3, 1, rows, wide), lambda r, l: (0, 0, r, 0, 0)),
                pl.BlockSpec((parts, 1, rows, wide), lambda r, l: (0, r, 0, 0)),
                pl.BlockSpec((parts, 1, rows, wide), lambda r, l: (0, r, 0, 0)),
                pl.BlockSpec((1, nh, 1, total), lambda r, l: (r, 0, 0, 0)),
                pl.BlockSpec(memory_space=pl.ANY),
            ],
            out_specs=[
                pl.BlockSpec((parts, 3, 1, rows, wide), lambda r, l: (0, 0, r, 0, 0)),
                pl.BlockSpec((nh, 8, strip.shape[2]), lambda r, l: (0, 0, 0)),
            ],
            scratch_shapes=[
                several, several, several, single, single, pltpu.VMEM((wide, total), BF),
                pltpu.VMEM((wide, total), F32), pltpu.VMEM((nh, 1, total), F32), part, part, single, single,
                pltpu.VMEM(strip.shape, F32), pltpu.VMEM(strip.shape, F32), pltpu.SemaphoreType.DMA((1,)),
            ],
        ),
        out_shape=[
            jax.ShapeDtypeStruct((parts, 3, recs, rows, wide), BF),
            jax.ShapeDtypeStruct((nh, 8, strip.shape[2]), F32),
        ],
        compiler_params=pltpu.CompilerParams(vmem_limit_bytes=58 * MEGA),
        cost_estimate=cost(15),
    )(lengths, x, do, o, lse, strip)


def tn(a, b):
    return lax.dot_general(a, b, (((0,), (0,)), ((), ())), preferred_element_type=F32)


def sigmoid(v):
    return 0.5 * jnp.tanh(0.5 * v) + 0.5


LINES = {
    "early_gain": 0, "early_shift": 1, "attend_gain": 2, "attend_shift": 3, "convolve_gain": 4, "convolve_shift": 5,
    "late_gain": 6, "late_shift": 7, "final_gain": 8, "final_shift": 9, "inner_gain": 10,
}


def row(ref, name):
    place = LINES[name]
    return ref[place : place + 1, :]


def broad_row(ref, name, width):
    blocks = width // 512
    place = LINES["inner_gain"] + (blocks if name == "inner_shift" else 0)
    return jnp.concatenate([ref[place + c : place + c + 1, :] for c in range(blocks)], axis=1)


def part_of(index, size=512):
    return pl.ds(pl.multiple_of(index * size, 128), size)


def repeat(count, step):
    def turn(index, carried):
        step(index)
        return carried

    lax.fori_loop(0, count, turn, 0)


def mover(sems):
    spent = []

    def move(source, target):
        copy = pltpu.make_async_copy(source, target, sems.at[len(spent)])
        spent.append(copy)
        copy.start()
        return copy

    return move


def pieces(width):
    return [slice(first, first + 512) for first in range(0, width, 512)]


def settle(copies):
    for copy in copies:
        copy.wait()


class Lane:
    def __init__(self, sems, first, parts, make):
        self.sems, self.first, self.parts, self.make = sems, first, parts, make
        self.each = len(make(0))

    def copies(self, part):
        place = self.first + part * self.each
        return [
            pltpu.make_async_copy(source, target, self.sems.at[place + k])
            for k, (source, target) in enumerate(self.make(part))
        ]

    def start(self, part=0):
        for copy in self.copies(part):
            copy.start()

    def wait(self, part=0):
        for copy in self.copies(part):
            copy.wait()

    def start_all(self):
        for part in range(self.parts):
            self.start(part)

    def wait_all(self):
        repeat(self.parts, self.wait)


def lanes(sems):
    spent = [0]

    def lane(parts, make):
        made = Lane(sems, spent[0], parts, make)
        spent[0] += parts * made.each
        return made

    return lane


def one(*pairs):
    return 1, lambda part: list(pairs)


def feed(h, wu, wd, up, down, keep):
    y = None
    for f in range(wu.shape[1] // 512):
        at = slice(512 * f, 512 * f + 512)
        up(f)
        z = nn(h, wu[:, at])
        sig = sigmoid(z)
        a = (z * sig).astype(BF)
        keep(f, at, a, (sig * (1.0 + z * (1.0 - sig))).astype(BF))
        down(f)
        part = nn(a, wd[at, :])
        y = part if y is None else y + part
    return y


def feed_back(dy, wu, wd, up, down, slope, keep):
    dh = None
    for f in range(wu.shape[1] // 512):
        at = slice(512 * f, 512 * f + 512)
        down(f)
        dz = (nt(dy, wd[at, :]) * slope(f, at).astype(F32)).astype(BF)
        keep(f, at, dz)
        up(f)
        part = nt(dz, wu[:, at])
        dh = part if dh is None else dh + part
    return dh


def over_rows(rows, step):
    step(slice(0, rows))


def over_tiles(rows, step):
    def tile(t):
        step(part_of(t, 128))

    repeat(rows // 128, tile)


def share_columns(held, place, left, right, ready, send):
    height = left.shape[1] // (held.shape[0] * held.shape[1])

    def step(f):
        ready(f)
        block = tn(left[...], right[:, part_of(f)]).astype(BF)
        there = pl.ds(pl.multiple_of(place + f * height, 16), height)
        held[:, :, there, :] = block.reshape(held.shape[:2] + (height, 512))
        send(f, pl.ds(0, held.shape[0]), there)

    repeat(right.shape[1] // 512, step)


def share_rows(held, place, left, right, ready, send):
    height = left.shape[1] // (held.shape[0] * held.shape[1])
    each = 512 // (held.shape[1] * height)

    def step(f):
        ready(f)
        block = tn(left[:, part_of(f)], right[...]).astype(BF)
        who, there = pl.ds(each * f, each), pl.ds(place, height)
        held[who, :, there, :] = block.reshape(each, held.shape[1], height, 512)
        send(f, who, there)

    repeat(left.shape[1] // 512, step)


def columns_of(held, place, left, right):
    height = left.shape[1] // (held.shape[0] * held.shape[1])
    return lambda f: (pl.ds(0, held.shape[0]), pl.ds(pl.multiple_of(place + f * height, 16), height))


def rows_of(held, place, left, right):
    height = left.shape[1] // (held.shape[0] * held.shape[1])
    each = 512 // (held.shape[1] * height)
    return lambda f: (pl.ds(each * f, each), pl.ds(place, height))


def spread_columns(send, held, place, left, right, ready):
    count = held.shape[0] * held.shape[1]
    height = left.shape[1] // count
    for f, at in enumerate(pieces(right.shape[1])):
        ready(f)
        there = slice(place, place + height)
        block = tn(left[...], right[:, at]).astype(BF)
        held[:, :, there, :] = block.reshape(held.shape[:2] + (height, 512))
        send(slice(0, held.shape[0]), there)
        place += height
    return place


def spread_rows(send, held, place, left, right, ready):
    height = left.shape[1] // (held.shape[0] * held.shape[1])
    each = 512 // (held.shape[1] * height)
    for f, at in enumerate(pieces(left.shape[1])):
        ready(f)
        who, there = slice(each * f, each * f + each), slice(place, place + height)
        block = tn(left[:, at], right[...]).astype(BF)
        held[who, :, there, :] = block.reshape(each, held.shape[1], height, 512)
        send(who, there)
    return place + height


def norm_parts(v):
    center = v - jnp.mean(v, axis=-1, keepdims=True)
    inverse = lax.rsqrt(jnp.mean(center * center, axis=-1, keepdims=True) + EPSILON)
    return center * inverse, inverse


def norm_pull(n, inverse, gain, grad):
    dn = grad * gain
    return (
        dn - jnp.mean(dn, axis=-1, keepdims=True) - n * jnp.mean(dn * n, axis=-1, keepdims=True)
    ) * inverse


def add_rows(ref, place, values):
    total = jnp.sum(values, axis=0, keepdims=True)
    for c in range(values.shape[1] // 512):
        ref[place + c : place + c + 1, :] += total[:, 512 * c : 512 * c + 512]


def start_small(ref):
    @pl.when(pl.program_id(0) == 0)
    def _():
        ref[...] = jnp.zeros_like(ref)


def put_heads(write, value, nh):
    for pair in range(value.shape[1] // 128):
        part = value[:, 128 * pair : 128 * pair + 128]
        if nh == 2:
            write(pair, part.astype(BF))
        else:
            low = lax.broadcasted_iota(jnp.int32, part.shape, 1) < 64
            write(2 * pair, jnp.where(low, part, 0.0).astype(BF))
            write(2 * pair + 1, jnp.where(low, pltpu.roll(part, 64, 1), 0.0).astype(BF))


def take_heads(read, units, nh):
    if nh == 2:
        return jnp.concatenate([read(u) for u in range(units)], axis=1)
    pairs = [
        (read(2 * u).astype(F32) + pltpu.roll(read(2 * u + 1).astype(F32), 64, 1)).astype(BF)
        for u in range(units // 2)
    ]
    return jnp.concatenate(pairs, axis=1)


def lines_kernel(*refs):
    out = refs[-1]
    out[...] = jnp.zeros_like(out)
    place = 0
    for ref in refs[:-1]:
        for c in range(ref.shape[0] // 512):
            out[place : place + 1, :] = ref[512 * c : 512 * c + 512].astype(F32).reshape(1, 512)
            place += 1


def open_kernel(
    x_ref, g1_ref, s1_ref, g2_ref, s2_ref, wu_ref, wd_ref, wi_ref, x1_ref, h1_ref, a_ref, sp_ref, h2_ref, u_ref,
    x, g1, s1, g2, s2, wu, wd, wi, x1, h1, a1, sp, h2, u, total, sems, *, nh, first, recs,
):
    turn = pl.program_id(0)
    rec = first + turn
    rows = x.shape[0]
    parts = wu.shape[1] // 512
    lane = lanes(sems)
    ahead = lane(*one((x_ref.at[rec], x), (g1_ref, g1), (s1_ref, s1), (g2_ref, g2), (s2_ref, s2)))
    line = lambda ref: ref[...].astype(F32).reshape(1, 512)
    up = lane(parts, lambda f: [(wu_ref.at[:, part_of(f)], wu.at[:, part_of(f)])])
    down = lane(parts, lambda f: [(wd_ref.at[part_of(f), :], wd.at[part_of(f), :])])
    wide = lane(3, lambda f: [(wi_ref.at[:, part_of(f)], wi.at[:, part_of(f)])])
    out_h1 = lane(*one((h1, h1_ref.at[rec])))
    out_hidden = lane(
        parts,
        lambda f: [
            (a1.at[:, part_of(f)], a_ref.at[rec, :, part_of(f)]),
            (sp.at[:, part_of(f)], sp_ref.at[rec, :, part_of(f)]),
        ],
    )
    out_x1 = lane(*one((x1, x1_ref.at[rec]), (h2, h2_ref.at[rec])))
    out_u = lane(3, lambda f: [(u.at[f], u_ref.at[:, turn // recs, f, turn % recs])])
    ahead.start()
    for f in range(parts):
        up.start(f)
        down.start(f)
    wide.start_all()
    ahead.wait()

    def normal(at):
        n, _ = norm_parts(x[at, :].astype(F32))
        h1[at, :] = (n * line(g1) + line(s1)).astype(BF)

    over_rows(rows, normal)
    out_h1.start()

    def keep(f, at, a, slope):
        a1[:, at] = a
        sp[:, at] = slope
        out_hidden.start(f)

    total[...] = feed(h1[...], wu, wd, up.wait, down.wait, keep)

    def second(at):
        value = x[at, :].astype(F32) + 0.5 * total[at, :]
        x1[at, :] = value
        n, _ = norm_parts(value)
        h2[at, :] = (n * line(g2) + line(s2)).astype(BF)

    over_rows(rows, second)
    out_x1.start()

    def project(kind):
        wide.wait(kind)

        def write(unit, part):
            u[kind, unit] = part

        put_heads(write, nn(h2[...], wi[:, part_of(kind)]), nh)
        out_u.start(kind)

    repeat(3, project)
    for out in (out_h1, out_hidden, out_x1, out_u):
        out.wait_all()


def gate_kernel(
    len_ref, o_ref, x1_ref, lines_ref, wo_ref, wc_ref, att_ref, x2_ref, h3_ref, g_ref, ga_ref, gb_ref,
    o, x1, lines, wo, wc, att, x2, h3, g, ga, gb, sems, *, nh, first, recs,
):
    turn = pl.program_id(0)
    rec = first + turn
    rows = x1.shape[0]
    channels = g.shape[1]
    parts = channels // 512
    lane = lanes(sems)
    ahead = lane(*one((o_ref.at[:, turn // recs, turn % recs], o), (wo_ref, wo)))
    then = lane(*one((x1_ref.at[rec], x1), (lines_ref, lines)))
    wide = lane(
        parts,
        lambda f: [
            (wc_ref.at[:, part_of(f)], wc.at[:, part_of(f)]),
            (wc_ref.at[:, part_of(f + parts)], wc.at[:, part_of(f + parts)]),
        ],
    )
    out_att = lane(*one((att, att_ref.at[rec])))
    out_x2 = lane(*one((x2, x2_ref.at[rec]), (h3, h3_ref.at[rec])))
    out_g = lane(
        parts,
        lambda f: [
            (held.at[:, part_of(f)], out.at[rec, :, part_of(f)])
            for held, out in ((g, g_ref), (ga, ga_ref), (gb, gb_ref))
        ],
    )
    ahead.start()
    then.start()
    wide.start_all()
    ahead.wait()
    att[...] = take_heads(lambda unit: o[unit], o.shape[0], nh)
    out_att.start()
    then.wait()
    x2[...] = x1[...] + nn(att[...], wo[...])

    def normal(at):
        n, _ = norm_parts(x2[at, :])
        h3[at, :] = (n * row(lines, "convolve_gain") + row(lines, "convolve_shift")).astype(BF)

    over_tiles(rows, normal)
    out_x2.start()
    limit = len_ref[rec]
    place = lax.broadcasted_iota(jnp.int32, (rows, 1), 0)
    valid = jnp.where(place < limit, 1.0, 0.0)

    def step(f):
        at = part_of(f)
        wide.wait(f)
        lin = nn(h3[...], wc[:, at])
        sig = sigmoid(nn(h3[...], wc[:, part_of(f + parts)]))
        sv = sig * valid
        value = lin * sv
        g[:, at] = value.astype(BF)
        ga[:, at] = sv.astype(BF)
        gb[:, at] = (value * (1.0 - sig)).astype(BF)
        out_g.start(f)

    repeat(parts, step)
    for out in (out_att, out_x2, out_g):
        out.wait_all()


def middle_kernel(
    g_ref, halo_ref, x2_ref, cot_ref, dep, lines, wco, wu, wd,
    out_ref, dx3_ref, dg_ref, dhalo_ref, small_ref, ddep_ref, pack_ref,
    gx, cs, inv3, dcx, sp3, h4s, a4s, sp4, dz4s, dy4s, a3s, dy3s, tapped, dws, wcov, wuv, wdv, held, sems, out_sems,
):
    rec = pl.program_id(0)
    rows = x2_ref.shape[1]
    channels = g_ref.shape[2]
    strips = channels // 128
    taps = dep.shape[0] - 1
    start_small(small_ref)
    start_small(tapped)
    first = pl.multiple_of(rec * rows, 128)
    mine = pl.ds(first, rows)
    tile = 32
    fetched = [(wco, wcov)]
    for at in pieces(wu.shape[1]):
        fetched.append((wu.at[:, at], wuv.at[:, at]))
        fetched.append((wd.at[at, :], wdv.at[at, :]))
    fetched = [pltpu.make_async_copy(*pair, sems.at[k]) for k, pair in enumerate(fetched)]

    @pl.when(rec == 0)
    def _():
        for copy in fetched:
            copy.start()

    def ready(k):
        @pl.when(rec == 0)
        def _():
            fetched[k].wait()


    def conv(c):
        at = part_of(c, 128)
        gx[c, 0:16, :] = halo_ref[0, :, at].astype(F32)
        gx[c, 16:, :] = g_ref[0, :, at].astype(F32)
        for top in range(0, rows, tile):
            sums = dep[0:1, at] * gx[c, top + 2 : top + 2 + tile, :]
            for r in range(1, taps):
                sums = sums + dep[r : r + 1, at] * gx[c, top + 2 + r : top + 2 + r + tile, :]
            cs[top : top + tile, at] = sums

    repeat(strips, conv)

    def inner(t):
        there = pl.ds(pl.multiple_of(t * 384, 384), 384)
        n, inverse = norm_parts(cs[there, :])
        cs[there, :] = n
        inv3[there, :] = inverse
        w = n * broad_row(lines, "inner_gain", channels) + broad_row(lines, "inner_shift", channels)
        sig = sigmoid(w)
        a3s[pl.ds(first + pl.multiple_of(t * 384, 384), 384), :] = (w * sig).astype(BF)
        sp3[there, :] = (sig * (1.0 + w * (1.0 - sig))).astype(BF)

    repeat(rows // 384, inner)
    ready(0)
    x3 = x2_ref[0] + nn(a3s[mine, :], wcov[...])
    n4, inv4 = norm_parts(x3)
    h4 = (n4 * row(lines, "late_gain") + row(lines, "late_shift")).astype(BF)
    h4s[mine, :] = h4

    def keep(f, at, a, slope):
        a4s[mine, at] = a
        sp4[:, at] = slope

    y = feed(h4, wuv, wdv, lambda f: ready(1 + 2 * f), lambda f: ready(2 + 2 * f), keep)
    x4 = x3 + 0.5 * y
    n5, inv5 = norm_parts(x4)
    out_ref[0] = (n5 * row(lines, "final_gain") + row(lines, "final_shift")).astype(BF)
    cot = cot_ref[0].astype(F32)
    add_rows(small_ref, 8, cot * n5)
    add_rows(small_ref, 9, cot)
    dx4 = norm_pull(n5, inv5, row(lines, "final_gain"), cot)
    dx3_ref[0] = dx4
    dy4 = (0.5 * dx4).astype(BF)
    dy4s[mine, :] = dy4

    def keep_back(f, at, dz):
        dz4s[mine, at] = dz

    done = lambda f: None
    dh = feed_back(dy4, wuv, wdv, done, done, lambda f, at: sp4[:, at], keep_back)
    add_rows(small_ref, 6, dh * n4)
    add_rows(small_ref, 7, dh)
    dx3 = dx3_ref[0] + norm_pull(n4, inv4, row(lines, "late_gain"), dh)
    dx3_ref[0] = dx3
    dy3s[mine, :] = dx3.astype(BF)

    def pull(f):
        at = part_of(f)
        dws[:, at] = nt(dy3s[mine, :], wcov[at, :]) * sp3[:, at].astype(F32)

    repeat(channels // 512, pull)

    def inner_back(t):
        there = pl.ds(pl.multiple_of(t * 384, 384), 384)
        dw = dws[there, :]
        n = cs[there, :]
        add_rows(small_ref, 2, dw * n)
        add_rows(small_ref, 4, dw)
        cs[there, :] = norm_pull(n, inv3[there, :], broad_row(lines, "inner_gain", channels), dw)

    repeat(rows // 384, inner_back)

    def conv_back(c):
        at = part_of(c, 128)
        dcx[0:16, :] = jnp.zeros((16, 128), F32)
        dcx[16 : 16 + rows, :] = cs[:, at]
        dcx[16 + rows :, :] = jnp.zeros((16, 128), F32)
        sums = [jnp.zeros((8, 128), F32)] * taps
        for top in range(0, rows, tile):
            dc = dcx[16 + top : 16 + top + tile, :]
            for r in range(taps):
                term = dc * gx[c, top + 2 + r : top + 2 + r + tile, :]
                sums[r] = sums[r] + jnp.sum(term.reshape(tile // 8, 8, 128), axis=0)
        for r in range(taps):
            tapped[c, 8 * r : 8 * r + 8, :] += sums[r]
        for top in range(0, rows + 16, tile):
            size = min(tile, rows + 16 - top)
            sums = dep[0:1, at] * dcx[top + 14 : top + 14 + size, :]
            for r in range(1, taps):
                sums = sums + dep[r : r + 1, at] * dcx[top + 14 - r : top + 14 - r + size, :]
            if top == 0:
                dhalo_ref[0, :, at] = sums[0:16].astype(BF)
                dg_ref[0, 0 : size - 16, at] = sums[16:].astype(BF)
            else:
                dg_ref[0, top - 16 : top - 16 + size, at] = sums.astype(BF)

    repeat(strips, conv_back)

    @pl.when(rec == pl.num_programs(0) - 1)
    def _():
        def depth(c):
            for r in range(taps):
                ddep_ref[r : r + 1, part_of(c, 128)] = jnp.sum(
                    tapped[c, 8 * r : 8 * r + 8, :], axis=0, keepdims=True
                )

        ddep_ref[taps:, :] = jnp.zeros((1, channels), F32)
        repeat(strips, depth)
        move = mover(out_sems)
        sent = []

        def send(who, there):
            sent.append(move(held.at[who, :, there], pack_ref.at[who, :, there]))

        place = spread_columns(send, held, 0, h4s, dz4s, done)
        place = spread_rows(send, held, place, a4s, dy4s, done)
        spread_rows(send, held, place, a3s, dy3s, done)
        settle(sent)


def share(kind, lane, held, outs, core, place, left, right, ready):
    columns = kind == "columns"
    parts = (right if columns else left).shape[1] // 512
    where = (columns_of if columns else rows_of)(held, place, left, right)

    def make(f):
        who, there = where(f)
        if core is None:
            return [(held.at[who, :, there], outs[0].at[who, :, there])]
        return [(held.at[who, c, there], out.at[who, there]) for c, out in zip((core, 1 - core), outs)]

    out = lane(parts, make)
    (share_columns if columns else share_rows)(
        held, place, left, right, ready, lambda f, who, there: out.start(f)
    )
    height = left.shape[1] // (held.shape[0] * held.shape[1])
    return place + height * (parts if columns else 1), out


def ungate_kernel(
    dg_ref, back_ref, ga_ref, gb_ref, dx3_ref, x2_ref, lines_ref, wc_ref, wo_ref,
    dx2_ref, du_ref, dy2_ref, do_ref, small_ref,
    dg, back, lines, wc, wo, ga, gb, dx3, x2, dx2, du, dy2, do, small, dgx, total, sems, *, nh, first, recs,
):
    turn = pl.program_id(0)
    rec = first + turn
    rows = x2.shape[0]
    channels = ga.shape[1]
    parts = channels // 512
    lane = lanes(sems)
    ahead = lane(*one((back_ref.at[rec], back)))
    fetch = lane(
        parts,
        lambda f: [
            (dg_ref.at[rec, :, part_of(f)], dg.at[:, part_of(f)]),
            (ga_ref.at[rec, :, part_of(f)], ga.at[:, part_of(f)]),
            (gb_ref.at[rec, :, part_of(f)], gb.at[:, part_of(f)]),
            (wc_ref.at[:, part_of(f)], wc.at[:, part_of(f)]),
            (wc_ref.at[:, part_of(f + parts)], wc.at[:, part_of(f + parts)]),
        ],
    )
    then = lane(*one((x2_ref.at[rec], x2), (dx3_ref.at[rec], dx3), (lines_ref, lines), (wo_ref, wo)))
    out_du = lane(
        parts,
        lambda f: [
            (du.at[:, part_of(f)], du_ref.at[rec, :, part_of(f)]),
            (du.at[:, part_of(f + parts)], du_ref.at[rec, :, part_of(f + parts)]),
        ],
    )
    out_dx2 = lane(*one((dx2, dx2_ref.at[rec]), (dy2, dy2_ref.at[rec]), (small, small_ref)))
    out_do = lane(*one((do, do_ref.at[:, turn // recs, turn % recs])))
    ahead.start()
    fetch.start_all()
    then.start()
    start_small(small)
    total[...] = jnp.zeros_like(total)
    ahead.wait()

    def step(f):
        at = part_of(f)
        up = part_of(f + parts)
        fetch.wait(f)
        dgx[...] = dg[:, at].astype(F32)
        dgx[rows - 16 :, :] += back[:, at].astype(F32)
        value = dgx[...]
        lin = (value * ga[:, at].astype(F32)).astype(BF)
        gate = (value * gb[:, at].astype(F32)).astype(BF)
        du[:, at] = lin
        du[:, up] = gate
        out_du.start(f)
        total[...] += nt(lin, wc[:, at]) + nt(gate, wc[:, up])

    repeat(parts, step)
    then.wait()

    def pull(at):
        n, inverse = norm_parts(x2[at, :])
        dh = total[at, :]
        add_rows(small, 0, dh * n)
        add_rows(small, 1, dh)
        value = dx3[at, :] + norm_pull(n, inverse, row(lines, "convolve_gain"), dh)
        dx2[at, :] = value
        dy2[at, :] = value.astype(BF)

    over_rows(rows, pull)
    out_dx2.start()

    def write(unit, part):
        do[unit] = part

    put_heads(write, nt(dy2[...], wo[...]), nh)
    out_do.start()
    for out in (out_du, out_dx2, out_do):
        out.wait_all()


def project_kernel(
    u_ref, x1_ref, dx2_ref, lines_ref, wi_ref, dx1_ref, dy_ref, dp_ref, small_ref,
    lines, wi, u, x1, dx2, dx1, dy, dp, small, total, sems, *, nh, first, recs,
):
    turn = pl.program_id(0)
    rec = first + turn
    rows = x1.shape[0]
    lane = lanes(sems)
    fetch = lane(
        3,
        lambda f: [
            (u_ref.at[:, turn // recs, f, turn % recs], u.at[f]), (wi_ref.at[:, part_of(f)], wi.at[:, part_of(f)]),
        ],
    )
    then = lane(*one((x1_ref.at[rec], x1), (dx2_ref.at[rec], dx2), (lines_ref, lines)))
    out_dp = lane(3, lambda f: [(dp.at[:, part_of(f)], dp_ref.at[rec, :, part_of(f)])])
    out_dx1 = lane(*one((dx1, dx1_ref.at[rec]), (dy, dy_ref.at[rec]), (small, small_ref)))
    fetch.start_all()
    then.start()
    start_small(small)
    total[...] = jnp.zeros_like(total)

    def step(kind):
        at = part_of(kind)
        fetch.wait(kind)
        value = take_heads(lambda unit: u[kind, unit], u.shape[1], nh)
        dp[:, at] = value
        out_dp.start(kind)
        total[...] += nt(value, wi[:, at])

    repeat(3, step)
    then.wait()

    def pull(at):
        n, inverse = norm_parts(x1[at, :])
        dh = total[at, :]
        add_rows(small, 0, dh * n)
        add_rows(small, 1, dh)
        value = dx2[at, :] + norm_pull(n, inverse, row(lines, "attend_gain"), dh)
        dx1[at, :] = value
        dy[at, :] = (0.5 * value).astype(BF)

    over_rows(rows, pull)
    out_dx1.start()
    for out in (out_dp, out_dx1):
        out.wait_all()


def close_kernel(
    dy_ref, dx1_ref, x_ref, sp_ref, lines_ref, wu_ref, wd_ref, out_ref, dz_ref, small_ref,
    dy, lines, wu, wd, sp, dx1, x, dz, out, small, total, sems, *, first,
):
    rec = first + pl.program_id(0)
    rows = x.shape[0]
    parts = wu.shape[1] // 512
    lane = lanes(sems)
    ahead = lane(*one((dy_ref.at[rec], dy)))
    down = lane(
        parts,
        lambda f: [
            (wd_ref.at[part_of(f), :], wd.at[part_of(f), :]), (sp_ref.at[rec, :, part_of(f)], sp.at[:, part_of(f)]),
        ],
    )
    up = lane(parts, lambda f: [(wu_ref.at[:, part_of(f)], wu.at[:, part_of(f)])])
    then = lane(*one((x_ref.at[rec], x), (dx1_ref.at[rec], dx1), (lines_ref, lines)))
    out_dz = lane(parts, lambda f: [(dz.at[:, part_of(f)], dz_ref.at[rec, :, part_of(f)])])
    out_dx = lane(*one((out, out_ref.at[rec]), (small, small_ref)))
    ahead.start()
    for f in range(parts):
        down.start(f)
        up.start(f)
    then.start()
    start_small(small)
    ahead.wait()

    def keep(f, at, value):
        dz[:, at] = value
        out_dz.start(f)

    total[...] = feed_back(dy[...], wu, wd, up.wait, down.wait, lambda f, at: sp[:, at], keep)
    then.wait()

    def pull(at):
        n, inverse = norm_parts(x[at, :].astype(F32))
        dh = total[at, :]
        add_rows(small, 0, dh * n)
        add_rows(small, 1, dh)
        out[at, :] = (dx1[at, :] + norm_pull(n, inverse, row(lines, "early_gain"), dh)).astype(BF)

    over_rows(rows, pull)
    out_dx.start()
    for lane_out in (out_dz, out_dx):
        lane_out.wait_all()


def share_kernel(core_ref, *refs, kinds, extra, apart):
    jobs = len(kinds)
    ins = refs[: 2 * jobs]
    more = refs[2 * jobs : 2 * jobs + extra]
    outs = refs[2 * jobs + extra : 2 * jobs + extra + 1 + apart]
    held = refs[2 * jobs + extra + 1 + apart :]
    packed, small, sems = held[2 * jobs :]
    core = core_ref[0] if apart else None
    lane = lanes(sems)
    plan = []
    for k, kind in enumerate(kinds):
        left, right = ins[2 * k : 2 * k + 2]
        left_held, right_held = held[2 * k : 2 * k + 2]
        if kind == "columns":
            first = lane(*one((left, left_held)))
            source, target = right, right_held
        else:
            first = lane(*one((right, right_held)))
            source, target = left, left_held
        parts = lane(
            source.shape[1] // 512,
            lambda f, source=source, target=target: [(source.at[:, part_of(f)], target.at[:, part_of(f)])],
        )
        first.start()
        parts.start_all()
        plan.append((left_held, right_held, first, parts))
    waits = []
    place = 0
    for kind, (left, right, first, parts) in zip(kinds, plan):
        first.wait()
        place, out = share(kind, lane, packed, outs, core, place, left, right, parts.wait)
        waits.append(out)
    if extra:
        small_shares(more, packed, small, place)
        there = pl.ds(place, packed.shape[2] - place)
        out = lane(
            *one(*[(packed.at[:, c, there], target.at[:, there]) for c, target in zip((core, 1 - core), outs)])
        )
        out.start()
        waits.append(out)
    for out in waits:
        out.wait_all()


def small_shares(refs, packed, small, place):
    small_mid, ddep, table = refs[:3]
    batches = (len(refs) - 3) // 3
    count = packed.shape[0] * packed.shape[1]
    small[...] = jnp.zeros_like(small)
    for k in range(3):
        for ref in refs[3 + k * batches : 3 + k * batches + batches]:
            small[2 * k : 2 * k + 2, :] += ref[0:2, :]
    small[6:10, :] = small_mid[6:10, :]
    narrow = 512 // count
    broad = ddep.shape[1] // count
    high = table.shape[0] // count
    packed[:, :, place:, :] = jnp.zeros(packed.shape[:2] + (packed.shape[2] - place, 512), BF)
    blocks = ddep.shape[1] // 512
    inner = [
        jnp.concatenate([small_mid[first + c : first + c + 1, :] for c in range(blocks)], axis=1)
        for first in (2, 4)
    ]
    inner = jnp.concatenate(inner, axis=0)
    for s in range(count):
        there = slice(place, place + 16)
        packed[s // 2, s % 2, there, 0:narrow] = small[:, narrow * s : narrow * s + narrow].astype(BF)
        packed[s // 2, s % 2, place : place + 2, 128 : 128 + broad] = inner[
            :, broad * s : broad * s + broad
        ].astype(BF)
        packed[s // 2, s % 2, there, 256 : 256 + broad] = ddep[:, broad * s : broad * s + broad].astype(BF)
        packed[s // 2, s % 2, place : place + high, 384 : 384 + table.shape[1]] = table[
            high * s : high * s + high, :
        ].astype(BF)


def finish_kernel(index_ref, *refs, parts):
    outs = refs[3 * parts : len(refs) - 3]
    sums, proj, last = refs[len(refs) - 3 :]
    for group, held in enumerate((sums, proj, last)):
        for k in range(parts):
            held[index_ref[0] ^ k] = refs[group * parts + k][...]
    (
        e_gain, e_shift, e_up, e_down, a_gain, a_shift, a_in, a_out, table, c_gain, c_shift, c_in, depth,
        i_gain, i_shift, c_out, l_gain, l_shift, l_up, l_down, f_gain, f_shift,
    ) = outs

    def reader(ref):
        def read(first, size):
            if len(ref.shape) == 2:
                return ref[first : first + size, :].astype(F32)
            height = ref.shape[1]
            pieces = []
            while size:
                piece, top = divmod(first, height)
                here = min(size, height - top)
                pieces.append(ref[piece].astype(F32)[top : top + here, :])
                first += here
                size -= here
            return pieces[0] if len(pieces) == 1 else jnp.concatenate(pieces, axis=0)

        return read

    def put(read, place, out):
        height = out.shape[0]
        for f in range(out.shape[1] // 512):
            out[:, 512 * f : 512 * f + 512] = read(place, height)
            place += height
        return place

    sums, proj, last = reader(sums), reader(proj), reader(last)
    put(sums, put(sums, put(sums, put(sums, put(sums, 0, l_up), l_down), c_out), c_in), a_out)
    put(proj, put(proj, 0, a_in), e_down)
    place = put(last, 0, e_up)
    small = last(place, 16)
    for line, out in enumerate(
        (e_gain, e_shift, a_gain, a_shift, c_gain, c_shift, l_gain, l_shift, f_gain, f_shift)
    ):
        out[...] = small[line : line + 1, 0 : out.shape[1]]
    i_gain[...] = small[0:1, 128 : 128 + i_gain.shape[1]]
    i_shift[...] = small[1:2, 128 : 128 + i_shift.shape[1]]
    depth[...] = small[0 : depth.shape[0], 256 : 256 + depth.shape[1]]
    table[...] = small[0 : table.shape[0], 384 : 384 + table.shape[1]]


def per_rec(array, first=0):
    shape = (1,) + array.shape[1:]
    tail = (0,) * (array.ndim - 1)
    return pl.BlockSpec(shape, lambda r, *_: (r + first,) + tail)


def whole(array):
    zeros = (0,) * array.ndim
    return pl.BlockSpec(array.shape, lambda r, *_: zeros, pipeline_mode=pl.Buffered(1))


def whole_out(array):
    zeros = (0,) * len(array.shape)
    return pl.BlockSpec(array.shape, lambda r, *_: zeros)


def per_unit(array, recs):
    units, rest = array.shape[0], array.shape[2:]
    if len(array.shape) == 6:
        return pl.BlockSpec(
            (units, 1, rest[0], 1) + rest[2:], lambda r, *_: (0, r // recs, 0, r % recs, 0, 0)
        )
    return pl.BlockSpec((units, 1, 1) + rest[1:], lambda r, *_: (0, r // recs, r % recs, 0, 0))


def far(array):
    return pl.BlockSpec(memory_space=pl.ANY)


def spot(shape, kind=F32):
    return jax.ShapeDtypeStruct(shape, kind)


def run(
    kernel, seqs, ins, in_specs, outs, out_specs, scratch=(), prefetch=(), after=(), into=(),
    micros=6,
):
    held = (*after, *into)
    plain = kernel
    place = len(prefetch) + len(ins)

    def kernel(*refs):
        plain(*refs[:place], *refs[place + len(held) :])

    return pl.pallas_call(
        kernel,
        grid_spec=pltpu.PrefetchScalarGridSpec(
            num_scalar_prefetch=len(prefetch),
            grid=(seqs,),
            in_specs=[*in_specs, *(pl.BlockSpec(memory_space=pl.ANY) for _ in held)],
            out_specs=out_specs,
            scratch_shapes=list(scratch),
        ),
        out_shape=outs,
        cost_estimate=cost(micros),
        input_output_aliases={place + len(after) + k: k for k in range(len(into))},
        compiler_params=pltpu.CompilerParams(vmem_limit_bytes=58 * MEGA),
    )(*prefetch, *ins, *held)


def unit_plan(seqs, heads):
    parts = lax.axis_size("tm")
    if parts <= heads:
        return heads // parts, seqs, 1
    return 1, seqs * heads // parts, parts // heads


def distance_hot(seq_total, bucket_count):
    limits = jnp.array(boundaries(seq_total), jnp.int32)
    places = jnp.arange(seq_total, dtype=jnp.int32)
    bucket = jnp.sum((places[:, None] >= limits[None, :]).astype(jnp.int32), axis=1)
    return (bucket[:, None] == jnp.arange(bucket_count, dtype=jnp.int32)[None, :]).astype(FLOAT)


def bias_strip(table, hot, nh, split):
    first = lax.axis_index("tm") // split * nh
    mine = lax.dynamic_slice_in_dim(table, first, nh, 1)
    per = jnp.dot(hot, mine, precision=HIGHEST).T
    pad = 2 * KEYS
    shifted = [
        jnp.pad(per, ((0, 0), (pad + s, 0)), constant_values=NEGATIVE)[:, : pad + hot.shape[0]]
        for s in range(8)
    ]
    return make_strip(jnp.stack(shifted, 1))


def table_grad(diagonals, hot, nh, split, heads):
    per = sum(jnp.pad(diagonals[:, s, KEYS + s :], ((0, 0), (0, s))) for s in range(8))
    mine = jnp.dot(hot.T, per.T, precision=HIGHEST)
    first = lax.axis_index("tm") // split * nh
    return lax.dynamic_update_slice_in_dim(
        jnp.zeros((hot.shape[1], heads), FLOAT), mine, first, 1
    )


def swap(values):
    return lax.all_to_all(values, "tm", 0, 0, tiled=True)


def body(
    frames, cotangent, lengths,
    early_gain, early_shift, early_up, early_down,
    attend_gain, attend_shift, attend_input, attend_output, distance_bias,
    convolve_gain, convolve_shift, convolve_input, depthwise, inner_gain, inner_shift, convolve_output,
    late_gain, late_shift, late_up, late_down, final_gain, final_shift,
):
    seqs, rows, width = frames.shape
    heads = distance_bias.shape[1]
    count = lax.axis_size("rows")
    parts = lax.axis_size("tm")
    hidden = early_up.shape[1]
    channels = convolve_output.shape[0]
    nh, recs, split = unit_plan(seqs, heads)
    units = heads // nh
    batches = seqs if split == 1 else 1
    here = seqs // batches
    recs = recs // batches
    tokens = seqs * rows
    vectors = (
        early_gain, early_shift, attend_gain, attend_shift, convolve_gain, convolve_shift,
        late_gain, late_shift, final_gain, final_shift, inner_gain, inner_shift,
    )
    lines = pl.pallas_call(lines_kernel, out_shape=spot((16, 512)))(*vectors)
    core = (lax.axis_index("rows") % 2).astype(jnp.int32)[None]
    merge = lambda v: v.reshape(tokens, -1)

    def wide(*kinds):
        return spot((units, split, *kinds, recs, rows, 128), BF)

    def held(columns, kind=BF):
        return pltpu.VMEM((rows, columns), kind)

    def like(array):
        return pltpu.VMEM(array.shape, array.dtype)

    def sems(size):
        return pltpu.SemaphoreType.DMA((size,))

    def shares(kinds, ins, height, extra=(), after=(), apart=True):
        shape = (count // 2, 2, height // 512 // count, 512)
        outs = (spot((shape[0],) + shape[2:], BF),) * 2 if apart else (spot(shape, BF),)
        return run(
            functools.partial(share_kernel, kinds=kinds, extra=len(extra), apart=apart), 1, (*ins, *extra),
            [far(v) for v in ins] + [whole(v) for v in extra], outs, [far(v) for v in outs],
            scratch=[like(v) for v in ins] + [pltpu.VMEM(shape, BF), pltpu.VMEM((16, 512), F32), sems(40)],
            after=after, prefetch=(core,),
        )

    def own(columns, kind=BF):
        return spot((seqs, rows, columns), kind)

    kept = ()
    sent = []
    for batch in range(batches):
        ins = (
            frames, early_gain, early_shift, attend_gain, attend_shift, early_up, early_down, attend_input,
        )
        outs = (own(width, F32), own(width), own(hidden), own(hidden), own(width), wide(3))
        *kept, qkv = run(
            functools.partial(open_kernel, nh=nh, first=batch * here, recs=recs), here, ins,
            [far(v) for v in ins], outs, [far(v) for v in outs],
            scratch=(
                held(width), like(early_gain), like(early_shift), like(attend_gain), like(attend_shift),
                like(early_up), like(early_down), like(attend_input), held(width, F32),
                held(width), held(hidden), held(hidden), held(width), pltpu.VMEM((3, units, rows, 128), BF),
                held(width, F32), sems(40),
            ),
            into=kept,
        )
        sent.append(swap(qkv.reshape(parts, 3, recs, rows, 128)))
    x1, h1, a1, sp1, h2 = kept
    hot = distance_hot(rows * parts, distance_bias.shape[0])
    strip = bias_strip(distance_bias.astype(FLOAT), hot, nh, split)
    mine = [
        lax.dynamic_slice_in_dim(lengths, batch * here + lax.axis_index("tm") % split * recs, recs, 0)
        for batch in range(batches)
    ]
    attended = [attn_fwd(mine[batch], sent[batch], strip, nh) for batch in range(batches)]

    limits = lengths - lax.axis_index("tm").astype(jnp.int32) * rows
    kept = ()
    for batch in range(batches):
        back = swap(attended[batch][0]).reshape(units, split, recs, rows, 128)
        ins = (back, x1, lines, attend_output, convolve_input)
        outs = (own(width), own(width, F32), own(width), own(channels), own(channels), own(channels))
        kept = run(
            functools.partial(gate_kernel, nh=nh, first=batch * here, recs=recs), here, ins,
            [far(v) for v in ins], outs, [far(v) for v in outs], prefetch=(limits,), into=kept,
            scratch=(
                pltpu.VMEM((units, rows, 128), BF), held(width, F32), like(lines), like(attend_output),
                like(convolve_input), held(width), held(width, F32), held(width),
                held(channels), held(channels), held(channels), sems(40),
            ),
        )
    att, x2, h3, g, ga, gb = kept
    halo = passed_along(g[:, rows - 16 :, :], "tm", 1)

    dep = jnp.pad(depthwise.astype(FLOAT).T, ((0, 1), (0, 0)))
    ins = (g, halo, x2, cotangent, dep, lines, convolve_output, late_up, late_down)
    height = (width * hidden * 2 + channels * width) // 512 // count
    outs = (
        own(width), own(width, F32), own(channels), spot((seqs, 16, channels), BF),
        spot((16, 512)), spot((16, channels)), spot((count // 2, 2, height, 512), BF),
    )
    layer_out, dx3, dg, dhalo, small_mid, ddep, pack_mid = run(
        middle_kernel, seqs, ins,
        [per_rec(v) for v in ins[:4]] + [whole(v) for v in ins[4:6]] + [far(v) for v in ins[6:]],
        outs, [per_rec(v) for v in outs[:4]] + [whole_out(v) for v in outs[4:6]] + [far(outs[6])],
        scratch=(
            pltpu.VMEM((channels // 128, rows + 16, 128), F32), pltpu.VMEM((rows, channels), F32),
            pltpu.VMEM((rows, 1), F32), pltpu.VMEM((rows + 32, 128), F32), pltpu.VMEM((rows, channels), BF),
            pltpu.VMEM((tokens, width), BF), pltpu.VMEM((tokens, hidden), BF), pltpu.VMEM((rows, hidden), BF),
            pltpu.VMEM((tokens, hidden), BF), pltpu.VMEM((tokens, width), BF),
            pltpu.VMEM((tokens, channels), BF), pltpu.VMEM((tokens, width), BF),
            pltpu.VMEM((channels // 128, 128, 128), F32), pltpu.VMEM((rows, channels), F32),
            like(convolve_output), like(late_up), like(late_down), like(outs[6]), sems(16), sems(16),
        ),
        micros=200,
    )
    returned = passed_along(dhalo, "tm", -1)
    sums_mid = offloaded(pack_mid)

    kept = ()
    sent_back = []
    small_gate = []
    for batch in range(batches):
        ins = (dg, returned, ga, gb, dx3, x2, lines, convolve_input, attend_output)
        outs = (own(width, F32), own(2 * channels), own(width), wide(), spot((8, 512)))
        *kept, do, small = run(
            functools.partial(ungate_kernel, nh=nh, first=batch * here, recs=recs), here, ins,
            [far(v) for v in ins], outs, [far(v) for v in outs],
            scratch=(
                held(channels), pltpu.VMEM((16, channels), BF), like(lines), like(convolve_input), like(attend_output),
                held(channels), held(channels), held(width, F32), held(width, F32), held(width, F32),
                held(2 * channels), held(width), pltpu.VMEM((units, rows, 128), BF), pltpu.VMEM((8, 512), F32),
                held(512, F32), held(width, F32), sems(40),
            ),
            into=kept,
        )
        small_gate.append(small)
        sent_back.append(swap(do.reshape(parts, recs, rows, 128)))
    dx2, du, dy2 = kept
    pack_gate = shares(
        ("columns", "columns"), (merge(h3), merge(du), merge(att), merge(dy2)), 2 * channels * width + width * width,
        apart=False,
    )
    own_grads = []
    diagonals = 0.0
    for batch in range(batches):
        out, lse = attended[batch]
        grad, diagonal = attn_bwd(mine[batch], sent[batch], sent_back[batch], out, lse, strip, nh)
        diagonals = diagonals + diagonal
        own_grads.append(swap(grad).reshape(units, split, 3, recs, rows, 128))
    sums_gate = offloaded(pack_gate[0])
    grad_table = table_grad(diagonals, hot, nh, split, heads)

    kept = ()
    kept_two = ()
    small_proj = []
    small_first = []
    for batch in range(batches):
        ins = (own_grads[batch], x1, dx2, lines, attend_input)
        outs = (own(width, F32), own(width), own(3 * width), spot((8, 512)))
        if batch == batches - 1:
            part_rest = time_sum(jnp.concatenate([sums_mid, sums_gate], axis=0))
        *kept, small = run(
            functools.partial(project_kernel, nh=nh, first=batch * here, recs=recs), here, ins,
            [far(v) for v in ins], outs, [far(v) for v in outs],
            scratch=(
                like(lines), like(attend_input), pltpu.VMEM((3, units, rows, 128), BF), held(width, F32),
                held(width, F32), held(width, F32), held(width), held(3 * width), pltpu.VMEM((8, 512), F32),
                held(width, F32), sems(40),
            ),
            into=kept, after=(sums_mid,) if batch == batches - 1 else (),
        )
        small_proj.append(small)
        dx1, dy1, dp = kept
        if batch == batches - 1:
            pack_proj = shares(
                ("columns", "rows"), (merge(h2), merge(dp), merge(a1), merge(dy1)), width * hidden + width * 3 * width,
                apart=False,
            )
            sums_proj = offloaded(pack_proj[0])
            before = ()
        else:
            before = ()
        ins = (dy1, dx1, frames, sp1, lines, early_up, early_down)
        outs = (own(width), own(hidden), spot((8, 512)))
        *kept_two, small = run(
            functools.partial(close_kernel, first=batch * here), here, ins,
            [far(v) for v in ins], outs, [far(v) for v in outs],
            scratch=(
                held(width), like(lines), like(early_up), like(early_down), held(hidden), held(width, F32),
                held(width), held(hidden), held(width), pltpu.VMEM((8, 512), F32), held(width, F32), sems(40),
            ),
            into=kept_two, after=before,
        )
        small_first.append(small)
    dx0, dz1 = kept_two
    pack_last = shares(
        ("columns",), (merge(h1), merge(dz1)), width * hidden + 32 * 512 * count,
        extra=(small_mid, ddep, grad_table, *small_first, *small_proj, *small_gate), after=(part_rest,),
    )
    part_last = along_chips(along_time(between_cores(*pack_last)))
    part_proj = time_sum_by_steps(sums_proj)
    totals = (part_rest, *others(part_rest), part_proj, *others(part_proj), part_last, *others(part_last))
    return (layer_out, dx0) + finish(
        totals, count, parts, width, hidden, channels, depthwise.shape[1], distance_bias.shape
    )


def offloaded(packed):
    sent = packed.reshape(-1, packed.shape[3])
    return lax.psum_scatter(sent, "rows", scatter_dimension=0, tiled=True)


def with_others(mine):
    parts = lax.axis_size("tm")
    return lax.all_to_all(jnp.broadcast_to(mine, (parts,) + mine.shape), "tm", 0, 0, tiled=True)


def total(blocks):
    return jnp.sum(blocks.astype(FLOAT), axis=0).astype(BF)


def between_cores(keep, send):
    devices = range(lax.axis_size("rows"))
    got = lax.ppermute(send, "rows", [(i, i ^ 1) for i in devices])
    return (keep.astype(FLOAT) + got.astype(FLOAT)).astype(BF)


def time_sum(share):
    parts = lax.axis_size("tm")
    blocks = share.reshape((parts, share.shape[0] // parts) + share.shape[1:])
    return total(lax.all_to_all(blocks, "tm", 0, 0, tiled=True))


def time_sum_by_steps(share):
    parts = lax.axis_size("tm")
    me = lax.axis_index("tm")
    blocks = share.reshape((parts, share.shape[0] // parts) + share.shape[1:])
    pick = lambda k: lax.dynamic_index_in_dim(blocks, me ^ k, 0, keepdims=False)
    sums = pick(0).astype(FLOAT)
    for k in range(1, parts):
        got = lax.ppermute(pick(k), "tm", [(i, i ^ k) for i in range(parts)])
        sums = sums + got.astype(FLOAT)
    return sums.astype(BF)


def others(mine):
    parts = lax.axis_size("tm")
    return [lax.ppermute(mine, "tm", [(i, i ^ k) for i in range(parts)]) for k in range(1, parts)]


def along_time(half):
    chips, height, width = half.shape
    parts = lax.axis_size("tm")
    blocks = jnp.transpose(half.reshape(chips, parts, height // parts, width), (1, 0, 2, 3))
    return total(lax.all_to_all(blocks, "tm", 0, 0, tiled=True))


def along_chips(part):
    devices = range(lax.axis_size("rows"))
    groups = [[i for i in devices if i % 2 == core] for core in range(2)]
    return total(lax.all_to_all(part, "rows", 0, 0, axis_index_groups=groups, tiled=True))


def finish(totals, count, parts, width, hidden, channels, taps, table_shape):
    share = width // count
    line = (1, share)
    broad = (1, channels // count)
    shapes = (
        line, line, (share, hidden), (hidden // count, width), line, line, (share, 3 * width), (share, width),
        (table_shape[0] // count, table_shape[1]), line, line, (share, 2 * channels), (taps, channels // count),
        broad, broad, (channels // count, width), line, line, (share, hidden), (hidden // count, width), line, line,
    )
    outs = tuple(spot(shape) for shape in shapes)
    me = lax.axis_index("tm").astype(jnp.int32)[None]
    got = list(
        run(
            functools.partial(finish_kernel, parts=parts), 1, totals, [whole(v) for v in totals],
            outs, [whole_out(v) for v in outs], prefetch=(me,), micros=3,
            scratch=[pltpu.VMEM((parts,) + v.shape, BF) for v in totals[::parts]],
        )
    )
    got[12] = got[12].T
    for place, shape in enumerate(shapes):
        if shape[0] == 1:
            got[place] = got[place].reshape(-1)
    return tuple(got)


def solution(mesh):
    placed = (
        P("rows", "tm", None),
        P("rows", "tm", None),
        P("rows"),
        P(),
        P(),
        P(),
        P(),
        P(),
        P(),
        P(),
        P(),
        P(),
        P(),
        P(),
        P(),
        P(),
        P(),
        P(),
        P(),
        P(),
        P(),
        P(),
        P(),
        P(),
        P(),
    )
    return jax.shard_map(
        body,
        mesh=mesh,
        in_specs=placed,
        out_specs=(
            P("rows", "tm", None),
            P("rows", "tm", None),
            P("rows"),
            P("rows"),
            P("rows", None),
            P("rows", None),
            P("rows"),
            P("rows"),
            P("rows", None),
            P("rows", None),
            P("rows", None),
            P("rows"),
            P("rows"),
            P("rows", None),
            P("rows", None),
            P("rows"),
            P("rows"),
            P("rows", None),
            P("rows"),
            P("rows"),
            P("rows", None),
            P("rows", None),
            P("rows"),
            P("rows"),
        ),
        check_vma=False,
    )
```

```python
import functools

import jax
import jax.numpy as jnp
from jax import lax
from jax.experimental import pallas as pl
from jax.experimental.pallas import tpu as pltpu
from jax.sharding import PartitionSpec as P

EPSILON = 1e-05
NEGATIVE = -1e30
HIGHEST = lax.Precision.HIGHEST
BFLOAT = jnp.bfloat16
FLOAT = jnp.float32
NEG = NEGATIVE
F32 = FLOAT
BF = BFLOAT


MEGA = 2**20
SCALE = 1


def cost(micros):
    micros = micros * SCALE
    return pl.CostEstimate(
        flops=int(micros * 1.1e9), bytes_accessed=int(micros * 3.6e6), transcendentals=0
    )


def passed_along(block, axis, distance):
    devices = range(lax.axis_size(axis))
    route = [(i - distance, i) for i in devices if i - distance in devices]
    return lax.ppermute(block, axis, route)


def boundaries(seq_total):
    edges_list = list(range(1, 16))
    for exponent in range(16):
        edges_list.append(int(16.0 * (seq_total / 16.0) ** (exponent / 16.0)))
    return edges_list


KEYS = 256
QUERIES = 512


def nt(a, b):
    return lax.dot_general(a, b, (((1,), (1,)), ((), ())), preferred_element_type=F32)


def nn(a, b):
    return lax.dot_general(a, b, (((1,), (0,)), ((), ())), preferred_element_type=F32)


def strip_kernel(base_ref, out_ref):
    heads, keys, _ = out_ref.shape
    for h in range(heads):
        base = base_ref[h]
        for g in range(keys // 8):
            out_ref[h, 8 * g : 8 * g + 8, :] = pltpu.roll(base, 8 * g, 1)[:, keys:] if g else base[:, keys:]


def make_strip(base):
    heads, _, wide = base.shape
    return pl.pallas_call(
        strip_kernel,
        out_shape=jax.ShapeDtypeStruct((heads, KEYS, wide - KEYS), F32),
        compiler_params=pltpu.CompilerParams(vmem_limit_bytes=58 * MEGA),
        cost_estimate=cost(3),
    )(base)


def head_lanes(shape, h):
    lane = lax.broadcasted_iota(jnp.int32, shape, 1)
    return (lane >= 64 * h) & (lane < 64 * h + 64), lane == ((64 * h + 64) % 128)


def masked_queries(q, h):
    mine, spare = head_lanes(q.shape, h)
    return jnp.where(mine, q, jnp.where(spare, 1.0, 0.0)).astype(BF)


def masked_keys(k, h, first, length):
    mine, spare = head_lanes(k.shape, h)
    beyond = first + lax.broadcasted_iota(jnp.int32, k.shape, 0) >= length
    return jnp.where(mine, k, jnp.where(spare & beyond, NEG, 0.0)).astype(BF)


def block_of(index, size):
    return pl.ds(pl.multiple_of(index * size, 128), size)


def loop(first, last, step):
    def turn(index, carried):
        step(index)
        return carried

    lax.fori_loop(first, last, turn, 0)


def attend_kernel(len_ref, x_ref, bias_ref, o_ref, lse_ref, kh, vt, qh, acc, ot, strip_ref, sem, *, nh):
    parts, rows = x_ref.shape[0], x_ref.shape[3]
    total = parts * rows
    length = len_ref[pl.program_id(0)]
    bias = pltpu.make_async_copy(bias_ref, strip_ref, sem.at[0])
    bias.start()

    def prepare(t):
        at = block_of(t, rows)
        q = x_ref[t, 0, 0].astype(F32) * 0.125
        k = x_ref[t, 1, 0].astype(F32)
        v = x_ref[t, 2, 0].astype(F32).T.astype(BF)
        for h in range(nh):
            qh[h, at, :] = masked_queries(q, h)
            kh[h, at, :] = masked_keys(k, h, t * rows, length)
            vt[h, 0:64, at] = v[64 * h : 64 * h + 64]
            ones = lax.broadcasted_iota(jnp.int32, (16, rows), 0) == 0
            vt[h, 64:80, at] = jnp.where(ones, 1.0, 0.0).astype(BF)

    loop(0, parts, prepare)
    bias.wait()

    def queries(qb):
        at = block_of(qb, QUERIES)
        for h in range(nh):
            acc[h] = jnp.zeros((80, QUERIES), F32)

        def keys(kb, peaks):
            there = block_of(kb, QUERIES)
            after = []
            for h in range(nh):
                scores = []
                for half in range(QUERIES // KEYS):
                    first = kb * QUERIES + half * KEYS
                    off = pl.ds(pl.multiple_of(KEYS + qb * QUERIES - first, 128), QUERIES)
                    k = kh[h, pl.ds(pl.multiple_of(first, 128), KEYS), :]
                    scores.append(nt(k, qh[h, at, :]) + strip_ref[h, :, off])
                peak = peaks[h]
                for s in scores:
                    peak = jnp.maximum(peak, jnp.max(s, axis=0, keepdims=True))
                p = jnp.concatenate([jnp.exp(s - peak).astype(BF) for s in scores], axis=0)
                acc[h] = acc[h] * jnp.exp(peaks[h] - peak) + nn(vt[h, :, there], p)
                after.append(peak)
            return tuple(after)

        last = jnp.minimum(qb + 1, (length + QUERIES - 1) // QUERIES)
        peaks = lax.fori_loop(
            0, last, keys, tuple(jnp.full((1, QUERIES), NEG, F32) for _ in range(nh))
        )
        for h in range(nh):
            sums = acc[h, 64:65, :]
            lse_ref[0, h, :, at] = peaks[h] + jnp.log(sums)
            ot[64 * h : 64 * h + 64, at] = acc[h, 0:64, :] / sums
        if nh == 1:
            ot[64:128, at] = jnp.zeros((64, QUERIES), F32)

    loop(0, total // QUERIES, queries)

    def give(t):
        o_ref[t, 0] = ot[:, block_of(t, rows)].T.astype(BF)

    loop(0, parts, give)


def attn_fwd(lengths, x, strip, nh):
    parts, _, recs, rows, wide = x.shape
    total = parts * rows
    return pl.pallas_call(
        functools.partial(attend_kernel, nh=nh),
        grid_spec=pltpu.PrefetchScalarGridSpec(
            num_scalar_prefetch=1,
            grid=(recs,),
            in_specs=[
                pl.BlockSpec((parts, 3, 1, rows, wide), lambda r, l: (0, 0, r, 0, 0)), pl.BlockSpec(memory_space=pl.ANY),
            ],
            out_specs=[
                pl.BlockSpec((parts, 1, rows, wide), lambda r, l: (0, r, 0, 0)),
                pl.BlockSpec((1, nh, 1, total), lambda r, l: (r, 0, 0, 0)),
            ],
            scratch_shapes=[
                pltpu.VMEM((nh, total, wide), BF), pltpu.VMEM((nh, 80, total), BF),
                pltpu.VMEM((nh, total, wide), BF), pltpu.VMEM((nh, 80, QUERIES), F32),
                pltpu.VMEM((wide, total), F32), pltpu.VMEM(strip.shape, F32), pltpu.SemaphoreType.DMA((1,)),
            ],
        ),
        out_shape=[
            jax.ShapeDtypeStruct((parts, recs, rows, wide), BF),
            jax.ShapeDtypeStruct((recs, nh, 1, total), F32),
        ],
        compiler_params=pltpu.CompilerParams(vmem_limit_bytes=58 * MEGA),
        cost_estimate=cost(11),
    )(lengths, x, strip)


def attend_back_kernel(
    len_ref, x_ref, do_ref, o_ref, lse_ref, bias_ref, dx_ref, db_ref,
    kh, vh, qh, qs, dos, kt, dqt, delta, dk, dv, dks, dvs, dbs, strip_ref, sem, *, nh,
):
    parts, rows = x_ref.shape[0], x_ref.shape[3]
    total = parts * rows
    length = len_ref[pl.program_id(0)]
    blocks = (length + KEYS - 1) // KEYS
    bias = pltpu.make_async_copy(bias_ref, strip_ref, sem.at[0])
    bias.start()

    @pl.when(pl.program_id(0) == 0)
    def _():
        dbs[...] = jnp.zeros_like(dbs)

    dqt[...] = jnp.zeros_like(dqt)

    def prepare(t):
        at = block_of(t, rows)
        q = x_ref[t, 0, 0].astype(F32) * 0.125
        k = x_ref[t, 1, 0].astype(F32)
        v = x_ref[t, 2, 0].astype(F32)
        do = do_ref[t, 0]
        qs[at, :] = q.astype(BF)
        dos[at, :] = do
        kt[:, at] = k.T.astype(BF)
        product = (do.astype(F32) * o_ref[t, 0].astype(F32)).T
        for h in range(nh):
            qh[h, at, :] = masked_queries(q, h)
            kh[h, at, :] = masked_keys(k, h, t * rows, length)
            vh[h, at, :] = jnp.where(head_lanes(v.shape, h)[0], v, 0.0).astype(BF)
            delta[h, :, at] = jnp.sum(product[64 * h : 64 * h + 64], axis=0, keepdims=True)

    loop(0, parts, prepare)
    bias.wait()

    def keys(kb):
        there = block_of(kb, KEYS)
        dk[...] = jnp.zeros_like(dk)
        dv[...] = jnp.zeros_like(dv)

        def queries(qb):
            at = block_of(qb, QUERIES)
            off = pl.ds(pl.multiple_of(KEYS + qb * QUERIES - kb * KEYS, 128), QUERIES)
            for h in range(nh):
                s = nt(kh[h, there, :], qh[h, at, :]) + strip_ref[h, :, off]
                p = jnp.exp(s - lse_ref[0, h, :, at])
                ds = p * (nt(vh[h, there, :], dos[at, :]) - delta[h, :, at])
                low = ds.astype(BF)
                dv[h] += nn(p.astype(BF), dos[at, :])
                dk[h] += nn(low, qs[at, :])
                dqt[64 * h : 64 * h + 64, at] += nn(kt[64 * h : 64 * h + 64, there], low)
                dbs[h, :, off] += ds

        loop(kb * KEYS // QUERIES, total // QUERIES, queries)
        first, _ = head_lanes((KEYS, 128), 0)
        dks[there, :] = (jnp.where(first, dk[0], dk[1]) if nh == 2 else dk[0]).astype(BF)
        dvs[there, :] = (jnp.where(first, dv[0], dv[1]) if nh == 2 else dv[0]).astype(BF)

    loop(0, blocks, keys)

    def nothing(kb):
        dks[block_of(kb, KEYS), :] = jnp.zeros((KEYS, 128), BF)
        dvs[block_of(kb, KEYS), :] = jnp.zeros((KEYS, 128), BF)

    loop(blocks, total // KEYS, nothing)

    def give(t):
        at = block_of(t, rows)
        dx_ref[t, 0, 0] = (dqt[:, at] * 0.125).T.astype(BF)
        dx_ref[t, 1, 0] = dks[at, :]
        dx_ref[t, 2, 0] = dvs[at, :]

    loop(0, parts, give)

    @pl.when(pl.program_id(0) == pl.num_programs(0) - 1)
    def _():
        wide = dbs.shape[2]
        for h in range(nh):
            sums = dbs[h, 0:8, :]
            for g in range(1, KEYS // 8):
                sums = sums + pltpu.roll(dbs[h, 8 * g : 8 * g + 8, :], wide - 8 * g, 1)
            db_ref[h] = sums


def attn_bwd(lengths, x, do, o, lse, strip, nh):
    parts, _, recs, rows, wide = x.shape
    total = parts * rows
    several = pltpu.VMEM((nh, total, wide), BF)
    single = pltpu.VMEM((total, wide), BF)
    part = pltpu.VMEM((nh, KEYS, wide), F32)
    return pl.pallas_call(
        functools.partial(attend_back_kernel, nh=nh),
        grid_spec=pltpu.PrefetchScalarGridSpec(
            num_scalar_prefetch=1,
            grid=(recs,),
            in_specs=[
                pl.BlockSpec((parts, 3, 1, rows, wide), lambda r, l: (0, 0, r, 0, 0)),
                pl.BlockSpec((parts, 1, rows, wide), lambda r, l: (0, r, 0, 0)),
                pl.BlockSpec((parts, 1, rows, wide), lambda r, l: (0, r, 0, 0)),
                pl.BlockSpec((1, nh, 1, total), lambda r, l: (r, 0, 0, 0)),
                pl.BlockSpec(memory_space=pl.ANY),
            ],
            out_specs=[
                pl.BlockSpec((parts, 3, 1, rows, wide), lambda r, l: (0, 0, r, 0, 0)),
                pl.BlockSpec((nh, 8, strip.shape[2]), lambda r, l: (0, 0, 0)),
            ],
            scratch_shapes=[
                several, several, several, single, single, pltpu.VMEM((wide, total), BF),
                pltpu.VMEM((wide, total), F32), pltpu.VMEM((nh, 1, total), F32), part, part, single, single,
                pltpu.VMEM(strip.shape, F32), pltpu.VMEM(strip.shape, F32), pltpu.SemaphoreType.DMA((1,)),
            ],
        ),
        out_shape=[
            jax.ShapeDtypeStruct((parts, 3, recs, rows, wide), BF),
            jax.ShapeDtypeStruct((nh, 8, strip.shape[2]), F32),
        ],
        compiler_params=pltpu.CompilerParams(vmem_limit_bytes=58 * MEGA),
        cost_estimate=cost(15),
    )(lengths, x, do, o, lse, strip)


def tn(a, b):
    return lax.dot_general(a, b, (((0,), (0,)), ((), ())), preferred_element_type=F32)


def sigmoid(v):
    return 0.5 * jnp.tanh(0.5 * v) + 0.5


LINES = {
    "early_gain": 0, "early_shift": 1, "attend_gain": 2, "attend_shift": 3, "convolve_gain": 4, "convolve_shift": 5,
    "late_gain": 6, "late_shift": 7, "final_gain": 8, "final_shift": 9, "inner_gain": 10,
}


def row(ref, name):
    place = LINES[name]
    return ref[place : place + 1, :]


def broad_row(ref, name, width):
    blocks = width // 512
    place = LINES["inner_gain"] + (blocks if name == "inner_shift" else 0)
    return jnp.concatenate([ref[place + c : place + c + 1, :] for c in range(blocks)], axis=1)


def part_of(index, size=512):
    return pl.ds(pl.multiple_of(index * size, 128), size)


def repeat(count, step):
    def turn(index, carried):
        step(index)
        return carried

    lax.fori_loop(0, count, turn, 0)


def mover(sems):
    spent = []

    def move(source, target):
        copy = pltpu.make_async_copy(source, target, sems.at[len(spent)])
        spent.append(copy)
        copy.start()
        return copy

    return move


def pieces(width):
    return [slice(first, first + 512) for first in range(0, width, 512)]


def settle(copies):
    for copy in copies:
        copy.wait()


class Lane:
    def __init__(self, sems, first, parts, make):
        self.sems, self.first, self.parts, self.make = sems, first, parts, make
        self.each = len(make(0))

    def copies(self, part):
        place = self.first + part * self.each
        return [
            pltpu.make_async_copy(source, target, self.sems.at[place + k])
            for k, (source, target) in enumerate(self.make(part))
        ]

    def start(self, part=0):
        for copy in self.copies(part):
            copy.start()

    def wait(self, part=0):
        for copy in self.copies(part):
            copy.wait()

    def start_all(self):
        for part in range(self.parts):
            self.start(part)

    def wait_all(self):
        repeat(self.parts, self.wait)


def lanes(sems):
    spent = [0]

    def lane(parts, make):
        made = Lane(sems, spent[0], parts, make)
        spent[0] += parts * made.each
        return made

    return lane


def one(*pairs):
    return 1, lambda part: list(pairs)


def feed(h, wu, wd, up, down, keep):
    y = None
    for f in range(wu.shape[1] // 512):
        at = slice(512 * f, 512 * f + 512)
        up(f)
        z = nn(h, wu[:, at])
        sig = sigmoid(z)
        a = (z * sig).astype(BF)
        keep(f, at, a, (sig * (1.0 + z * (1.0 - sig))).astype(BF))
        down(f)
        part = nn(a, wd[at, :])
        y = part if y is None else y + part
    return y


def feed_back(dy, wu, wd, up, down, slope, keep):
    dh = None
    for f in range(wu.shape[1] // 512):
        at = slice(512 * f, 512 * f + 512)
        down(f)
        dz = (nt(dy, wd[at, :]) * slope(f, at).astype(F32)).astype(BF)
        keep(f, at, dz)
        up(f)
        part = nt(dz, wu[:, at])
        dh = part if dh is None else dh + part
    return dh


def over_rows(rows, step):
    step(slice(0, rows))


def over_tiles(rows, step):
    def tile(t):
        step(part_of(t, 128))

    repeat(rows // 128, tile)


def share_columns(held, place, left, right, ready, send):
    height = left.shape[1] // (held.shape[0] * held.shape[1])

    def step(f):
        ready(f)
        block = tn(left[...], right[:, part_of(f)]).astype(BF)
        there = pl.ds(pl.multiple_of(place + f * height, 16), height)
        held[:, :, there, :] = block.reshape(held.shape[:2] + (height, 512))
        send(f, pl.ds(0, held.shape[0]), there)

    repeat(right.shape[1] // 512, step)


def share_rows(held, place, left, right, ready, send):
    height = left.shape[1] // (held.shape[0] * held.shape[1])
    each = 512 // (held.shape[1] * height)

    def step(f):
        ready(f)
        block = tn(left[:, part_of(f)], right[...]).astype(BF)
        who, there = pl.ds(each * f, each), pl.ds(place, height)
        held[who, :, there, :] = block.reshape(each, held.shape[1], height, 512)
        send(f, who, there)

    repeat(left.shape[1] // 512, step)


def columns_of(held, place, left, right):
    height = left.shape[1] // (held.shape[0] * held.shape[1])
    return lambda f: (pl.ds(0, held.shape[0]), pl.ds(pl.multiple_of(place + f * height, 16), height))


def rows_of(held, place, left, right):
    height = left.shape[1] // (held.shape[0] * held.shape[1])
    each = 512 // (held.shape[1] * height)
    return lambda f: (pl.ds(each * f, each), pl.ds(place, height))


def spread_columns(send, held, place, left, right, ready):
    count = held.shape[0] * held.shape[1]
    height = left.shape[1] // count
    for f, at in enumerate(pieces(right.shape[1])):
        ready(f)
        there = slice(place, place + height)
        block = tn(left[...], right[:, at]).astype(BF)
        held[:, :, there, :] = block.reshape(held.shape[:2] + (height, 512))
        send(slice(0, held.shape[0]), there)
        place += height
    return place


def spread_rows(send, held, place, left, right, ready):
    height = left.shape[1] // (held.shape[0] * held.shape[1])
    each = 512 // (held.shape[1] * height)
    for f, at in enumerate(pieces(left.shape[1])):
        ready(f)
        who, there = slice(each * f, each * f + each), slice(place, place + height)
        block = tn(left[:, at], right[...]).astype(BF)
        held[who, :, there, :] = block.reshape(each, held.shape[1], height, 512)
        send(who, there)
    return place + height


def norm_parts(v):
    center = v - jnp.mean(v, axis=-1, keepdims=True)
    inverse = lax.rsqrt(jnp.mean(center * center, axis=-1, keepdims=True) + EPSILON)
    return center * inverse, inverse


def norm_pull(n, inverse, gain, grad):
    dn = grad * gain
    return (
        dn - jnp.mean(dn, axis=-1, keepdims=True) - n * jnp.mean(dn * n, axis=-1, keepdims=True)
    ) * inverse


def add_rows(ref, place, values):
    total = jnp.sum(values, axis=0, keepdims=True)
    for c in range(values.shape[1] // 512):
        ref[place + c : place + c + 1, :] += total[:, 512 * c : 512 * c + 512]


def start_small(ref):
    @pl.when(pl.program_id(0) == 0)
    def _():
        ref[...] = jnp.zeros_like(ref)


def put_heads(write, value, nh):
    for pair in range(value.shape[1] // 128):
        part = value[:, 128 * pair : 128 * pair + 128]
        if nh == 2:
            write(pair, part.astype(BF))
        else:
            low = lax.broadcasted_iota(jnp.int32, part.shape, 1) < 64
            write(2 * pair, jnp.where(low, part, 0.0).astype(BF))
            write(2 * pair + 1, jnp.where(low, pltpu.roll(part, 64, 1), 0.0).astype(BF))


def take_heads(read, units, nh):
    if nh == 2:
        return jnp.concatenate([read(u) for u in range(units)], axis=1)
    pairs = [
        (read(2 * u).astype(F32) + pltpu.roll(read(2 * u + 1).astype(F32), 64, 1)).astype(BF)
        for u in range(units // 2)
    ]
    return jnp.concatenate(pairs, axis=1)


def lines_kernel(*refs):
    out = refs[-1]
    out[...] = jnp.zeros_like(out)
    place = 0
    for ref in refs[:-1]:
        for c in range(ref.shape[0] // 512):
            out[place : place + 1, :] = ref[512 * c : 512 * c + 512].astype(F32).reshape(1, 512)
            place += 1


def open_kernel(
    x_ref, g1_ref, s1_ref, g2_ref, s2_ref, wu_ref, wd_ref, wi_ref, x1_ref, h1_ref, a_ref, sp_ref, h2_ref, u_ref,
    x, g1, s1, g2, s2, wu, wd, wi, x1, h1, a1, sp, h2, u, total, sems, *, nh, first, recs,
):
    turn = pl.program_id(0)
    rec = first + turn
    rows = x.shape[0]
    parts = wu.shape[1] // 512
    lane = lanes(sems)
    ahead = lane(*one((x_ref.at[rec], x), (g1_ref, g1), (s1_ref, s1), (g2_ref, g2), (s2_ref, s2)))
    line = lambda ref: ref[...].astype(F32).reshape(1, 512)
    up = lane(parts, lambda f: [(wu_ref.at[:, part_of(f)], wu.at[:, part_of(f)])])
    down = lane(parts, lambda f: [(wd_ref.at[part_of(f), :], wd.at[part_of(f), :])])
    wide = lane(3, lambda f: [(wi_ref.at[:, part_of(f)], wi.at[:, part_of(f)])])
    out_h1 = lane(*one((h1, h1_ref.at[rec])))
    out_hidden = lane(
        parts,
        lambda f: [
            (a1.at[:, part_of(f)], a_ref.at[rec, :, part_of(f)]),
            (sp.at[:, part_of(f)], sp_ref.at[rec, :, part_of(f)]),
        ],
    )
    out_x1 = lane(*one((x1, x1_ref.at[rec]), (h2, h2_ref.at[rec])))
    out_u = lane(3, lambda f: [(u.at[f], u_ref.at[:, turn // recs, f, turn % recs])])
    ahead.start()
    for f in range(parts):
        up.start(f)
        down.start(f)
    wide.start_all()
    ahead.wait()

    def normal(at):
        n, _ = norm_parts(x[at, :].astype(F32))
        h1[at, :] = (n * line(g1) + line(s1)).astype(BF)

    over_rows(rows, normal)
    out_h1.start()

    def keep(f, at, a, slope):
        a1[:, at] = a
        sp[:, at] = slope
        out_hidden.start(f)

    total[...] = feed(h1[...], wu, wd, up.wait, down.wait, keep)

    def second(at):
        value = x[at, :].astype(F32) + 0.5 * total[at, :]
        x1[at, :] = value
        n, _ = norm_parts(value)
        h2[at, :] = (n * line(g2) + line(s2)).astype(BF)

    over_rows(rows, second)
    out_x1.start()

    def project(kind):
        wide.wait(kind)

        def write(unit, part):
            u[kind, unit] = part

        put_heads(write, nn(h2[...], wi[:, part_of(kind)]), nh)
        out_u.start(kind)

    repeat(3, project)
    for out in (out_h1, out_hidden, out_x1, out_u):
        out.wait_all()


def gate_kernel(
    len_ref, o_ref, x1_ref, lines_ref, wo_ref, wc_ref, att_ref, x2_ref, h3_ref, g_ref, ga_ref, gb_ref,
    o, x1, lines, wo, wc, att, x2, h3, g, ga, gb, sems, *, nh, first, recs,
):
    turn = pl.program_id(0)
    rec = first + turn
    rows = x1.shape[0]
    channels = g.shape[1]
    parts = channels // 512
    lane = lanes(sems)
    ahead = lane(*one((o_ref.at[:, turn // recs, turn % recs], o), (wo_ref, wo)))
    then = lane(*one((x1_ref.at[rec], x1), (lines_ref, lines)))
    wide = lane(
        parts,
        lambda f: [
            (wc_ref.at[:, part_of(f)], wc.at[:, part_of(f)]),
            (wc_ref.at[:, part_of(f + parts)], wc.at[:, part_of(f + parts)]),
        ],
    )
    out_att = lane(*one((att, att_ref.at[rec])))
    out_x2 = lane(*one((x2, x2_ref.at[rec]), (h3, h3_ref.at[rec])))
    out_g = lane(
        parts,
        lambda f: [
            (held.at[:, part_of(f)], out.at[rec, :, part_of(f)])
            for held, out in ((g, g_ref), (ga, ga_ref), (gb, gb_ref))
        ],
    )
    ahead.start()
    then.start()
    wide.start_all()
    ahead.wait()
    att[...] = take_heads(lambda unit: o[unit], o.shape[0], nh)
    out_att.start()
    then.wait()
    x2[...] = x1[...] + nn(att[...], wo[...])

    def normal(at):
        n, _ = norm_parts(x2[at, :])
        h3[at, :] = (n * row(lines, "convolve_gain") + row(lines, "convolve_shift")).astype(BF)

    over_tiles(rows, normal)
    out_x2.start()
    limit = len_ref[rec]
    place = lax.broadcasted_iota(jnp.int32, (rows, 1), 0)
    valid = jnp.where(place < limit, 1.0, 0.0)

    def step(f):
        at = part_of(f)
        wide.wait(f)
        lin = nn(h3[...], wc[:, at])
        sig = sigmoid(nn(h3[...], wc[:, part_of(f + parts)]))
        sv = sig * valid
        value = lin * sv
        g[:, at] = value.astype(BF)
        ga[:, at] = sv.astype(BF)
        gb[:, at] = (value * (1.0 - sig)).astype(BF)
        out_g.start(f)

    repeat(parts, step)
    for out in (out_att, out_x2, out_g):
        out.wait_all()


def middle_kernel(
    g_ref, halo_ref, x2_ref, cot_ref, dep, lines, wco, wu, wd,
    out_ref, dx3_ref, dg_ref, dhalo_ref, small_ref, ddep_ref, pack_ref,
    gx, cs, inv3, dcx, sp3, h4s, a4s, sp4, dz4s, dy4s, a3s, dy3s, tapped, dws, wcov, wuv, wdv, held, sems, out_sems,
):
    rec = pl.program_id(0)
    rows = x2_ref.shape[1]
    channels = g_ref.shape[2]
    strips = channels // 128
    taps = dep.shape[0] - 1
    start_small(small_ref)
    start_small(tapped)
    first = pl.multiple_of(rec * rows, 128)
    mine = pl.ds(first, rows)
    tile = 24
    fetched = [(wco, wcov)]
    for at in pieces(wu.shape[1]):
        fetched.append((wu.at[:, at], wuv.at[:, at]))
        fetched.append((wd.at[at, :], wdv.at[at, :]))
    fetched = [pltpu.make_async_copy(*pair, sems.at[k]) for k, pair in enumerate(fetched)]

    @pl.when(rec == 0)
    def _():
        for copy in fetched:
            copy.start()

    def ready(k):
        @pl.when(rec == 0)
        def _():
            fetched[k].wait()


    def conv(c):
        at = part_of(c, 128)
        gx[c, 0:16, :] = halo_ref[0, :, at].astype(F32)
        gx[c, 16:, :] = g_ref[0, :, at].astype(F32)
        for top in range(0, rows, tile):
            sums = dep[0:1, at] * gx[c, top + 2 : top + 2 + tile, :]
            for r in range(1, taps):
                sums = sums + dep[r : r + 1, at] * gx[c, top + 2 + r : top + 2 + r + tile, :]
            cs[top : top + tile, at] = sums

    repeat(strips, conv)

    def inner(t):
        there = pl.ds(pl.multiple_of(t * 384, 384), 384)
        n, inverse = norm_parts(cs[there, :])
        cs[there, :] = n
        inv3[there, :] = inverse
        w = n * broad_row(lines, "inner_gain", channels) + broad_row(lines, "inner_shift", channels)
        sig = sigmoid(w)
        a3s[pl.ds(first + pl.multiple_of(t * 384, 384), 384), :] = (w * sig).astype(BF)
        sp3[there, :] = (sig * (1.0 + w * (1.0 - sig))).astype(BF)

    repeat(rows // 384, inner)
    ready(0)
    x3 = x2_ref[0] + nn(a3s[mine, :], wcov[...])
    n4, inv4 = norm_parts(x3)
    h4 = (n4 * row(lines, "late_gain") + row(lines, "late_shift")).astype(BF)
    h4s[mine, :] = h4

    def keep(f, at, a, slope):
        a4s[mine, at] = a
        sp4[:, at] = slope

    y = feed(h4, wuv, wdv, lambda f: ready(1 + 2 * f), lambda f: ready(2 + 2 * f), keep)
    x4 = x3 + 0.5 * y
    n5, inv5 = norm_parts(x4)
    out_ref[0] = (n5 * row(lines, "final_gain") + row(lines, "final_shift")).astype(BF)
    cot = cot_ref[0].astype(F32)
    add_rows(small_ref, 8, cot * n5)
    add_rows(small_ref, 9, cot)
    dx4 = norm_pull(n5, inv5, row(lines, "final_gain"), cot)
    dx3_ref[0] = dx4
    dy4 = (0.5 * dx4).astype(BF)
    dy4s[mine, :] = dy4

    def keep_back(f, at, dz):
        dz4s[mine, at] = dz

    done = lambda f: None
    dh = feed_back(dy4, wuv, wdv, done, done, lambda f, at: sp4[:, at], keep_back)
    add_rows(small_ref, 6, dh * n4)
    add_rows(small_ref, 7, dh)
    dx3 = dx3_ref[0] + norm_pull(n4, inv4, row(lines, "late_gain"), dh)
    dx3_ref[0] = dx3
    dy3s[mine, :] = dx3.astype(BF)

    def pull(f):
        at = part_of(f)
        dws[:, at] = nt(dy3s[mine, :], wcov[at, :]) * sp3[:, at].astype(F32)

    for f in range(channels // 512):
        pull(f)

    def inner_back(t):
        there = pl.ds(pl.multiple_of(t * 384, 384), 384)
        dw = dws[there, :]
        n = cs[there, :]
        add_rows(small_ref, 2, dw * n)
        add_rows(small_ref, 4, dw)
        cs[there, :] = norm_pull(n, inv3[there, :], broad_row(lines, "inner_gain", channels), dw)

    repeat(rows // 384, inner_back)

    def conv_back(c):
        at = part_of(c, 128)
        dcx[0:16, :] = jnp.zeros((16, 128), F32)
        dcx[16 : 16 + rows, :] = cs[:, at]
        dcx[16 + rows :, :] = jnp.zeros((16, 128), F32)
        sums = [jnp.zeros((8, 128), F32)] * taps
        for top in range(0, rows, tile):
            dc = dcx[16 + top : 16 + top + tile, :]
            for r in range(taps):
                term = dc * gx[c, top + 2 + r : top + 2 + r + tile, :]
                sums[r] = sums[r] + jnp.sum(term.reshape(tile // 8, 8, 128), axis=0)
        for r in range(taps):
            tapped[c, 8 * r : 8 * r + 8, :] += sums[r]
        for top in range(0, rows + 16, tile):
            size = min(tile, rows + 16 - top)
            sums = dep[0:1, at] * dcx[top + 14 : top + 14 + size, :]
            for r in range(1, taps):
                sums = sums + dep[r : r + 1, at] * dcx[top + 14 - r : top + 14 - r + size, :]
            if top == 0:
                dhalo_ref[0, :, at] = sums[0:16].astype(BF)
                dg_ref[0, 0 : size - 16, at] = sums[16:].astype(BF)
            else:
                dg_ref[0, top - 16 : top - 16 + size, at] = sums.astype(BF)

    repeat(strips, conv_back)

    @pl.when(rec == pl.num_programs(0) - 1)
    def _():
        def depth(c):
            for r in range(taps):
                ddep_ref[r : r + 1, part_of(c, 128)] = jnp.sum(
                    tapped[c, 8 * r : 8 * r + 8, :], axis=0, keepdims=True
                )

        ddep_ref[taps:, :] = jnp.zeros((1, channels), F32)
        repeat(strips, depth)
        move = mover(out_sems)
        sent = []

        def send(who, there):
            sent.append(move(held.at[who, :, there], pack_ref.at[who, :, there]))

        place = spread_columns(send, held, 0, h4s, dz4s, done)
        place = spread_rows(send, held, place, a4s, dy4s, done)
        spread_rows(send, held, place, a3s, dy3s, done)
        settle(sent)


def share(kind, lane, held, outs, core, place, left, right, ready):
    columns = kind == "columns"
    parts = (right if columns else left).shape[1] // 512
    where = (columns_of if columns else rows_of)(held, place, left, right)

    def make(f):
        who, there = where(f)
        if core is None:
            return [(held.at[who, :, there], outs[0].at[who, :, there])]
        return [(held.at[who, c, there], out.at[who, there]) for c, out in zip((core, 1 - core), outs)]

    out = lane(parts, make)
    (share_columns if columns else share_rows)(
        held, place, left, right, ready, lambda f, who, there: out.start(f)
    )
    height = left.shape[1] // (held.shape[0] * held.shape[1])
    return place + height * (parts if columns else 1), out


def ungate_kernel(
    dg_ref, back_ref, ga_ref, gb_ref, dx3_ref, x2_ref, lines_ref, wc_ref, wo_ref,
    dx2_ref, du_ref, dy2_ref, do_ref, small_ref,
    dg, back, lines, wc, wo, ga, gb, dx3, x2, dx2, du, dy2, do, small, dgx, total, sems, *, nh, first, recs,
):
    turn = pl.program_id(0)
    rec = first + turn
    rows = x2.shape[0]
    channels = ga.shape[1]
    parts = channels // 512
    lane = lanes(sems)
    ahead = lane(*one((back_ref.at[rec], back)))
    fetch = lane(
        parts,
        lambda f: [
            (dg_ref.at[rec, :, part_of(f)], dg.at[:, part_of(f)]),
            (ga_ref.at[rec, :, part_of(f)], ga.at[:, part_of(f)]),
            (gb_ref.at[rec, :, part_of(f)], gb.at[:, part_of(f)]),
            (wc_ref.at[:, part_of(f)], wc.at[:, part_of(f)]),
            (wc_ref.at[:, part_of(f + parts)], wc.at[:, part_of(f + parts)]),
        ],
    )
    then = lane(*one((x2_ref.at[rec], x2), (dx3_ref.at[rec], dx3), (lines_ref, lines), (wo_ref, wo)))
    out_du = lane(
        parts,
        lambda f: [
            (du.at[:, part_of(f)], du_ref.at[rec, :, part_of(f)]),
            (du.at[:, part_of(f + parts)], du_ref.at[rec, :, part_of(f + parts)]),
        ],
    )
    out_dx2 = lane(*one((dx2, dx2_ref.at[rec]), (dy2, dy2_ref.at[rec]), (small, small_ref)))
    out_do = lane(*one((do, do_ref.at[:, turn // recs, turn % recs])))
    ahead.start()
    fetch.start_all()
    then.start()
    start_small(small)
    total[...] = jnp.zeros_like(total)
    ahead.wait()

    def step(f):
        at = part_of(f)
        up = part_of(f + parts)
        fetch.wait(f)
        dgx[...] = dg[:, at].astype(F32)
        dgx[rows - 16 :, :] += back[:, at].astype(F32)
        value = dgx[...]
        lin = (value * ga[:, at].astype(F32)).astype(BF)
        gate = (value * gb[:, at].astype(F32)).astype(BF)
        du[:, at] = lin
        du[:, up] = gate
        out_du.start(f)
        total[...] += nt(lin, wc[:, at]) + nt(gate, wc[:, up])

    repeat(parts, step)
    then.wait()

    def pull(at):
        n, inverse = norm_parts(x2[at, :])
        dh = total[at, :]
        add_rows(small, 0, dh * n)
        add_rows(small, 1, dh)
        value = dx3[at, :] + norm_pull(n, inverse, row(lines, "convolve_gain"), dh)
        dx2[at, :] = value
        dy2[at, :] = value.astype(BF)

    over_rows(rows, pull)
    out_dx2.start()

    def write(unit, part):
        do[unit] = part

    put_heads(write, nt(dy2[...], wo[...]), nh)
    out_do.start()
    for out in (out_du, out_dx2, out_do):
        out.wait_all()


def project_kernel(
    u_ref, x1_ref, dx2_ref, lines_ref, wi_ref, dx1_ref, dy_ref, dp_ref, small_ref,
    lines, wi, u, x1, dx2, dx1, dy, dp, small, total, sems, *, nh, first, recs,
):
    turn = pl.program_id(0)
    rec = first + turn
    rows = x1.shape[0]
    lane = lanes(sems)
    fetch = lane(
        3,
        lambda f: [
            (u_ref.at[:, turn // recs, f, turn % recs], u.at[f]), (wi_ref.at[:, part_of(f)], wi.at[:, part_of(f)]),
        ],
    )
    then = lane(*one((x1_ref.at[rec], x1), (dx2_ref.at[rec], dx2), (lines_ref, lines)))
    out_dp = lane(3, lambda f: [(dp.at[:, part_of(f)], dp_ref.at[rec, :, part_of(f)])])
    out_dx1 = lane(*one((dx1, dx1_ref.at[rec]), (dy, dy_ref.at[rec]), (small, small_ref)))
    fetch.start_all()
    then.start()
    start_small(small)
    total[...] = jnp.zeros_like(total)

    def step(kind):
        at = part_of(kind)
        fetch.wait(kind)
        value = take_heads(lambda unit: u[kind, unit], u.shape[1], nh)
        dp[:, at] = value
        out_dp.start(kind)
        total[...] += nt(value, wi[:, at])

    repeat(3, step)
    then.wait()

    def pull(at):
        n, inverse = norm_parts(x1[at, :])
        dh = total[at, :]
        add_rows(small, 0, dh * n)
        add_rows(small, 1, dh)
        value = dx2[at, :] + norm_pull(n, inverse, row(lines, "attend_gain"), dh)
        dx1[at, :] = value
        dy[at, :] = (0.5 * value).astype(BF)

    over_rows(rows, pull)
    out_dx1.start()
    for out in (out_dp, out_dx1):
        out.wait_all()


def close_kernel(
    dy_ref, dx1_ref, x_ref, sp_ref, lines_ref, wu_ref, wd_ref, out_ref, dz_ref, small_ref,
    dy, lines, wu, wd, sp, dx1, x, dz, out, small, total, sems, *, first,
):
    rec = first + pl.program_id(0)
    rows = x.shape[0]
    parts = wu.shape[1] // 512
    lane = lanes(sems)
    ahead = lane(*one((dy_ref.at[rec], dy)))
    down = lane(
        parts,
        lambda f: [
            (wd_ref.at[part_of(f), :], wd.at[part_of(f), :]), (sp_ref.at[rec, :, part_of(f)], sp.at[:, part_of(f)]),
        ],
    )
    up = lane(parts, lambda f: [(wu_ref.at[:, part_of(f)], wu.at[:, part_of(f)])])
    then = lane(*one((x_ref.at[rec], x), (dx1_ref.at[rec], dx1), (lines_ref, lines)))
    out_dz = lane(parts, lambda f: [(dz.at[:, part_of(f)], dz_ref.at[rec, :, part_of(f)])])
    out_dx = lane(*one((out, out_ref.at[rec]), (small, small_ref)))
    ahead.start()
    for f in range(parts):
        down.start(f)
        up.start(f)
    then.start()
    start_small(small)
    ahead.wait()

    def keep(f, at, value):
        dz[:, at] = value
        out_dz.start(f)

    total[...] = feed_back(dy[...], wu, wd, up.wait, down.wait, lambda f, at: sp[:, at], keep)
    then.wait()

    def pull(at):
        n, inverse = norm_parts(x[at, :].astype(F32))
        dh = total[at, :]
        add_rows(small, 0, dh * n)
        add_rows(small, 1, dh)
        out[at, :] = (dx1[at, :] + norm_pull(n, inverse, row(lines, "early_gain"), dh)).astype(BF)

    over_rows(rows, pull)
    out_dx.start()
    for lane_out in (out_dz, out_dx):
        lane_out.wait_all()


def share_kernel(core_ref, *refs, kinds, extra, apart):
    jobs = len(kinds)
    ins = refs[: 2 * jobs]
    more = refs[2 * jobs : 2 * jobs + extra]
    outs = refs[2 * jobs + extra : 2 * jobs + extra + 1 + apart]
    held = refs[2 * jobs + extra + 1 + apart :]
    packed, small, sems = held[2 * jobs :]
    core = core_ref[0] if apart else None
    lane = lanes(sems)
    plan = []
    for k, kind in enumerate(kinds):
        left, right = ins[2 * k : 2 * k + 2]
        left_held, right_held = held[2 * k : 2 * k + 2]
        if kind == "columns":
            first = lane(*one((left, left_held)))
            source, target = right, right_held
        else:
            first = lane(*one((right, right_held)))
            source, target = left, left_held
        parts = lane(
            source.shape[1] // 512,
            lambda f, source=source, target=target: [(source.at[:, part_of(f)], target.at[:, part_of(f)])],
        )
        first.start()
        parts.start_all()
        plan.append((left_held, right_held, first, parts))
    waits = []
    place = 0
    for kind, (left, right, first, parts) in zip(kinds, plan):
        first.wait()
        place, out = share(kind, lane, packed, outs, core, place, left, right, parts.wait)
        waits.append(out)
    if extra:
        small_shares(more, packed, small, place)
        there = pl.ds(place, packed.shape[2] - place)
        out = lane(
            *one(*[(packed.at[:, c, there], target.at[:, there]) for c, target in zip((core, 1 - core), outs)])
        )
        out.start()
        waits.append(out)
    for out in waits:
        out.wait_all()


def small_shares(refs, packed, small, place):
    small_mid, ddep, table = refs[:3]
    batches = (len(refs) - 3) // 3
    count = packed.shape[0] * packed.shape[1]
    small[...] = jnp.zeros_like(small)
    for k in range(3):
        for ref in refs[3 + k * batches : 3 + k * batches + batches]:
            small[2 * k : 2 * k + 2, :] += ref[0:2, :]
    small[6:10, :] = small_mid[6:10, :]
    narrow = 512 // count
    broad = ddep.shape[1] // count
    high = table.shape[0] // count
    packed[:, :, place:, :] = jnp.zeros(packed.shape[:2] + (packed.shape[2] - place, 512), BF)
    blocks = ddep.shape[1] // 512
    inner = [
        jnp.concatenate([small_mid[first + c : first + c + 1, :] for c in range(blocks)], axis=1)
        for first in (2, 4)
    ]
    inner = jnp.concatenate(inner, axis=0)
    for s in range(count):
        there = slice(place, place + 16)
        packed[s // 2, s % 2, there, 0:narrow] = small[:, narrow * s : narrow * s + narrow].astype(BF)
        packed[s // 2, s % 2, place : place + 2, 128 : 128 + broad] = inner[
            :, broad * s : broad * s + broad
        ].astype(BF)
        packed[s // 2, s % 2, there, 256 : 256 + broad] = ddep[:, broad * s : broad * s + broad].astype(BF)
        packed[s // 2, s % 2, place : place + high, 384 : 384 + table.shape[1]] = table[
            high * s : high * s + high, :
        ].astype(BF)


def finish_kernel(index_ref, *refs, parts):
    outs = refs[3 * parts : len(refs) - 3]
    sums, proj, last = refs[len(refs) - 3 :]
    for group, held in enumerate((sums, proj, last)):
        for k in range(parts):
            held[index_ref[0] ^ k] = refs[group * parts + k][...]
    (
        e_gain, e_shift, e_up, e_down, a_gain, a_shift, a_in, a_out, table, c_gain, c_shift, c_in, depth,
        i_gain, i_shift, c_out, l_gain, l_shift, l_up, l_down, f_gain, f_shift,
    ) = outs

    def reader(ref):
        def read(first, size):
            if len(ref.shape) == 2:
                return ref[first : first + size, :].astype(F32)
            height = ref.shape[1]
            pieces = []
            while size:
                piece, top = divmod(first, height)
                here = min(size, height - top)
                pieces.append(ref[piece].astype(F32)[top : top + here, :])
                first += here
                size -= here
            return pieces[0] if len(pieces) == 1 else jnp.concatenate(pieces, axis=0)

        return read

    def put(read, place, out):
        height = out.shape[0]
        for f in range(out.shape[1] // 512):
            out[:, 512 * f : 512 * f + 512] = read(place, height)
            place += height
        return place

    sums, proj, last = reader(sums), reader(proj), reader(last)
    put(sums, put(sums, put(sums, put(sums, put(sums, 0, l_up), l_down), c_out), c_in), a_out)
    put(proj, put(proj, 0, a_in), e_down)
    place = put(last, 0, e_up)
    small = last(place, 16)
    for line, out in enumerate(
        (e_gain, e_shift, a_gain, a_shift, c_gain, c_shift, l_gain, l_shift, f_gain, f_shift)
    ):
        out[...] = small[line : line + 1, 0 : out.shape[1]]
    i_gain[...] = small[0:1, 128 : 128 + i_gain.shape[1]]
    i_shift[...] = small[1:2, 128 : 128 + i_shift.shape[1]]
    depth[...] = small[0 : depth.shape[0], 256 : 256 + depth.shape[1]]
    table[...] = small[0 : table.shape[0], 384 : 384 + table.shape[1]]


def per_rec(array, first=0):
    shape = (1,) + array.shape[1:]
    tail = (0,) * (array.ndim - 1)
    return pl.BlockSpec(shape, lambda r, *_: (r + first,) + tail)


def whole(array):
    zeros = (0,) * array.ndim
    return pl.BlockSpec(array.shape, lambda r, *_: zeros, pipeline_mode=pl.Buffered(1))


def whole_out(array):
    zeros = (0,) * len(array.shape)
    return pl.BlockSpec(array.shape, lambda r, *_: zeros)


def per_unit(array, recs):
    units, rest = array.shape[0], array.shape[2:]
    if len(array.shape) == 6:
        return pl.BlockSpec(
            (units, 1, rest[0], 1) + rest[2:], lambda r, *_: (0, r // recs, 0, r % recs, 0, 0)
        )
    return pl.BlockSpec((units, 1, 1) + rest[1:], lambda r, *_: (0, r // recs, r % recs, 0, 0))


def far(array):
    return pl.BlockSpec(memory_space=pl.ANY)


def spot(shape, kind=F32):
    return jax.ShapeDtypeStruct(shape, kind)


def run(
    kernel, seqs, ins, in_specs, outs, out_specs, scratch=(), prefetch=(), after=(), into=(),
    micros=6,
):
    held = (*after, *into)
    plain = kernel
    place = len(prefetch) + len(ins)

    def kernel(*refs):
        plain(*refs[:place], *refs[place + len(held) :])

    return pl.pallas_call(
        kernel,
        grid_spec=pltpu.PrefetchScalarGridSpec(
            num_scalar_prefetch=len(prefetch),
            grid=(seqs,),
            in_specs=[*in_specs, *(pl.BlockSpec(memory_space=pl.ANY) for _ in held)],
            out_specs=out_specs,
            scratch_shapes=list(scratch),
        ),
        out_shape=outs,
        cost_estimate=cost(micros),
        input_output_aliases={place + len(after) + k: k for k in range(len(into))},
        compiler_params=pltpu.CompilerParams(vmem_limit_bytes=58 * MEGA),
    )(*prefetch, *ins, *held)


def unit_plan(seqs, heads):
    parts = lax.axis_size("tm")
    if parts <= heads:
        return heads // parts, seqs, 1
    return 1, seqs * heads // parts, parts // heads


def distance_hot(seq_total, bucket_count):
    limits = jnp.array(boundaries(seq_total), jnp.int32)
    places = jnp.arange(seq_total, dtype=jnp.int32)
    bucket = jnp.sum((places[:, None] >= limits[None, :]).astype(jnp.int32), axis=1)
    return (bucket[:, None] == jnp.arange(bucket_count, dtype=jnp.int32)[None, :]).astype(FLOAT)


def bias_strip(table, hot, nh, split):
    first = lax.axis_index("tm") // split * nh
    mine = lax.dynamic_slice_in_dim(table, first, nh, 1)
    per = jnp.dot(hot, mine, precision=HIGHEST).T
    pad = 2 * KEYS
    shifted = [
        jnp.pad(per, ((0, 0), (pad + s, 0)), constant_values=NEGATIVE)[:, : pad + hot.shape[0]]
        for s in range(8)
    ]
    return make_strip(jnp.stack(shifted, 1))


def table_grad(diagonals, hot, nh, split, heads):
    per = sum(jnp.pad(diagonals[:, s, KEYS + s :], ((0, 0), (0, s))) for s in range(8))
    mine = jnp.dot(hot.T, per.T, precision=HIGHEST)
    first = lax.axis_index("tm") // split * nh
    return lax.dynamic_update_slice_in_dim(
        jnp.zeros((hot.shape[1], heads), FLOAT), mine, first, 1
    )


def swap(values):
    return lax.all_to_all(values, "tm", 0, 0, tiled=True)


def body(
    frames, cotangent, lengths,
    early_gain, early_shift, early_up, early_down,
    attend_gain, attend_shift, attend_input, attend_output, distance_bias,
    convolve_gain, convolve_shift, convolve_input, depthwise, inner_gain, inner_shift, convolve_output,
    late_gain, late_shift, late_up, late_down, final_gain, final_shift,
):
    seqs, rows, width = frames.shape
    heads = distance_bias.shape[1]
    count = lax.axis_size("rows")
    parts = lax.axis_size("tm")
    hidden = early_up.shape[1]
    channels = convolve_output.shape[0]
    nh, recs, split = unit_plan(seqs, heads)
    units = heads // nh
    batches = seqs if split == 1 else 1
    here = seqs // batches
    recs = recs // batches
    tokens = seqs * rows
    vectors = (
        early_gain, early_shift, attend_gain, attend_shift, convolve_gain, convolve_shift,
        late_gain, late_shift, final_gain, final_shift, inner_gain, inner_shift,
    )
    lines = pl.pallas_call(lines_kernel, out_shape=spot((16, 512)))(*vectors)
    core = (lax.axis_index("rows") % 2).astype(jnp.int32)[None]
    merge = lambda v: v.reshape(tokens, -1)

    def wide(*kinds):
        return spot((units, split, *kinds, recs, rows, 128), BF)

    def held(columns, kind=BF):
        return pltpu.VMEM((rows, columns), kind)

    def like(array):
        return pltpu.VMEM(array.shape, array.dtype)

    def sems(size):
        return pltpu.SemaphoreType.DMA((size,))

    def shares(kinds, ins, height, extra=(), after=(), apart=True):
        shape = (count // 2, 2, height // 512 // count, 512)
        outs = (spot((shape[0],) + shape[2:], BF),) * 2 if apart else (spot(shape, BF),)
        return run(
            functools.partial(share_kernel, kinds=kinds, extra=len(extra), apart=apart), 1, (*ins, *extra),
            [far(v) for v in ins] + [whole(v) for v in extra], outs, [far(v) for v in outs],
            scratch=[like(v) for v in ins] + [pltpu.VMEM(shape, BF), pltpu.VMEM((16, 512), F32), sems(40)],
            after=after, prefetch=(core,),
        )

    def own(columns, kind=BF):
        return spot((seqs, rows, columns), kind)

    kept = ()
    sent = []
    for batch in range(batches):
        ins = (
            frames, early_gain, early_shift, attend_gain, attend_shift, early_up, early_down, attend_input,
        )
        outs = (own(width, F32), own(width), own(hidden), own(hidden), own(width), wide(3))
        *kept, qkv = run(
            functools.partial(open_kernel, nh=nh, first=batch * here, recs=recs), here, ins,
            [far(v) for v in ins], outs, [far(v) for v in outs],
            scratch=(
                held(width), like(early_gain), like(early_shift), like(attend_gain), like(attend_shift),
                like(early_up), like(early_down), like(attend_input), held(width, F32),
                held(width), held(hidden), held(hidden), held(width), pltpu.VMEM((3, units, rows, 128), BF),
                held(width, F32), sems(40),
            ),
            into=kept,
        )
        sent.append(swap(qkv.reshape(parts, 3, recs, rows, 128)))
    x1, h1, a1, sp1, h2 = kept
    hot = distance_hot(rows * parts, distance_bias.shape[0])
    strip = bias_strip(distance_bias.astype(FLOAT), hot, nh, split)
    mine = [
        lax.dynamic_slice_in_dim(lengths, batch * here + lax.axis_index("tm") % split * recs, recs, 0)
        for batch in range(batches)
    ]
    attended = [attn_fwd(mine[batch], sent[batch], strip, nh) for batch in range(batches)]

    limits = lengths - lax.axis_index("tm").astype(jnp.int32) * rows
    kept = ()
    for batch in range(batches):
        back = swap(attended[batch][0]).reshape(units, split, recs, rows, 128)
        ins = (back, x1, lines, attend_output, convolve_input)
        outs = (own(width), own(width, F32), own(width), own(channels), own(channels), own(channels))
        kept = run(
            functools.partial(gate_kernel, nh=nh, first=batch * here, recs=recs), here, ins,
            [far(v) for v in ins], outs, [far(v) for v in outs], prefetch=(limits,), into=kept,
            scratch=(
                pltpu.VMEM((units, rows, 128), BF), held(width, F32), like(lines), like(attend_output),
                like(convolve_input), held(width), held(width, F32), held(width),
                held(channels), held(channels), held(channels), sems(40),
            ),
        )
    att, x2, h3, g, ga, gb = kept
    halo = passed_along(g[:, rows - 16 :, :], "tm", 1)

    dep = jnp.pad(depthwise.astype(FLOAT).T, ((0, 1), (0, 0)))
    ins = (g, halo, x2, cotangent, dep, lines, convolve_output, late_up, late_down)
    height = (width * hidden * 2 + channels * width) // 512 // count
    outs = (
        own(width), own(width, F32), own(channels), spot((seqs, 16, channels), BF),
        spot((16, 512)), spot((16, channels)), spot((count // 2, 2, height, 512), BF),
    )
    layer_out, dx3, dg, dhalo, small_mid, ddep, pack_mid = run(
        middle_kernel, seqs, ins,
        [per_rec(v) for v in ins[:4]] + [whole(v) for v in ins[4:6]] + [far(v) for v in ins[6:]],
        outs, [per_rec(v) for v in outs[:4]] + [whole_out(v) for v in outs[4:6]] + [far(outs[6])],
        scratch=(
            pltpu.VMEM((channels // 128, rows + 16, 128), F32), pltpu.VMEM((rows, channels), F32),
            pltpu.VMEM((rows, 1), F32), pltpu.VMEM((rows + 32, 128), F32), pltpu.VMEM((rows, channels), BF),
            pltpu.VMEM((tokens, width), BF), pltpu.VMEM((tokens, hidden), BF), pltpu.VMEM((rows, hidden), BF),
            pltpu.VMEM((tokens, hidden), BF), pltpu.VMEM((tokens, width), BF),
            pltpu.VMEM((tokens, channels), BF), pltpu.VMEM((tokens, width), BF),
            pltpu.VMEM((channels // 128, 128, 128), F32), pltpu.VMEM((rows, channels), F32),
            like(convolve_output), like(late_up), like(late_down), like(outs[6]), sems(16), sems(16),
        ),
        micros=200,
    )
    returned = passed_along(dhalo, "tm", -1)
    sums_mid = offloaded(pack_mid)

    kept = ()
    sent_back = []
    small_gate = []
    for batch in range(batches):
        ins = (dg, returned, ga, gb, dx3, x2, lines, convolve_input, attend_output)
        outs = (own(width, F32), own(2 * channels), own(width), wide(), spot((8, 512)))
        *kept, do, small = run(
            functools.partial(ungate_kernel, nh=nh, first=batch * here, recs=recs), here, ins,
            [far(v) for v in ins], outs, [far(v) for v in outs],
            scratch=(
                held(channels), pltpu.VMEM((16, channels), BF), like(lines), like(convolve_input), like(attend_output),
                held(channels), held(channels), held(width, F32), held(width, F32), held(width, F32),
                held(2 * channels), held(width), pltpu.VMEM((units, rows, 128), BF), pltpu.VMEM((8, 512), F32),
                held(512, F32), held(width, F32), sems(40),
            ),
            into=kept,
        )
        small_gate.append(small)
        sent_back.append(swap(do.reshape(parts, recs, rows, 128)))
    dx2, du, dy2 = kept
    pack_gate = shares(
        ("columns", "columns"), (merge(h3), merge(du), merge(att), merge(dy2)), 2 * channels * width + width * width,
        apart=False,
    )
    own_grads = []
    diagonals = 0.0
    for batch in range(batches):
        out, lse = attended[batch]
        grad, diagonal = attn_bwd(mine[batch], sent[batch], sent_back[batch], out, lse, strip, nh)
        diagonals = diagonals + diagonal
        own_grads.append(swap(grad).reshape(units, split, 3, recs, rows, 128))
    sums_gate = offloaded(pack_gate[0])
    grad_table = table_grad(diagonals, hot, nh, split, heads)

    kept = ()
    kept_two = ()
    small_proj = []
    small_first = []
    for batch in range(batches):
        ins = (own_grads[batch], x1, dx2, lines, attend_input)
        outs = (own(width, F32), own(width), own(3 * width), spot((8, 512)))
        if batch == batches - 1:
            part_rest = time_sum(jnp.concatenate([sums_mid, sums_gate], axis=0))
        *kept, small = run(
            functools.partial(project_kernel, nh=nh, first=batch * here, recs=recs), here, ins,
            [far(v) for v in ins], outs, [far(v) for v in outs],
            scratch=(
                like(lines), like(attend_input), pltpu.VMEM((3, units, rows, 128), BF), held(width, F32),
                held(width, F32), held(width, F32), held(width), held(3 * width), pltpu.VMEM((8, 512), F32),
                held(width, F32), sems(40),
            ),
            into=kept, after=(sums_mid,) if batch == batches - 1 else (),
        )
        small_proj.append(small)
        dx1, dy1, dp = kept
        if batch == batches - 1:
            pack_proj = shares(
                ("columns", "rows"), (merge(h2), merge(dp), merge(a1), merge(dy1)), width * hidden + width * 3 * width,
                apart=False,
            )
            sums_proj = offloaded(pack_proj[0])
            before = ()
        else:
            before = ()
        ins = (dy1, dx1, frames, sp1, lines, early_up, early_down)
        outs = (own(width), own(hidden), spot((8, 512)))
        *kept_two, small = run(
            functools.partial(close_kernel, first=batch * here), here, ins,
            [far(v) for v in ins], outs, [far(v) for v in outs],
            scratch=(
                held(width), like(lines), like(early_up), like(early_down), held(hidden), held(width, F32),
                held(width), held(hidden), held(width), pltpu.VMEM((8, 512), F32), held(width, F32), sems(40),
            ),
            into=kept_two, after=before,
        )
        small_first.append(small)
    dx0, dz1 = kept_two
    pack_last = shares(
        ("columns",), (merge(h1), merge(dz1)), width * hidden + 32 * 512 * count,
        extra=(small_mid, ddep, grad_table, *small_first, *small_proj, *small_gate), after=(part_rest,),
    )
    part_last = along_chips(along_time(between_cores(*pack_last)))
    part_proj = time_sum_by_steps(sums_proj)
    totals = (part_rest, *others(part_rest), part_proj, *others(part_proj), part_last, *others(part_last))
    return (layer_out, dx0) + finish(
        totals, count, parts, width, hidden, channels, depthwise.shape[1], distance_bias.shape
    )


def offloaded(packed):
    sent = packed.reshape(-1, packed.shape[3])
    return lax.psum_scatter(sent, "rows", scatter_dimension=0, tiled=True)


def with_others(mine):
    parts = lax.axis_size("tm")
    return lax.all_to_all(jnp.broadcast_to(mine, (parts,) + mine.shape), "tm", 0, 0, tiled=True)


def total(blocks):
    return jnp.sum(blocks.astype(FLOAT), axis=0).astype(BF)


def between_cores(keep, send):
    devices = range(lax.axis_size("rows"))
    got = lax.ppermute(send, "rows", [(i, i ^ 1) for i in devices])
    return (keep.astype(FLOAT) + got.astype(FLOAT)).astype(BF)


def time_sum(share):
    parts = lax.axis_size("tm")
    blocks = share.reshape((parts, share.shape[0] // parts) + share.shape[1:])
    return total(lax.all_to_all(blocks, "tm", 0, 0, tiled=True))


def time_sum_by_steps(share):
    parts = lax.axis_size("tm")
    me = lax.axis_index("tm")
    blocks = share.reshape((parts, share.shape[0] // parts) + share.shape[1:])
    pick = lambda k: lax.dynamic_index_in_dim(blocks, me ^ k, 0, keepdims=False)
    sums = pick(0).astype(FLOAT)
    for k in range(1, parts):
        got = lax.ppermute(pick(k), "tm", [(i, i ^ k) for i in range(parts)])
        sums = sums + got.astype(FLOAT)
    return sums.astype(BF)


def others(mine):
    parts = lax.axis_size("tm")
    return [lax.ppermute(mine, "tm", [(i, i ^ k) for i in range(parts)]) for k in range(1, parts)]


def along_time(half):
    chips, height, width = half.shape
    parts = lax.axis_size("tm")
    blocks = jnp.transpose(half.reshape(chips, parts, height // parts, width), (1, 0, 2, 3))
    return total(lax.all_to_all(blocks, "tm", 0, 0, tiled=True))


def along_chips(part):
    devices = range(lax.axis_size("rows"))
    groups = [[i for i in devices if i % 2 == core] for core in range(2)]
    return total(lax.all_to_all(part, "rows", 0, 0, axis_index_groups=groups, tiled=True))


def finish(totals, count, parts, width, hidden, channels, taps, table_shape):
    share = width // count
    line = (1, share)
    broad = (1, channels // count)
    shapes = (
        line, line, (share, hidden), (hidden // count, width), line, line, (share, 3 * width), (share, width),
        (table_shape[0] // count, table_shape[1]), line, line, (share, 2 * channels), (taps, channels // count),
        broad, broad, (channels // count, width), line, line, (share, hidden), (hidden // count, width), line, line,
    )
    outs = tuple(spot(shape) for shape in shapes)
    me = lax.axis_index("tm").astype(jnp.int32)[None]
    got = list(
        run(
            functools.partial(finish_kernel, parts=parts), 1, totals, [whole(v) for v in totals],
            outs, [whole_out(v) for v in outs], prefetch=(me,), micros=3,
            scratch=[pltpu.VMEM((parts,) + v.shape, BF) for v in totals[::parts]],
        )
    )
    got[12] = got[12].T
    for place, shape in enumerate(shapes):
        if shape[0] == 1:
            got[place] = got[place].reshape(-1)
    return tuple(got)


def solution(mesh):
    placed = (
        P("rows", "tm", None),
        P("rows", "tm", None),
        P("rows"),
        P(),
        P(),
        P(),
        P(),
        P(),
        P(),
        P(),
        P(),
        P(),
        P(),
        P(),
        P(),
        P(),
        P(),
        P(),
        P(),
        P(),
        P(),
        P(),
        P(),
        P(),
        P(),
    )
    return jax.shard_map(
        body,
        mesh=mesh,
        in_specs=placed,
        out_specs=(
            P("rows", "tm", None),
            P("rows", "tm", None),
            P("rows"),
            P("rows"),
            P("rows", None),
            P("rows", None),
            P("rows"),
            P("rows"),
            P("rows", None),
            P("rows", None),
            P("rows", None),
            P("rows"),
            P("rows"),
            P("rows", None),
            P("rows", None),
            P("rows"),
            P("rows"),
            P("rows", None),
            P("rows"),
            P("rows"),
            P("rows", None),
            P("rows", None),
            P("rows"),
            P("rows"),
        ),
        check_vma=False,
    )
```
